32 devices in a mesh: pipe: 4 (over y, x), dp: 8 (over z, core).
Axes of the slice: x: 2, y: 2, z: 4, core: 2. Of those that a mesh axis runs over, the one named last changes fastest.
Arguments:
- new_input: bfloat16 [4, 1024, 8192], P('pipe', 'dp'), may hold values from -400 to 400
- new_gain: bfloat16 [4, 8192], P('pipe'), may hold values from 0.5 to 1.5
- queries: bfloat16 [4, 1024, 4096], P('pipe', 'dp'), may hold values from -5 to 5
- new_keys: bfloat16 [4, 1024, 512], P('pipe', 'dp'), may hold values from -5 to 5
- context_grad: bfloat16 [4, 1024, 4096], P('pipe', 'dp'), may hold values from -0.08984375 to 0.08984375
- segment_ids: int32 [4, 1024], P('pipe', 'dp'), may hold values from 0 to 15, never falling along the last dimension, each value on 1 to 128 neighbouring positions
- frozen_input: bfloat16 [4, 1024, 8192], P('pipe', 'dp'), may hold values from -400 to 400
- frozen_gain: bfloat16 [4, 8192], P('pipe'), may hold values from 0.5 to 1.5
- output_grad: bfloat16 [4, 1024, 8192], P('pipe', 'dp'), may hold values from -6 to 6
- kv_grad: bfloat16 [4, 1024, 1024], P('pipe', 'dp'), may hold values from -18 to 18
- kv_weight: bfloat16 [4, 8192, 1024], P('pipe', 'dp'), may hold values from -0.0625 to 0.0625
Outputs:
- cot_below: bfloat16 [4, 1024, 8192], P('pipe', 'dp')
- value_grad: float32 [4, 8192, 512], P('pipe', 'dp')
The draws below stay inside these ranges and needn't reach their ends.
Inputs may be any that keep to these rules, and one draw needn't show every extreme that they name: `segment_ids`: within a section the numbers never fall; every number of 0 to 15 appears, on 1 to 128 positions in a row, one on exactly 128.
All inputs are finite; a program needn't handle non-finite values.
Results may differ from the reference program's by a relative error of at most 0.0056.
Values may be sent and summed in bfloat16 or wider, within the bound.
No kernel may reach another device: no remote copies, remote signals or barrier semaphores. Data moves between devices by JAX's collectives and lax.ppermute only.
A program may use at most 128 MiB of HBM per device.

```python
import math
import jax
import jax.numpy as jnp
import numpy as np
from jax import lax

D = 8192
HEAD = 128
KVHEADS = 4
GROUP = 8
QW = 4096
KVW = 512
TOK_DEV = 128
TOKENS = 1024
SEGS = 16
SECTIONS = 4


def scaled_rows(key, shape):
    key_base, key_rows, key_cols = jax.random.split(key, 3)
    base_vals = jnp.clip(jax.random.normal(key_base, shape, jnp.float32), -4.0, 4.0)
    col_shape = (shape[0], 1, shape[2])
    upper_log = math.log(10.0)
    row_scale = jnp.exp(jax.random.uniform(key_rows, (shape[0], shape[1], 1), jnp.float32, 0.0, upper_log))
    col_scale = jnp.exp(jax.random.uniform(key_cols, col_shape, jnp.float32, 0.0, math.log(4.0)))
    return base_vals * row_scale * col_scale


def draw_new_input(key, part):
    return scaled_rows(jax.random.fold_in(key, 3), (SECTIONS, TOKENS, D)).astype(jnp.bfloat16)


def draw_frozen_input(key, part):
    return scaled_rows(jax.random.fold_in(key, 5), (SECTIONS, TOKENS, D)).astype(jnp.bfloat16)


def drawn_pair(key):
    base_key = jax.random.fold_in(key, 17)
    key_query, key_key = jax.random.split(base_key, 2)
    query_vals = jnp.clip(jax.random.normal(key_query, (SECTIONS, TOKENS, KVHEADS, GROUP, HEAD), jnp.float32), -4.0, 4.0)
    key_vals = jnp.clip(jax.random.normal(key_key, (SECTIONS, TOKENS, KVHEADS, HEAD), jnp.float32), -4.0, 4.0)
    return (query_vals.reshape(SECTIONS, TOKENS, QW), key_vals.reshape(SECTIONS, TOKENS, KVW))


def draw_queries(key, part):
    return drawn_pair(key)[0].astype(jnp.bfloat16)


def draw_new_keys(key, part):
    return drawn_pair(key)[1].astype(jnp.bfloat16)


def levels(own_key, dims, cuts, least, largest):
    def one(dim, blocks):
        steps = jax.random.uniform(jax.random.fold_in(jax.random.fold_in(own_key, 6), dim), (blocks,), jnp.float32, least / len(cuts), largest / len(cuts))
        return jnp.repeat(jnp.exp(steps), dims[dim] // blocks).reshape((-1,) + (1,) * (len(dims) - dim - 1))

    loudness = one(*cuts[0])
    for cut in cuts[1:]:
        loudness = loudness * one(*cut)
    return loudness


def profile(number_of, total, limit, slope):
    weights = [(1 << 20) // math.isqrt(rank ** slope) + 1 for rank in range(2, number_of + 1)]
    surplus, given = total - limit - (number_of - 1), [1] * (number_of - 1)
    while surplus > 0:
        free = [i for i in range(number_of - 1) if given[i] < limit]
        pool, left = sum([weights[i] for i in free]), surplus
        for i in free:
            addition = min(limit - given[i], max(1, left * weights[i] // pool), surplus)
            given[i] = given[i] + addition
            surplus = surplus - addition
    return np.array([limit] + given)


def ragged(key, number_of, total, reach, skew):
    if number_of == 2:
        one = jax.random.randint(key, (), max(1, total - reach), min(reach, total - 1) + 1)
        return jnp.stack([one, total - one])
    sizes = jnp.asarray(profile(number_of, total, reach, skew), jnp.int32)
    pairs = (number_of - 1) // 2
    source_of, taker = sizes[1:1 + 2 * pairs:2], sizes[2:2 + 2 * pairs:2]
    margin = jnp.minimum(source_of - 1, reach - taker)
    shifted = jax.random.randint(jax.random.fold_in(key, 1), (pairs,), 0, 1 << 20) % (margin + 1)
    sizes = sizes.at[1:1 + 2 * pairs:2].set(source_of - shifted).at[2:2 + 2 * pairs:2].set(taker + shifted)
    return sizes[jax.random.permutation(jax.random.fold_in(key, 2), number_of)]


def gaussian(own_key, extent, spread, most, cuts=(), held_as=jnp.bfloat16):
    values = jax.random.normal(own_key, extent, jnp.float32) * spread
    if len(cuts) > 0:
        values = levels(own_key, extent, cuts, -0.22, 0.18) * values
    return jnp.clip(values, min=-most, max=most).astype(held_as)


def setup_inputs(seed: int = 0) -> dict:
    key_list = jax.random.split(jax.random.key(seed), 12)
    new_input = draw_new_input(jax.random.fold_in(key_list[11], 71), 0)
    new_gain = jnp.clip(1.0 + 0.1 * jax.random.normal(key_list[1], (SECTIONS, D), jnp.float32), 0.5, 1.5).astype(jnp.bfloat16)
    queries = draw_queries(jax.random.fold_in(key_list[11], 71), 0)
    new_keys = draw_new_keys(jax.random.fold_in(key_list[11], 71), 0)
    context_grad = gaussian(key_list[4], (SECTIONS, TOKENS, QW), 0.015, 0.08984375, ((0, 4), (1, 8)))
    segment_ids = jax.vmap(lambda own: jnp.searchsorted(jnp.cumsum(ragged(own, SEGS, TOKENS, TOK_DEV, 0)), jnp.arange(TOKENS), side="right"))(jax.random.split(key_list[5], SECTIONS)).reshape((SECTIONS, TOKENS)).astype(jnp.int32)
    frozen_input = draw_frozen_input(jax.random.fold_in(key_list[11], 71), 0)
    frozen_gain = jnp.clip(1.0 + 0.1 * jax.random.normal(key_list[7], (SECTIONS, D), jnp.float32), 0.5, 1.5).astype(jnp.bfloat16)
    output_grad = gaussian(key_list[8], (SECTIONS, TOKENS, D), 1.0, 6.0, ((0, 4), (1, 8)))
    kv_grad = gaussian(key_list[9], (SECTIONS, TOKENS, 2 * KVW), 3.0, 18.0, ((0, 4), (1, 8)))
    kv_weight = gaussian(key_list[10], (SECTIONS, D, 2 * KVW), D ** -0.5, 0.0625, ((0, 4), (1, 8)))
    return dict(new_input=new_input, new_gain=new_gain, queries=queries, new_keys=new_keys, context_grad=context_grad, segment_ids=segment_ids, frozen_input=frozen_input, frozen_gain=frozen_gain, output_grad=output_grad, kv_grad=kv_grad, kv_weight=kv_weight)


norm_eps = 1e-05
masked_value = -1e+30

def normalize(rows, gain):
    values = rows.astype(jnp.float32)
    inverse = lax.rsqrt(lax.optimization_barrier(jnp.mean(values * values, axis=-1, keepdims=True)) + norm_eps)
    return values * inverse * gain.astype(jnp.float32)

def norm_backward(rows, gain, upstream):
    values = rows.astype(jnp.float32)
    inverse = lax.rsqrt(lax.optimization_barrier(jnp.mean(values * values, axis=-1, keepdims=True)) + norm_eps)
    scaled = gain.astype(jnp.float32) * upstream
    inner_mean = lax.optimization_barrier(jnp.mean(values * scaled, axis=-1, keepdims=True))
    return inverse * scaled - values * inverse * inverse * inverse * inner_mean

def masked_softmax(scores, visible):
    masked = jnp.where(visible, scores, masked_value)
    highest = lax.optimization_barrier(jnp.max(masked, axis=-1, keepdims=True))
    weights = jnp.where(visible, jnp.exp(masked - highest), 0.0)
    return weights / lax.optimization_barrier(jnp.sum(weights, axis=-1, keepdims=True))

def one_sequence(members):
    query_rows, key_rows, grad_rows, seg_rows = members
    rows = query_rows.shape[0]
    query_four = query_rows.astype(jnp.float32).reshape(rows, KVHEADS, GROUP, HEAD)
    grad_four = grad_rows.astype(jnp.float32).reshape(rows, KVHEADS, GROUP, HEAD)
    key_three = key_rows.astype(jnp.float32).reshape(rows, KVHEADS, HEAD)
    position = jnp.arange(rows, dtype=jnp.int32)
    visible = (seg_rows[:, None] == seg_rows[None, :]) & (position[None, :] <= position[:, None])
    scores = jnp.einsum('tkgd,jkd->kgtj', query_four, key_three) / math.sqrt(HEAD)
    attention = masked_softmax(scores, visible).astype(jnp.bfloat16)
    return jnp.einsum('kgtj,tkgd->jkd', attention.astype(jnp.float32), grad_four).reshape(rows, KVW)

def attend_values(query_rows, key_rows, grad_rows, seg_rows):
    count = query_rows.shape[0] // TOK_DEV
    members = (query_rows.reshape(count, TOK_DEV, QW), key_rows.reshape(count, TOK_DEV, KVW), grad_rows.reshape(count, TOK_DEV, QW), seg_rows.astype(jnp.int32).reshape(count, TOK_DEV))
    return lax.map(one_sequence, members).reshape(count * TOK_DEV, KVW)

def reference(new_input, new_gain, queries, new_keys, context_grad, segment_ids, frozen_input, frozen_gain, output_grad, kv_grad, kv_weight):
    grad_list = []
    cot_list = []
    for section_at in range(SECTIONS):
        normed_new = normalize(new_input[section_at], new_gain[section_at]).astype(jnp.bfloat16)
        value_cot = attend_values(queries[section_at], new_keys[section_at], context_grad[section_at], segment_ids[section_at]).astype(jnp.bfloat16)
        grad_list.append(jnp.dot(normed_new.T, value_cot, preferred_element_type=jnp.float32))
        normed_cot = jnp.dot(kv_grad[section_at], kv_weight[section_at].T, preferred_element_type=jnp.float32).astype(jnp.bfloat16)
        normed_cot = lax.optimization_barrier(normed_cot)
        input_cot = output_grad[section_at].astype(jnp.float32) + norm_backward(frozen_input[section_at], frozen_gain[section_at], normed_cot.astype(jnp.float32))
        cot_list.append(input_cot.astype(jnp.bfloat16))
    cot_below = jnp.stack(cot_list[1:] + [jnp.zeros_like(cot_list[0])], axis=0)
    return (cot_below, jnp.stack(grad_list, axis=0))
```

```python
import functools
import math

import jax
import jax.numpy as jnp
from jax import lax
from jax.experimental import pallas as pl
from jax.experimental.pallas import tpu as pltpu
from jax.sharding import PartitionSpec as P

HEAD = 128
CHUNKS = 2


norm_eps = 1e-05
masked_value = -1e30
MIB = 1 << 20


def from_behind(array, axis, by):
    length = lax.axis_size(axis)
    pairs = [(i, i + by) for i in range(length) if 0 <= i + by < length]
    return lax.ppermute(array, axis, pairs)


def params(vmem):
    return pltpu.CompilerParams(vmem_limit_bytes=vmem * MIB)


def cost(flops, nbytes):
    return pl.CostEstimate(flops=flops, bytes_accessed=nbytes, transcendentals=0)


def norm_kernel(x_ref, gain_ref, out_ref):
    values = x_ref[...].astype(jnp.float32)
    inverse = lax.rsqrt(jnp.mean(values * values, axis=-1, keepdims=True) + norm_eps)
    parts, _, width = out_ref.shape
    for part in range(parts):
        cols = slice(part * width, (part + 1) * width)
        out_ref[part] = (
            values[:, cols] * inverse * gain_ref[:, cols].astype(jnp.float32)
        ).astype(out_ref.dtype)


def normalize(rows, gain, parts, chunk, chunks):
    tokens, width = rows.shape
    taken = tokens // chunks
    block = min(taken, 32)
    first = chunk * (taken // block)
    return pl.pallas_call(
        norm_kernel,
        grid=(taken // block,),
        in_specs=[
            pl.BlockSpec((block, width), lambda i: (first + i, 0)),
            pl.BlockSpec((1, width), lambda i: (0, 0)),
        ],
        out_specs=pl.BlockSpec((parts, block, width // parts), lambda i: (0, i, 0)),
        out_shape=jax.ShapeDtypeStruct((parts, taken, width // parts), jnp.bfloat16),
        compiler_params=params(16),
        cost_estimate=cost(4 * taken * width, 4 * taken * width),
        name="norm_forward",
    )(rows, gain)


def attend_kernel(query_ref, key_ref, grad_ref, row_seg_ref, col_seg_ref, out_ref):
    tokens = key_ref.shape[0]
    group = query_ref.shape[1] // HEAD
    at_query = lax.broadcasted_iota(jnp.int32, (tokens, tokens), 0)
    at_key = lax.broadcasted_iota(jnp.int32, (tokens, tokens), 1)
    visible = (col_seg_ref[...] == row_seg_ref[...]) & (at_key <= at_query)
    keys = key_ref[...]
    total = jnp.zeros((tokens, HEAD), jnp.float32)
    for head in range(group):
        cols = slice(head * HEAD, (head + 1) * HEAD)
        scores = lax.dot_general(
            query_ref[:, cols], keys, (((1,), (1,)), ((), ())),
            preferred_element_type=jnp.float32,
        ) / math.sqrt(HEAD)
        masked = jnp.where(visible, scores, masked_value)
        highest = jnp.max(masked, axis=-1, keepdims=True)
        weights = jnp.where(visible, jnp.exp(masked - highest), 0.0)
        attention = (weights / jnp.sum(weights, axis=-1, keepdims=True)).astype(jnp.bfloat16)
        total += lax.dot_general(
            attention, grad_ref[:, cols], (((0,), (0,)), ((), ())),
            preferred_element_type=jnp.float32,
        )
    out_ref[...] = total.astype(out_ref.dtype)


def attend(queries, keys, grads, segments):
    tokens, kv_width = keys.shape
    heads = kv_width // HEAD
    wide = queries.shape[1] // heads
    return pl.pallas_call(
        attend_kernel,
        grid=(heads,),
        in_specs=[
            pl.BlockSpec((tokens, wide), lambda i: (0, i)),
            pl.BlockSpec((tokens, HEAD), lambda i: (0, i)),
            pl.BlockSpec((tokens, wide), lambda i: (0, i)),
            pl.BlockSpec((1, tokens), lambda i: (0, 0)),
            pl.BlockSpec((tokens, 1), lambda i: (0, 0)),
        ],
        out_specs=pl.BlockSpec((tokens, HEAD), lambda i: (0, i)),
        out_shape=jax.ShapeDtypeStruct((tokens, kv_width), jnp.bfloat16),
        compiler_params=params(16),
        cost_estimate=cost(4 * tokens * tokens * queries.shape[1], 4 * tokens * queries.shape[1]),
        name="attend",
    )(queries, keys, grads, segments, segments.reshape(tokens, 1))


def project_kernel(rows_ref, weight_ref, out_ref):
    parts, taken, depth = rows_ref.shape
    out_ref[...] = lax.dot_general(
        rows_ref[...].reshape(parts * taken, depth), weight_ref[...], (((1,), (1,)), ((), ())),
        preferred_element_type=jnp.float32,
    ).astype(out_ref.dtype).reshape(out_ref.shape)


def project(rows, weight, chunk, chunks):
    parts, tokens, depth = rows.shape
    width = weight.shape[0]
    taken = tokens // chunks
    block = min(width, 256)
    return pl.pallas_call(
        project_kernel,
        grid=(width // block,),
        in_specs=[
            pl.BlockSpec((parts, taken, depth), lambda i: (0, chunk, 0)),
            pl.BlockSpec((block, depth), lambda i: (i, 0)),
        ],
        out_specs=pl.BlockSpec((parts, taken, block), lambda i: (0, 0, i)),
        out_shape=jax.ShapeDtypeStruct((parts, taken, width), jnp.bfloat16),
        compiler_params=params(48),
        cost_estimate=cost(2 * parts * taken * depth * width, 2 * (parts * taken * (depth + width) + width * depth)),
        name="project",
    )(rows, weight)


def backward_kernel(cot_ref, x_ref, gain_ref, grad_ref, out_ref):
    parts, _, width = cot_ref.shape
    values = x_ref[...].astype(jnp.float32)
    inverse = lax.rsqrt(jnp.mean(values * values, axis=-1, keepdims=True) + norm_eps)
    inner = jnp.zeros_like(inverse)
    for part in range(parts):
        cols = slice(part * width, (part + 1) * width)
        scaled = gain_ref[:, cols].astype(jnp.float32) * cot_ref[part].astype(jnp.float32)
        inner += jnp.sum(values[:, cols] * scaled, axis=-1, keepdims=True)
    factor = inverse * inverse * inverse * (inner / (parts * width))
    for part in range(parts):
        cols = slice(part * width, (part + 1) * width)
        scaled = gain_ref[:, cols].astype(jnp.float32) * cot_ref[part].astype(jnp.float32)
        out_ref[:, cols] = (
            grad_ref[:, cols].astype(jnp.float32) + inverse * scaled - values[:, cols] * factor
        ).astype(out_ref.dtype)


def norm_backward(cot, rows, gain, grads, chunk, chunks):
    parts, taken, part_width = cot.shape
    tokens, width = rows.shape
    block = min(taken, 32)
    first = chunk * (taken // block)
    return pl.pallas_call(
        backward_kernel,
        grid=(taken // block,),
        in_specs=[
            pl.BlockSpec((parts, block, part_width), lambda i: (0, i, 0)),
            pl.BlockSpec((block, width), lambda i: (first + i, 0)),
            pl.BlockSpec((1, width), lambda i: (0, 0)),
            pl.BlockSpec((block, width), lambda i: (first + i, 0)),
        ],
        out_specs=pl.BlockSpec((block, width), lambda i: (i, 0)),
        out_shape=jax.ShapeDtypeStruct((taken, width), jnp.bfloat16),
        compiler_params=params(24),
        cost_estimate=cost(10 * taken * width, 8 * taken * width),
        name="norm_backward",
    )(cot, rows, gain, grads)


def outer_kernel(columns_ref, cot_ref, *rest):
    out_ref = rest[-1]
    parts, taken, width = columns_ref.shape
    product = lax.dot_general(
        columns_ref[...].reshape(parts * taken, width),
        cot_ref[...].reshape(parts * taken, cot_ref.shape[2]),
        (((0,), (0,)), ((), ())),
        preferred_element_type=jnp.float32,
    )
    if len(rest) > 1:
        product += rest[0][...]
    out_ref[...] = product


def outer(columns, cot, before, chunk, chunks):
    parts, taken, width = columns.shape
    cot_width = cot.shape[2]
    block = min(width, 256)
    out_spec = pl.BlockSpec((block, cot_width), lambda i: (i, 0))
    operands = [columns, cot] + ([] if before is None else [before])
    return pl.pallas_call(
        outer_kernel,
        grid=(width // block,),
        in_specs=[
            pl.BlockSpec((parts, taken, block), lambda i: (0, 0, i)),
            pl.BlockSpec((parts, taken, cot_width), lambda i: (0, chunk, 0)),
        ] + ([] if before is None else [out_spec]),
        out_specs=out_spec,
        out_shape=jax.ShapeDtypeStruct((width, cot_width), jnp.float32),
        compiler_params=params(32),
        cost_estimate=cost(2 * parts * taken * width * cot_width, 4 * parts * taken * width),
        name="outer",
    )(*operands)


def exchange(blocks):
    return lax.all_to_all(blocks, "dp", split_axis=0, concat_axis=0, tiled=True)


def shards(
    new_input,
    new_gain,
    queries,
    new_keys,
    context_grad,
    segment_ids,
    frozen_input,
    frozen_gain,
    output_grad,
    kv_grad,
    kv_weight,
):
    parts = lax.axis_size("dp")
    chunks = CHUNKS
    kv_all = lax.all_gather(kv_grad[0], "dp", axis=0, tiled=False)
    columns = [exchange(normalize(new_input[0], new_gain, parts, 0, chunks))]
    value_cot = attend(queries[0], new_keys[0], context_grad[0], segment_ids)
    cot_all = lax.all_gather(value_cot, "dp", axis=0, tiled=False)
    below = []
    for chunk in range(chunks):
        own = exchange(project(kv_all, kv_weight[0], chunk, chunks))
        input_cot = norm_backward(own, frozen_input[0], frozen_gain, output_grad[0], chunk, chunks)
        below.append(from_behind(input_cot, "pipe", -1))
    for chunk in range(1, chunks):
        columns.append(exchange(normalize(new_input[0], new_gain, parts, chunk, chunks)))
    grad = None
    for chunk in range(chunks):
        grad = outer(columns[chunk], cot_all, grad, chunk, chunks)
    return (jnp.concatenate(below, axis=0)[None], grad[None])


def solution(mesh):
    placed = (
        P("pipe", "dp", None),
        P("pipe", None),
        P("pipe", "dp", None),
        P("pipe", "dp", None),
        P("pipe", "dp", None),
        P("pipe", "dp"),
        P("pipe", "dp", None),
        P("pipe", None),
        P("pipe", "dp", None),
        P("pipe", "dp", None),
        P("pipe", "dp", None),
    )
    return jax.shard_map(
        shards,
        mesh=mesh,
        in_specs=placed,
        out_specs=(P("pipe", "dp", None), P("pipe", "dp", None)),
        check_vma=False,
    )
```

```python
import functools
import math

import jax
import jax.numpy as jnp
from jax import lax
from jax.experimental import pallas as pl
from jax.experimental.pallas import tpu as pltpu
from jax.sharding import PartitionSpec as P

HEAD = 128
CORES = 2
CHUNKS = 2
MIB = 1 << 20

norm_eps = 1e-05
masked_value = -1e30

whole = pl.BlockSpec(memory_space=pl.ANY)
scalars = pl.BlockSpec(memory_space=pltpu.SMEM)


def from_behind(array, axis, by):
    length = lax.axis_size(axis)
    pairs = [(i, i + by) for i in range(length) if 0 <= i + by < length]
    return lax.ppermute(array, axis, pairs)


def along_chips(array, by):
    length = lax.axis_size("dp")
    return lax.ppermute(array, "dp", [(i, (i + by * CORES) % length) for i in range(length)])


def swap_cores(array):
    length = lax.axis_size("dp")
    return lax.ppermute(array, "dp", [(i, i ^ 1) for i in range(length)])


def gather_chips(array):
    length = lax.axis_size("dp")
    groups = [list(range(core, length, CORES)) for core in range(CORES)]
    return lax.all_gather(array, "dp", axis=0, tiled=False, axis_index_groups=groups)


def call(body, name, flops, nbytes, vmem=24, **kwargs):
    return pl.pallas_call(
        body,
        name=name,
        compiler_params=pltpu.CompilerParams(vmem_limit_bytes=vmem * MIB),
        cost_estimate=pl.CostEstimate(flops=flops, bytes_accessed=nbytes, transcendentals=0),
        **kwargs,
    )


def part_columns(chip, half, core, width):
    owner = chip * CORES + (core if half == 0 else CORES - 1 - core)
    return pl.ds(pl.multiple_of(owner * width, width), width)


def norm_kernel(chips, ahead, place_ref, x_ref, gain_ref, *rest):
    out_refs = rest[-len(ahead):]
    chip, core = place_ref[0], place_ref[1]
    values = x_ref[...].astype(jnp.float32)
    inverse = lax.rsqrt(jnp.mean(values * values, axis=-1, keepdims=True) + norm_eps)
    width = out_refs[0].shape[1] // CORES
    for by, out_ref in zip(ahead, out_refs):
        to = lax.rem(chip + by, chips)
        for half in range(CORES):
            cols = part_columns(to, half, core, width)
            out_ref[:, half * width:(half + 1) * width] = (
                x_ref[:, cols].astype(jnp.float32) * inverse * gain_ref[:, cols].astype(jnp.float32)
            ).astype(out_ref.dtype)


def normalize(place, rows, gain, chips, ahead, after):
    tokens, width = rows.shape
    block = min(tokens, 32)
    out_width = width // chips
    return call(
        functools.partial(norm_kernel, chips, ahead), "norm_forward",
        4 * tokens * width, 2 * tokens * width + 2 * tokens * out_width * len(ahead),
        grid=(tokens // block,),
        in_specs=[
            scalars,
            pl.BlockSpec((block, width), lambda i: (i, 0)),
            pl.BlockSpec((1, width), lambda i: (0, 0)),
        ] + [whole] * len(after),
        out_specs=[pl.BlockSpec((block, out_width), lambda i: (i, 0))] * len(ahead),
        out_shape=[jax.ShapeDtypeStruct((tokens, out_width), jnp.bfloat16)] * len(ahead),
    )(place, rows, gain, *after)


def attend_kernel(query_ref, key_ref, grad_ref, row_seg_ref, col_seg_ref, out_ref):
    tokens = key_ref.shape[0]
    group = query_ref.shape[1] // HEAD
    at_query = lax.broadcasted_iota(jnp.int32, (tokens, tokens), 0)
    at_key = lax.broadcasted_iota(jnp.int32, (tokens, tokens), 1)
    visible = (col_seg_ref[...] == row_seg_ref[...]) & (at_key <= at_query)
    keys = key_ref[...]
    total = jnp.zeros((tokens, HEAD), jnp.float32)
    for head in range(group):
        cols = slice(head * HEAD, (head + 1) * HEAD)
        scores = lax.dot_general(
            query_ref[:, cols], keys, (((1,), (1,)), ((), ())),
            preferred_element_type=jnp.float32,
        ) / math.sqrt(HEAD)
        masked = jnp.where(visible, scores, masked_value)
        highest = jnp.max(masked, axis=-1, keepdims=True)
        weights = jnp.where(visible, jnp.exp(masked - highest), 0.0)
        attention = (weights / jnp.sum(weights, axis=-1, keepdims=True)).astype(jnp.bfloat16)
        total += lax.dot_general(
            attention, grad_ref[:, cols], (((0,), (0,)), ((), ())),
            preferred_element_type=jnp.float32,
        )
    out_ref[...] = total.astype(out_ref.dtype)


def attend(queries, keys, grads, segments):
    tokens, kv_width = keys.shape
    heads = kv_width // HEAD
    wide = queries.shape[1] // heads
    return call(
        attend_kernel, "attend",
        4 * tokens * tokens * queries.shape[1], 4 * tokens * queries.shape[1],
        grid=(heads,),
        in_specs=[
            pl.BlockSpec((tokens, wide), lambda i: (0, i)),
            pl.BlockSpec((tokens, HEAD), lambda i: (0, i)),
            pl.BlockSpec((tokens, wide), lambda i: (0, i)),
            pl.BlockSpec((1, tokens), lambda i: (0, 0)),
            pl.BlockSpec((tokens, 1), lambda i: (0, 0)),
        ],
        out_specs=pl.BlockSpec((tokens, HEAD), lambda i: (0, i)),
        out_shape=jax.ShapeDtypeStruct((tokens, kv_width), jnp.bfloat16),
    )(queries, keys, grads, segments, segments.reshape(tokens, 1))


def project_kernel(steps, place_ref, rows_ref, own_ref, other_ref, *rest):
    out_refs, turned = rest[:-1], rest[-1]
    chips, taken, depth = rows_ref.shape
    step = pl.program_id(0)

    @pl.when(step == 0)
    def _():
        for by in range(chips):
            turned[by] = rows_ref[lax.rem(place_ref[0] + by, chips)]

    def multiply(weight_ref):
        product = lax.dot_general(
            turned[...].reshape(chips * taken, depth), weight_ref[...], (((1,), (1,)), ((), ())),
            preferred_element_type=jnp.float32,
        ).astype(jnp.bfloat16)
        for by in range(chips):
            out_refs[by][...] = product[by * taken:(by + 1) * taken]

    @pl.when(step < steps)
    def _():
        multiply(own_ref)

    @pl.when(step >= steps)
    def _():
        multiply(other_ref)


def project(place, rows, own, other, chunk, chunks):
    chips, tokens, depth = rows.shape
    width = own.shape[0]
    taken = tokens // chunks
    block = min(width, 256)
    steps = width // block
    return call(
        functools.partial(project_kernel, steps), "project",
        4 * chips * taken * depth * width, 2 * (chips * taken * (depth + 2 * width) + 2 * width * depth),
        grid=(CORES * steps,),
        in_specs=[
            scalars,
            pl.BlockSpec((chips, taken, depth), lambda i: (0, chunk, 0)),
            pl.BlockSpec((block, depth), lambda i: (jnp.minimum(i, steps - 1), 0)),
            pl.BlockSpec((block, depth), lambda i: (jnp.maximum(i - steps, 0), 0)),
        ],
        out_specs=[pl.BlockSpec((taken, block), lambda i: (0, i))] * chips,
        out_shape=[jax.ShapeDtypeStruct((taken, CORES * width), jnp.bfloat16)] * chips,
        scratch_shapes=[pltpu.VMEM((chips, taken, depth), jnp.bfloat16)],
    )(place, rows, own, other)


def backward_kernel(chips, place_ref, x_ref, gain_ref, grad_ref, *rest):
    cot_refs, out_ref = rest[:-1], rest[-1]
    chip, core = place_ref[0], place_ref[1]
    values = x_ref[...].astype(jnp.float32)
    width = cot_refs[0].shape[1] // CORES
    inverse = lax.rsqrt(jnp.mean(values * values, axis=-1, keepdims=True) + norm_eps)
    inner = jnp.zeros_like(inverse)

    def parts():
        for by, cot_ref in enumerate(cot_refs):
            source = lax.rem(chip + chips - by, chips)
            for half in range(CORES):
                cols = part_columns(source, half, core, width)
                cot = cot_ref[:, half * width:(half + 1) * width].astype(jnp.float32)
                yield cols, gain_ref[:, cols].astype(jnp.float32) * cot

    for cols, scaled in parts():
        inner += jnp.sum(x_ref[:, cols].astype(jnp.float32) * scaled, axis=-1, keepdims=True)
    factor = inverse * inverse * inverse * (inner / x_ref.shape[1])
    for cols, scaled in parts():
        out_ref[:, cols] = (
            grad_ref[:, cols].astype(jnp.float32)
            + inverse * scaled
            - x_ref[:, cols].astype(jnp.float32) * factor
        ).astype(out_ref.dtype)


def norm_backward(place, cots, rows, gain, grads, chunk, chunks):
    tokens, width = rows.shape
    taken, part_width = cots[0].shape
    block = min(taken, 32)
    first = chunk * (taken // block)
    return call(
        functools.partial(backward_kernel, len(cots)), "norm_backward",
        10 * taken * width, 8 * taken * width,
        grid=(taken // block,),
        in_specs=[
            scalars,
            pl.BlockSpec((block, width), lambda i: (first + i, 0)),
            pl.BlockSpec((1, width), lambda i: (0, 0)),
            pl.BlockSpec((block, width), lambda i: (first + i, 0)),
        ] + [pl.BlockSpec((block, part_width), lambda i: (i, 0))] * len(cots),
        out_specs=pl.BlockSpec((block, width), lambda i: (i, 0)),
        out_shape=jax.ShapeDtypeStruct((taken, width), jnp.bfloat16),
    )(place, rows, gain, grads, *cots)


def outer_kernel(chips, aheads, sums, place_ref, cot_ref, *rest):
    columns, terms, out_ref = rest[:len(aheads)], rest[len(aheads):-1], rest[-1]
    total = None
    for by, column_ref in zip(aheads, columns):
        source = lax.rem(place_ref[0] + chips - by, chips)
        product = lax.dot_general(
            column_ref[...], cot_ref[source], (((0,), (0,)), ((), ())),
            preferred_element_type=jnp.float32,
        )
        total = product if total is None else total + product
    for term in terms:
        total += term[...].astype(jnp.float32)
    out_ref[...] = total.astype(out_ref.dtype)


def outer(place, columns, cot, aheads, half, before, dtype):
    chips, tokens, cot_width = cot.shape
    width = columns[0].shape[1] // CORES
    block = min(width, 256)
    first = half * (width // block)
    out_spec = pl.BlockSpec((block, cot_width), lambda i: (i, 0))
    return call(
        functools.partial(outer_kernel, chips, aheads, len(before)), "outer",
        2 * len(columns) * tokens * width * cot_width, 2 * len(columns) * tokens * width + 4 * width * cot_width,
        grid=(width // block,),
        in_specs=[
            scalars,
            pl.BlockSpec((chips, tokens, cot_width), lambda i: (0, 0, 0)),
        ] + [pl.BlockSpec((tokens, block), lambda i: (0, first + i))] * len(columns)
        + [out_spec] * len(before),
        out_specs=out_spec,
        out_shape=jax.ShapeDtypeStruct((width, cot_width), dtype),
    )(place, cot, *columns, *before)


def shards(
    new_input,
    new_gain,
    queries,
    new_keys,
    context_grad,
    segment_ids,
    frozen_input,
    frozen_gain,
    output_grad,
    kv_grad,
    kv_weight,
):
    chips = lax.axis_size("dp") // CORES
    chunks = CHUNKS
    at = lax.axis_index("dp")
    place = jnp.stack([at // CORES, at % CORES]).astype(jnp.int32)
    middle = chips // 2
    order = [by for by in range(1, chips) if by != middle] + [middle]

    kv_all = gather_chips(kv_grad[0])
    other_weight = swap_cores(kv_weight[0])
    value_cot = attend(queries[0], new_keys[0], context_grad[0], segment_ids)
    cot_all = gather_chips(value_cot)

    projected, arrived = [], []
    for chunk in range(chunks):
        blocks = project(place, kv_all, kv_weight[0], other_weight, chunk, chunks)
        projected.append(blocks[0])
        arrived.append([blocks[0]] + [along_chips(blocks[by], by) for by in range(1, chips)])

    aheads = [0] + order
    blocks = normalize(place, new_input[0], new_gain, chips, aheads, projected)
    columns = [blocks[0]] + [along_chips(block, by) for block, by in zip(blocks[1:], order)]

    below = []
    for chunk in range(chunks):
        input_cot = norm_backward(place, arrived[chunk], frozen_input[0], frozen_gain, output_grad[0], chunk, chunks)
        below.append(from_behind(input_cot, "pipe", -1))

    early = [
        outer(place, columns[:-1], cot_all, aheads[:-1], half, [], jnp.float32) for half in range(CORES)
    ]
    given = outer(place, columns[-1:], cot_all, aheads[-1:], 1, [early[1]], jnp.bfloat16)
    taken = swap_cores(given)
    grad = outer(place, columns[-1:], cot_all, aheads[-1:], 0, [early[0], taken], jnp.float32)
    return (jnp.concatenate(below, axis=0)[None], grad[None])


def solution(mesh):
    placed = (
        P("pipe", "dp", None),
        P("pipe", None),
        P("pipe", "dp", None),
        P("pipe", "dp", None),
        P("pipe", "dp", None),
        P("pipe", "dp"),
        P("pipe", "dp", None),
        P("pipe", None),
        P("pipe", "dp", None),
        P("pipe", "dp", None),
        P("pipe", "dp", None),
    )
    return jax.shard_map(
        shards,
        mesh=mesh,
        in_specs=placed,
        out_specs=(P("pipe", "dp", None), P("pipe", "dp", None)),
        check_vma=False,
    )
```

```python
import functools
import math

import jax
import jax.numpy as jnp
from jax import lax
from jax.experimental import pallas as pl
from jax.experimental.pallas import tpu as pltpu
from jax.sharding import PartitionSpec as P

HEAD = 128
CORES = 2
MIB = 1 << 20

norm_eps = 1e-05
masked_value = -1e30

whole = pl.BlockSpec(memory_space=pl.ANY)
scalars = pl.BlockSpec(memory_space=pltpu.SMEM)


def from_behind(array, axis, by):
    length = lax.axis_size(axis)
    pairs = [(i, i + by) for i in range(length) if 0 <= i + by < length]
    return lax.ppermute(array, axis, pairs)


def along_chips(array, by):
    length = lax.axis_size("dp")
    return lax.ppermute(array, "dp", [(i, (i + by * CORES) % length) for i in range(length)])


def swap_cores(array):
    length = lax.axis_size("dp")
    return lax.ppermute(array, "dp", [(i, i ^ 1) for i in range(length)])


def call(body, name, flops, nbytes, vmem=24, **kwargs):
    return pl.pallas_call(
        body,
        name=name,
        compiler_params=pltpu.CompilerParams(vmem_limit_bytes=vmem * MIB),
        cost_estimate=pl.CostEstimate(flops=flops, bytes_accessed=nbytes, transcendentals=0),
        **kwargs,
    )


def part_columns(chip, half, core, width):
    owner = chip * CORES + (core if half == 0 else CORES - 1 - core)
    return pl.ds(pl.multiple_of(owner * width, width), width)


def norm_kernel(chips, ahead, place_ref, x_ref, gain_ref, cot_ref, *rest):
    out_refs = rest[-len(ahead):]
    chip, core = place_ref[0], place_ref[1]
    values = x_ref[...].astype(jnp.float32)
    inverse = lax.rsqrt(jnp.mean(values * values, axis=-1, keepdims=True) + norm_eps)
    front = cot_ref.shape[1]
    width = (out_refs[0].shape[1] - front) // CORES
    for by, out_ref in zip(ahead, out_refs):
        to = lax.rem(chip + by, chips)
        out_ref[:, :front] = cot_ref[...]
        for half in range(CORES):
            cols = part_columns(to, half, core, width)
            out_ref[:, front + half * width:front + (half + 1) * width] = (
                x_ref[:, cols].astype(jnp.float32) * inverse * gain_ref[:, cols].astype(jnp.float32)
            ).astype(out_ref.dtype)


def normalize(place, rows, gain, cot, chips, ahead, after):
    tokens, width = rows.shape
    front = cot.shape[1]
    block = min(tokens, 32)
    out_width = front + width // chips
    return call(
        functools.partial(norm_kernel, chips, ahead), "norm_forward",
        4 * tokens * width, 2 * tokens * width + 2 * tokens * out_width * len(ahead),
        grid=(tokens // block,),
        in_specs=[
            scalars,
            pl.BlockSpec((block, width), lambda i: (i, 0)),
            pl.BlockSpec((1, width), lambda i: (0, 0)),
            pl.BlockSpec((block, front), lambda i: (i, 0)),
        ] + [whole] * len(after),
        out_specs=[pl.BlockSpec((block, out_width), lambda i: (i, 0))] * len(ahead),
        out_shape=[jax.ShapeDtypeStruct((tokens, out_width), jnp.bfloat16)] * len(ahead),
    )(place, rows, gain, cot, *after)


def attend_kernel(query_ref, key_ref, grad_ref, row_seg_ref, col_seg_ref, out_ref):
    tokens = key_ref.shape[0]
    group = query_ref.shape[1] // HEAD
    at_query = lax.broadcasted_iota(jnp.int32, (tokens, tokens), 0)
    at_key = lax.broadcasted_iota(jnp.int32, (tokens, tokens), 1)
    visible = (col_seg_ref[...] == row_seg_ref[...]) & (at_key <= at_query)
    keys = key_ref[...]
    total = jnp.zeros((tokens, HEAD), jnp.float32)
    for head in range(group):
        cols = slice(head * HEAD, (head + 1) * HEAD)
        scores = lax.dot_general(
            query_ref[:, cols], keys, (((1,), (1,)), ((), ())),
            preferred_element_type=jnp.float32,
        ) / math.sqrt(HEAD)
        masked = jnp.where(visible, scores, masked_value)
        highest = jnp.max(masked, axis=-1, keepdims=True)
        weights = jnp.where(visible, jnp.exp(masked - highest), 0.0)
        attention = (weights / jnp.sum(weights, axis=-1, keepdims=True)).astype(jnp.bfloat16)
        total += lax.dot_general(
            attention, grad_ref[:, cols], (((0,), (0,)), ((), ())),
            preferred_element_type=jnp.float32,
        )
    out_ref[...] = total.astype(out_ref.dtype)


def attend(queries, keys, grads, segments):
    tokens, kv_width = keys.shape
    heads = kv_width // HEAD
    wide = queries.shape[1] // heads
    return call(
        attend_kernel, "attend",
        4 * tokens * tokens * queries.shape[1], 4 * tokens * queries.shape[1],
        grid=(heads,),
        in_specs=[
            pl.BlockSpec((tokens, wide), lambda i: (0, i)),
            pl.BlockSpec((tokens, HEAD), lambda i: (0, i)),
            pl.BlockSpec((tokens, wide), lambda i: (0, i)),
            pl.BlockSpec((1, tokens), lambda i: (0, 0)),
            pl.BlockSpec((tokens, 1), lambda i: (0, 0)),
        ],
        out_specs=pl.BlockSpec((tokens, HEAD), lambda i: (0, i)),
        out_shape=jax.ShapeDtypeStruct((tokens, kv_width), jnp.bfloat16),
    )(queries, keys, grads, segments, segments.reshape(tokens, 1))


def project_kernel(chips, steps, own_ref, other_ref, *rest):
    row_refs, out_refs, gathered = rest[:chips], rest[-chips - 1:-1], rest[-1]
    taken, depth = row_refs[0].shape
    step = pl.program_id(0)

    @pl.when(step == 0)
    def _():
        for by in range(chips):
            gathered[by] = row_refs[by][...]

    def multiply(weight_ref):
        product = lax.dot_general(
            gathered[...].reshape(chips * taken, depth), weight_ref[...], (((1,), (1,)), ((), ())),
            preferred_element_type=jnp.float32,
        ).astype(jnp.bfloat16)
        for by in range(chips):
            out_refs[by][...] = product[by * taken:(by + 1) * taken]

    @pl.when(step < steps)
    def _():
        multiply(own_ref)

    @pl.when(step >= steps)
    def _():
        multiply(other_ref)


def project(rows, own, other, after):
    chips = len(rows)
    taken, depth = rows[0].shape
    width = own.shape[0]
    block = min(width, 256)
    steps = width // block
    return call(
        functools.partial(project_kernel, chips, steps), "project",
        4 * chips * taken * depth * width, 2 * (chips * taken * (depth + 2 * width) + 2 * width * depth),
        grid=(CORES * steps,),
        in_specs=[
            pl.BlockSpec((block, depth), lambda i: (jnp.minimum(i, steps - 1), 0)),
            pl.BlockSpec((block, depth), lambda i: (jnp.maximum(i - steps, 0), 0)),
        ] + [pl.BlockSpec((taken, depth), lambda i: (0, 0))] * chips + [whole] * len(after),
        out_specs=[pl.BlockSpec((taken, block), lambda i: (0, i))] * chips,
        out_shape=[jax.ShapeDtypeStruct((taken, CORES * width), jnp.bfloat16)] * chips,
        scratch_shapes=[pltpu.VMEM((chips, taken, depth), jnp.bfloat16)],
    )(own, other, *rows, *after)


def backward_kernel(chips, place_ref, x_ref, gain_ref, grad_ref, *rest):
    cot_refs, out_ref = rest[:chips], rest[-1]
    chip, core = place_ref[0], place_ref[1]
    values = x_ref[...].astype(jnp.float32)
    width = cot_refs[0].shape[1] // CORES
    inverse = lax.rsqrt(jnp.mean(values * values, axis=-1, keepdims=True) + norm_eps)
    inner = jnp.zeros_like(inverse)

    def parts():
        for by, cot_ref in enumerate(cot_refs):
            source = lax.rem(chip + chips - by, chips)
            for half in range(CORES):
                cols = part_columns(source, half, core, width)
                cot = cot_ref[:, half * width:(half + 1) * width].astype(jnp.float32)
                yield cols, gain_ref[:, cols].astype(jnp.float32) * cot

    for cols, scaled in parts():
        inner += jnp.sum(x_ref[:, cols].astype(jnp.float32) * scaled, axis=-1, keepdims=True)
    factor = inverse * inverse * inverse * (inner / x_ref.shape[1])
    for cols, scaled in parts():
        out_ref[:, cols] = (
            grad_ref[:, cols].astype(jnp.float32)
            + inverse * scaled
            - x_ref[:, cols].astype(jnp.float32) * factor
        ).astype(out_ref.dtype)


def norm_backward(place, cots, rows, gain, grads, after):
    tokens, width = rows.shape
    taken, part_width = cots[0].shape
    block = min(taken, 32)
    return call(
        functools.partial(backward_kernel, len(cots)), "norm_backward",
        10 * taken * width, 8 * taken * width,
        grid=(taken // block,),
        in_specs=[
            scalars,
            pl.BlockSpec((block, width), lambda i: (i, 0)),
            pl.BlockSpec((1, width), lambda i: (0, 0)),
            pl.BlockSpec((block, width), lambda i: (i, 0)),
        ] + [pl.BlockSpec((block, part_width), lambda i: (i, 0))] * len(cots) + [whole] * len(after),
        out_specs=pl.BlockSpec((block, width), lambda i: (i, 0)),
        out_shape=jax.ShapeDtypeStruct((taken, width), jnp.bfloat16),
    )(place, rows, gain, grads, *cots, *after)


def outer_kernel(arrays, sums, *refs):
    cots, columns, terms = refs[:arrays], refs[arrays:2 * arrays], refs[2 * arrays:2 * arrays + sums]
    total = None
    for cot_ref, column_ref in zip(cots, columns):
        product = lax.dot_general(
            column_ref[...], cot_ref[...], (((0,), (0,)), ((), ())),
            preferred_element_type=jnp.float32,
        )
        total = product if total is None else total + product
    for term in terms:
        total += term[...].astype(jnp.float32)
    refs[-1][...] = total.astype(refs[-1].dtype)


def outer(payloads, cot_width, half, before, dtype, after):
    tokens, wide = payloads[0].shape
    width = (wide - cot_width) // CORES
    block = math.gcd(math.gcd(width, 256), cot_width)
    first = (cot_width + half * width) // block
    out_spec = pl.BlockSpec((block, cot_width), lambda i: (i, 0))
    arrays = len(payloads)
    return call(
        functools.partial(outer_kernel, arrays, len(before)), "outer",
        2 * arrays * tokens * width * cot_width, 2 * arrays * tokens * width + 4 * width * cot_width,
        grid=(width // block,),
        in_specs=[pl.BlockSpec((tokens, cot_width), lambda i: (0, 0))] * arrays
        + [pl.BlockSpec((tokens, block), lambda i: (0, first + i))] * arrays
        + [out_spec] * len(before) + [whole] * len(after),
        out_specs=out_spec,
        out_shape=jax.ShapeDtypeStruct((width, cot_width), dtype),
    )(*payloads, *payloads, *before, *after)


def shards(
    new_input,
    new_gain,
    queries,
    new_keys,
    context_grad,
    segment_ids,
    frozen_input,
    frozen_gain,
    output_grad,
    kv_grad,
    kv_weight,
):
    chips = lax.axis_size("dp") // CORES
    kv_width = new_keys.shape[2]
    at = lax.axis_index("dp")
    place = jnp.stack([at // CORES, at % CORES]).astype(jnp.int32)
    middle = chips // 2
    order = [by for by in range(1, chips) if by != middle] + [middle]
    first, later = order[:1], order[1:]

    rows = [kv_grad[0]] + [along_chips(kv_grad[0], chips - by) for by in range(1, chips)]
    other_weight = swap_cores(kv_weight[0])
    value_cot = attend(queries[0], new_keys[0], context_grad[0], segment_ids)

    after = [rows[by] for by in order[:-1]]
    early = normalize(place, new_input[0], new_gain, value_cot, chips, [0] + first, after)
    columns = [early[0]] + [along_chips(block, by) for block, by in zip(early[1:], first)]

    parts = project(rows, kv_weight[0], other_weight, early[:1])
    arrived = [parts[0]] + [along_chips(parts[by], by) for by in range(1, chips)]

    after = [arrived[by] for by in order[:-1]]
    late = normalize(place, new_input[0], new_gain, value_cot, chips, later, after)
    columns += [along_chips(block, by) for block, by in zip(late, later)]

    input_cot = norm_backward(place, arrived, frozen_input[0], frozen_gain, output_grad[0], [late[0]] + columns[1:1 + len(first)])
    cot_below = from_behind(input_cot, "pipe", -1)

    sums = [outer(columns[:-1], kv_width, half, [], jnp.float32, []) for half in range(CORES)]
    given = outer(columns[-1:], kv_width, 1, [sums[1]], jnp.bfloat16, [cot_below])
    taken = swap_cores(given)
    grad = outer(columns[-1:], kv_width, 0, [sums[0], taken], jnp.float32, [])
    return (cot_below[None], grad[None])


def solution(mesh):
    placed = (
        P("pipe", "dp", None),
        P("pipe", None),
        P("pipe", "dp", None),
        P("pipe", "dp", None),
        P("pipe", "dp", None),
        P("pipe", "dp"),
        P("pipe", "dp", None),
        P("pipe", None),
        P("pipe", "dp", None),
        P("pipe", "dp", None),
        P("pipe", "dp", None),
    )
    return jax.shard_map(
        shards,
        mesh=mesh,
        in_specs=placed,
        out_specs=(P("pipe", "dp", None), P("pipe", "dp", None)),
        check_vma=False,
    )
```

```python
import functools
import math

import jax
import jax.numpy as jnp
from jax import lax
from jax.experimental import pallas as pl
from jax.experimental.pallas import tpu as pltpu
from jax.sharding import PartitionSpec as P

HEAD = 128
CORES = 2
MIB = 1 << 20

norm_eps = 1e-05
masked_value = -1e30

whole = pl.BlockSpec(memory_space=pl.ANY)
scalars = pl.BlockSpec(memory_space=pltpu.SMEM)


def from_behind(array, axis, by):
    length = lax.axis_size(axis)
    pairs = [(i, i + by) for i in range(length) if 0 <= i + by < length]
    return lax.ppermute(array, axis, pairs)


def along_chips(array, by):
    length = lax.axis_size("dp")
    return lax.ppermute(array, "dp", [(i, (i + by * CORES) % length) for i in range(length)])


def swap_cores(array):
    length = lax.axis_size("dp")
    return lax.ppermute(array, "dp", [(i, i ^ 1) for i in range(length)])


def call(body, name, flops, nbytes, vmem=24, **kwargs):
    return pl.pallas_call(
        body,
        name=name,
        compiler_params=pltpu.CompilerParams(vmem_limit_bytes=vmem * MIB),
        cost_estimate=pl.CostEstimate(flops=flops, bytes_accessed=nbytes, transcendentals=0),
        **kwargs,
    )


def part_columns(chip, half, core, width):
    owner = chip * CORES + (core if half == 0 else CORES - 1 - core)
    return pl.ds(pl.multiple_of(owner * width, width), width)


def norm_kernel(chips, ahead, place_ref, x_ref, gain_ref, cot_ref, *rest):
    out_refs = rest[-len(ahead):]
    chip, core = place_ref[0], place_ref[1]
    values = x_ref[...].astype(jnp.float32)
    inverse = lax.rsqrt(jnp.mean(values * values, axis=-1, keepdims=True) + norm_eps)
    front = cot_ref.shape[1]
    width = (out_refs[0].shape[1] - front) // CORES
    for by, out_ref in zip(ahead, out_refs):
        to = lax.rem(chip + by, chips)
        out_ref[:, :front] = cot_ref[...]
        for half in range(CORES):
            cols = part_columns(to, half, core, width)
            out_ref[:, front + half * width:front + (half + 1) * width] = (
                x_ref[:, cols].astype(jnp.float32) * inverse * gain_ref[:, cols].astype(jnp.float32)
            ).astype(out_ref.dtype)


def normalize(place, rows, gain, cot, chips, ahead, after):
    tokens, width = rows.shape
    front = cot.shape[1]
    block = min(tokens, 32)
    out_width = front + width // chips
    return call(
        functools.partial(norm_kernel, chips, ahead), "norm_forward",
        4 * tokens * width, 2 * tokens * width + 2 * tokens * out_width * len(ahead),
        grid=(tokens // block,),
        in_specs=[
            scalars,
            pl.BlockSpec((block, width), lambda i: (i, 0)),
            pl.BlockSpec((1, width), lambda i: (0, 0)),
            pl.BlockSpec((block, front), lambda i: (i, 0)),
        ] + [whole] * len(after),
        out_specs=[pl.BlockSpec((block, out_width), lambda i: (i, 0))] * len(ahead),
        out_shape=[jax.ShapeDtypeStruct((tokens, out_width), jnp.bfloat16)] * len(ahead),
    )(place, rows, gain, cot, *after)


def attend_kernel(query_ref, key_ref, grad_ref, row_seg_ref, col_seg_ref, out_ref):
    tokens = key_ref.shape[0]
    group = query_ref.shape[1] // HEAD
    at_query = lax.broadcasted_iota(jnp.int32, (tokens, tokens), 0)
    at_key = lax.broadcasted_iota(jnp.int32, (tokens, tokens), 1)
    visible = (col_seg_ref[...] == row_seg_ref[...]) & (at_key <= at_query)
    keys = key_ref[...]
    total = jnp.zeros((tokens, HEAD), jnp.float32)
    for head in range(group):
        cols = slice(head * HEAD, (head + 1) * HEAD)
        scores = lax.dot_general(
            query_ref[:, cols], keys, (((1,), (1,)), ((), ())),
            preferred_element_type=jnp.float32,
        ) / math.sqrt(HEAD)
        masked = jnp.where(visible, scores, masked_value)
        highest = jnp.max(masked, axis=-1, keepdims=True)
        weights = jnp.where(visible, jnp.exp(masked - highest), 0.0)
        attention = (weights / jnp.sum(weights, axis=-1, keepdims=True)).astype(jnp.bfloat16)
        total += lax.dot_general(
            attention, grad_ref[:, cols], (((0,), (0,)), ((), ())),
            preferred_element_type=jnp.float32,
        )
    out_ref[...] = total.astype(out_ref.dtype)


def attend(queries, keys, grads, segments):
    tokens, kv_width = keys.shape
    heads = kv_width // HEAD
    wide = queries.shape[1] // heads
    return call(
        attend_kernel, "attend",
        4 * tokens * tokens * queries.shape[1], 4 * tokens * queries.shape[1],
        grid=(heads,),
        in_specs=[
            pl.BlockSpec((tokens, wide), lambda i: (0, i)),
            pl.BlockSpec((tokens, HEAD), lambda i: (0, i)),
            pl.BlockSpec((tokens, wide), lambda i: (0, i)),
            pl.BlockSpec((1, tokens), lambda i: (0, 0)),
            pl.BlockSpec((tokens, 1), lambda i: (0, 0)),
        ],
        out_specs=pl.BlockSpec((tokens, HEAD), lambda i: (0, i)),
        out_shape=jax.ShapeDtypeStruct((tokens, kv_width), jnp.bfloat16),
    )(queries, keys, grads, segments, segments.reshape(tokens, 1))


def project_kernel(chips, steps, own_ref, other_ref, *rest):
    row_refs, out_refs, gathered = rest[:chips], rest[-chips - 1:-1], rest[-1]
    taken, depth = row_refs[0].shape
    step = pl.program_id(0)

    @pl.when(step == 0)
    def _():
        for by in range(chips):
            gathered[by] = row_refs[by][...]

    def multiply(weight_ref):
        product = lax.dot_general(
            gathered[...].reshape(chips * taken, depth), weight_ref[...], (((1,), (1,)), ((), ())),
            preferred_element_type=jnp.float32,
        ).astype(jnp.bfloat16)
        for by in range(chips):
            out_refs[by][...] = product[by * taken:(by + 1) * taken]

    @pl.when(step < steps)
    def _():
        multiply(own_ref)

    @pl.when(step >= steps)
    def _():
        multiply(other_ref)


def project(rows, own, other, after):
    chips = len(rows)
    taken, depth = rows[0].shape
    width = own.shape[0]
    block = min(width, 256)
    steps = width // block
    return call(
        functools.partial(project_kernel, chips, steps), "project",
        4 * chips * taken * depth * width, 2 * (chips * taken * (depth + 2 * width) + 2 * width * depth),
        grid=(CORES * steps,),
        in_specs=[
            pl.BlockSpec((block, depth), lambda i: (jnp.minimum(i, steps - 1), 0)),
            pl.BlockSpec((block, depth), lambda i: (jnp.maximum(i - steps, 0), 0)),
        ] + [pl.BlockSpec((taken, depth), lambda i: (0, 0))] * chips + [whole] * len(after),
        out_specs=[pl.BlockSpec((taken, block), lambda i: (0, i))] * chips,
        out_shape=[jax.ShapeDtypeStruct((taken, CORES * width), jnp.bfloat16)] * chips,
        scratch_shapes=[pltpu.VMEM((chips, taken, depth), jnp.bfloat16)],
    )(own, other, *rows, *after)


def backward_kernel(chips, place_ref, x_ref, gain_ref, grad_ref, *rest):
    cot_refs, out_ref = rest[:chips], rest[-1]
    chip, core = place_ref[0], place_ref[1]
    values = x_ref[...].astype(jnp.float32)
    width = cot_refs[0].shape[1] // CORES
    inverse = lax.rsqrt(jnp.mean(values * values, axis=-1, keepdims=True) + norm_eps)
    inner = jnp.zeros_like(inverse)

    def parts():
        for by, cot_ref in enumerate(cot_refs):
            source = lax.rem(chip + chips - by, chips)
            for half in range(CORES):
                cols = part_columns(source, half, core, width)
                cot = cot_ref[:, half * width:(half + 1) * width].astype(jnp.float32)
                yield cols, gain_ref[:, cols].astype(jnp.float32) * cot

    for cols, scaled in parts():
        inner += jnp.sum(x_ref[:, cols].astype(jnp.float32) * scaled, axis=-1, keepdims=True)
    factor = inverse * inverse * inverse * (inner / x_ref.shape[1])
    for cols, scaled in parts():
        out_ref[:, cols] = (
            grad_ref[:, cols].astype(jnp.float32)
            + inverse * scaled
            - x_ref[:, cols].astype(jnp.float32) * factor
        ).astype(out_ref.dtype)


def norm_backward(place, cots, rows, gain, grads, after):
    tokens, width = rows.shape
    taken, part_width = cots[0].shape
    block = min(taken, 32)
    return call(
        functools.partial(backward_kernel, len(cots)), "norm_backward",
        10 * taken * width, 8 * taken * width,
        grid=(taken // block,),
        in_specs=[
            scalars,
            pl.BlockSpec((block, width), lambda i: (i, 0)),
            pl.BlockSpec((1, width), lambda i: (0, 0)),
            pl.BlockSpec((block, width), lambda i: (i, 0)),
        ] + [pl.BlockSpec((block, part_width), lambda i: (i, 0))] * len(cots) + [whole] * len(after),
        out_specs=pl.BlockSpec((block, width), lambda i: (i, 0)),
        out_shape=jax.ShapeDtypeStruct((taken, width), jnp.bfloat16),
    )(place, rows, gain, grads, *cots, *after)


def outer_kernel(arrays, sums, *refs):
    cots, columns, terms = refs[:arrays], refs[arrays:2 * arrays], refs[2 * arrays:2 * arrays + sums]
    total = None
    for cot_ref, column_ref in zip(cots, columns):
        product = lax.dot_general(
            column_ref[...], cot_ref[...], (((0,), (0,)), ((), ())),
            preferred_element_type=jnp.float32,
        )
        total = product if total is None else total + product
    for term in terms:
        total += term[...].astype(jnp.float32)
    refs[-1][...] = total.astype(refs[-1].dtype)


def outer(payloads, cot_width, half, before, dtype, after):
    tokens, wide = payloads[0].shape
    width = (wide - cot_width) // CORES
    block = math.gcd(math.gcd(width, 256), cot_width)
    first = (cot_width + half * width) // block
    out_spec = pl.BlockSpec((block, cot_width), lambda i: (i, 0))
    arrays = len(payloads)
    return call(
        functools.partial(outer_kernel, arrays, len(before)), "outer",
        2 * arrays * tokens * width * cot_width, 2 * arrays * tokens * width + 4 * width * cot_width,
        grid=(width // block,),
        in_specs=[pl.BlockSpec((tokens, cot_width), lambda i: (0, 0))] * arrays
        + [pl.BlockSpec((tokens, block), lambda i: (0, first + i))] * arrays
        + [out_spec] * len(before) + [whole] * len(after),
        out_specs=out_spec,
        out_shape=jax.ShapeDtypeStruct((width, cot_width), dtype),
    )(*payloads, *payloads, *before, *after)


def shards(
    new_input,
    new_gain,
    queries,
    new_keys,
    context_grad,
    segment_ids,
    frozen_input,
    frozen_gain,
    output_grad,
    kv_grad,
    kv_weight,
):
    chips = lax.axis_size("dp") // CORES
    kv_width = new_keys.shape[2]
    at = lax.axis_index("dp")
    place = jnp.stack([at // CORES, at % CORES]).astype(jnp.int32)
    middle = chips // 2
    order = [by for by in range(1, chips) if by != middle] + [middle]
    first, later = order[:1], order[1:]

    rows = [kv_grad[0]] + [along_chips(kv_grad[0], chips - by) for by in range(1, chips)]
    other_weight = swap_cores(kv_weight[0])
    value_cot = attend(queries[0], new_keys[0], context_grad[0], segment_ids)

    after = rows[1:]
    early = normalize(place, new_input[0], new_gain, value_cot, chips, [0] + first, after)
    columns = [early[0]] + [along_chips(block, by) for block, by in zip(early[1:], first)]

    parts = project(rows, kv_weight[0], other_weight, early[:1])
    arrived = [parts[0]] + [along_chips(parts[by], by) for by in range(1, chips)]

    after = [arrived[by] for by in order[:-1]]
    late = normalize(place, new_input[0], new_gain, value_cot, chips, later, after)
    columns += [along_chips(block, by) for block, by in zip(late, later)]

    input_cot = norm_backward(place, arrived, frozen_input[0], frozen_gain, output_grad[0], [late[0]] + columns[1:1 + len(first)])
    cot_below = from_behind(input_cot, "pipe", -1)

    sums = [outer(columns[:-1], kv_width, half, [], jnp.float32, []) for half in range(CORES)]
    given = outer(columns[-1:], kv_width, 1, [sums[1]], jnp.bfloat16, [])
    taken = swap_cores(given)
    grad = outer(columns[-1:], kv_width, 0, [sums[0], taken], jnp.float32, [])
    return (cot_below[None], grad[None])


def solution(mesh):
    placed = (
        P("pipe", "dp", None),
        P("pipe", None),
        P("pipe", "dp", None),
        P("pipe", "dp", None),
        P("pipe", "dp", None),
        P("pipe", "dp"),
        P("pipe", "dp", None),
        P("pipe", None),
        P("pipe", "dp", None),
        P("pipe", "dp", None),
        P("pipe", "dp", None),
    )
    return jax.shard_map(
        shards,
        mesh=mesh,
        in_specs=placed,
        out_specs=(P("pipe", "dp", None), P("pipe", "dp", None)),
        check_vma=False,
    )
```

```python
import functools
import math

import jax
import jax.numpy as jnp
from jax import lax
from jax.experimental import pallas as pl
from jax.experimental.pallas import tpu as pltpu
from jax.sharding import PartitionSpec as P

HEAD = 128
CORES = 2
MIB = 1 << 20

norm_eps = 1e-05
masked_value = -1e30

whole = pl.BlockSpec(memory_space=pl.ANY)
scalars = pl.BlockSpec(memory_space=pltpu.SMEM)


def from_behind(array, axis, by):
    length = lax.axis_size(axis)
    pairs = [(i, i + by) for i in range(length) if 0 <= i + by < length]
    return lax.ppermute(array, axis, pairs)


def along_chips(array, by, first=0):
    length = lax.axis_size("dp")
    pairs = [
        (line * length + i, line * length + (i + by * CORES) % length)
        for line in range(first, lax.axis_size("pipe")) for i in range(length)
    ]
    return lax.ppermute(array, ("pipe", "dp"), pairs)


def between_lines(array, source, target):
    length = lax.axis_size("dp")
    pairs = [(source * length + i, target * length + i) for i in range(length)]
    return lax.ppermute(array, ("pipe", "dp"), pairs)


def on_line(array, by, line):
    length = lax.axis_size("dp")
    pairs = [(line * length + i, line * length + (i + by * CORES) % length) for i in range(length)]
    return lax.ppermute(array, ("pipe", "dp"), pairs)


def swap_cores(array):
    length = lax.axis_size("dp")
    return lax.ppermute(array, "dp", [(i, i ^ 1) for i in range(length)])


def call(body, name, flops, nbytes, vmem=24, **kwargs):
    return pl.pallas_call(
        body,
        name=name,
        compiler_params=pltpu.CompilerParams(vmem_limit_bytes=vmem * MIB),
        cost_estimate=pl.CostEstimate(flops=flops, bytes_accessed=nbytes, transcendentals=0),
        **kwargs,
    )


def part_columns(chip, half, core, width):
    owner = chip * CORES + (core if half == 0 else CORES - 1 - core)
    return pl.ds(pl.multiple_of(owner * width, width), width)


def norm_kernel(chips, ahead, place_ref, x_ref, gain_ref, cot_ref, *rest):
    out_refs = rest[-len(ahead):]
    chip, core = place_ref[0], place_ref[1]
    values = x_ref[...].astype(jnp.float32)
    inverse = lax.rsqrt(jnp.mean(values * values, axis=-1, keepdims=True) + norm_eps)
    front = cot_ref.shape[1]
    width = (out_refs[0].shape[1] - front) // CORES
    for by, out_ref in zip(ahead, out_refs):
        to = lax.rem(chip + by, chips)
        out_ref[:, :front] = cot_ref[...]
        for half in range(CORES):
            cols = part_columns(to, half, core, width)
            out_ref[:, front + half * width:front + (half + 1) * width] = (
                x_ref[:, cols].astype(jnp.float32) * inverse * gain_ref[:, cols].astype(jnp.float32)
            ).astype(out_ref.dtype)


def normalize(place, rows, gain, cot, chips, ahead, start, count, after):
    width = rows.shape[1]
    front = cot.shape[1]
    block = math.gcd(math.gcd(start, count), 32)
    first = start // block
    out_width = front + width // chips
    return call(
        functools.partial(norm_kernel, chips, ahead), "norm_forward",
        4 * count * width, 2 * count * width + 2 * count * out_width * len(ahead),
        grid=(count // block,),
        in_specs=[
            scalars,
            pl.BlockSpec((block, width), lambda i: (first + i, 0)),
            pl.BlockSpec((1, width), lambda i: (0, 0)),
            pl.BlockSpec((block, front), lambda i: (first + i, 0)),
        ] + [whole] * len(after),
        out_specs=[pl.BlockSpec((block, out_width), lambda i: (i, 0))] * len(ahead),
        out_shape=[jax.ShapeDtypeStruct((count, out_width), jnp.bfloat16)] * len(ahead),
    )(place, rows, gain, cot, *after)


def stack_kernel(count, *refs):
    at = 0
    for ref in refs[:count]:
        refs[-1][at:at + ref.shape[0]] = ref[...]
        at += ref.shape[0]


def stack_rows(arrays, after):
    width = arrays[0].shape[1]
    tall = sum(array.shape[0] for array in arrays)
    return call(
        functools.partial(stack_kernel, len(arrays)), "stack_rows", 0, 4 * tall * width,
        grid=(1,),
        in_specs=[pl.BlockSpec(array.shape, lambda i: (0, 0)) for array in arrays] + [whole] * len(after),
        out_specs=pl.BlockSpec((tall, width), lambda i: (0, 0)),
        out_shape=jax.ShapeDtypeStruct((tall, width), arrays[0].dtype),
    )(*arrays, *after)


def attend_kernel(query_ref, key_ref, grad_ref, row_seg_ref, col_seg_ref, out_ref):
    tokens = key_ref.shape[0]
    group = query_ref.shape[1] // HEAD
    at_query = lax.broadcasted_iota(jnp.int32, (tokens, tokens), 0)
    at_key = lax.broadcasted_iota(jnp.int32, (tokens, tokens), 1)
    visible = (col_seg_ref[...] == row_seg_ref[...]) & (at_key <= at_query)
    keys = key_ref[...]
    total = jnp.zeros((tokens, HEAD), jnp.float32)
    for head in range(group):
        cols = slice(head * HEAD, (head + 1) * HEAD)
        scores = lax.dot_general(
            query_ref[:, cols], keys, (((1,), (1,)), ((), ())),
            preferred_element_type=jnp.float32,
        ) / math.sqrt(HEAD)
        masked = jnp.where(visible, scores, masked_value)
        highest = jnp.max(masked, axis=-1, keepdims=True)
        weights = jnp.where(visible, jnp.exp(masked - highest), 0.0)
        attention = (weights / jnp.sum(weights, axis=-1, keepdims=True)).astype(jnp.bfloat16)
        total += lax.dot_general(
            attention, grad_ref[:, cols], (((0,), (0,)), ((), ())),
            preferred_element_type=jnp.float32,
        )
    out_ref[...] = total.astype(out_ref.dtype)


def attend(queries, keys, grads, segments):
    tokens, kv_width = keys.shape
    heads = kv_width // HEAD
    wide = queries.shape[1] // heads
    return call(
        attend_kernel, "attend",
        4 * tokens * tokens * queries.shape[1], 4 * tokens * queries.shape[1],
        grid=(heads,),
        in_specs=[
            pl.BlockSpec((tokens, wide), lambda i: (0, i)),
            pl.BlockSpec((tokens, HEAD), lambda i: (0, i)),
            pl.BlockSpec((tokens, wide), lambda i: (0, i)),
            pl.BlockSpec((1, tokens), lambda i: (0, 0)),
            pl.BlockSpec((tokens, 1), lambda i: (0, 0)),
        ],
        out_specs=pl.BlockSpec((tokens, HEAD), lambda i: (0, i)),
        out_shape=jax.ShapeDtypeStruct((tokens, kv_width), jnp.bfloat16),
    )(queries, keys, grads, segments, segments.reshape(tokens, 1))


def project_kernel(chips, steps, own_ref, other_ref, *rest):
    row_refs, out_refs, gathered = rest[:chips], rest[-chips - 1:-1], rest[-1]
    taken, depth = row_refs[0].shape
    step = pl.program_id(0)

    @pl.when(step == 0)
    def _():
        for by in range(chips):
            gathered[by] = row_refs[by][...]

    def multiply(weight_ref):
        product = lax.dot_general(
            gathered[...].reshape(chips * taken, depth), weight_ref[...], (((1,), (1,)), ((), ())),
            preferred_element_type=jnp.float32,
        ).astype(jnp.bfloat16)
        for by in range(chips):
            out_refs[by][...] = product[by * taken:(by + 1) * taken]

    @pl.when(step < steps)
    def _():
        multiply(own_ref)

    @pl.when(step >= steps)
    def _():
        multiply(other_ref)


def project(rows, own, other, after):
    chips = len(rows)
    taken, depth = rows[0].shape
    width = own.shape[0]
    block = min(width, 256)
    steps = width // block
    return call(
        functools.partial(project_kernel, chips, steps), "project",
        4 * chips * taken * depth * width, 2 * (chips * taken * (depth + 2 * width) + 2 * width * depth),
        grid=(CORES * steps,),
        in_specs=[
            pl.BlockSpec((block, depth), lambda i: (jnp.minimum(i, steps - 1), 0)),
            pl.BlockSpec((block, depth), lambda i: (jnp.maximum(i - steps, 0), 0)),
        ] + [pl.BlockSpec((taken, depth), lambda i: (0, 0))] * chips + [whole] * len(after),
        out_specs=[pl.BlockSpec((taken, block), lambda i: (0, i))] * chips,
        out_shape=[jax.ShapeDtypeStruct((taken, CORES * width), jnp.bfloat16)] * chips,
        scratch_shapes=[pltpu.VMEM((chips, taken, depth), jnp.bfloat16)],
    )(own, other, *rows, *after)


def backward_kernel(chips, place_ref, x_ref, gain_ref, grad_ref, *rest):
    cot_refs, out_ref = rest[:chips], rest[-1]
    chip, core = place_ref[0], place_ref[1]
    values = x_ref[...].astype(jnp.float32)
    width = cot_refs[0].shape[1] // CORES
    inverse = lax.rsqrt(jnp.mean(values * values, axis=-1, keepdims=True) + norm_eps)
    inner = jnp.zeros_like(inverse)

    def parts():
        for by, cot_ref in enumerate(cot_refs):
            source = lax.rem(chip + chips - by, chips)
            for half in range(CORES):
                cols = part_columns(source, half, core, width)
                cot = cot_ref[:, half * width:(half + 1) * width].astype(jnp.float32)
                yield cols, gain_ref[:, cols].astype(jnp.float32) * cot

    for cols, scaled in parts():
        inner += jnp.sum(x_ref[:, cols].astype(jnp.float32) * scaled, axis=-1, keepdims=True)
    factor = inverse * inverse * inverse * (inner / x_ref.shape[1])
    for cols, scaled in parts():
        out_ref[:, cols] = (
            grad_ref[:, cols].astype(jnp.float32)
            + inverse * scaled
            - x_ref[:, cols].astype(jnp.float32) * factor
        ).astype(out_ref.dtype)


def norm_backward(place, cots, rows, gain, grads, after):
    tokens, width = rows.shape
    taken, part_width = cots[0].shape
    block = min(taken, 32)
    return call(
        functools.partial(backward_kernel, len(cots)), "norm_backward",
        10 * taken * width, 8 * taken * width,
        grid=(taken // block,),
        in_specs=[
            scalars,
            pl.BlockSpec((block, width), lambda i: (i, 0)),
            pl.BlockSpec((1, width), lambda i: (0, 0)),
            pl.BlockSpec((block, width), lambda i: (i, 0)),
        ] + [pl.BlockSpec((block, part_width), lambda i: (i, 0))] * len(cots) + [whole] * len(after),
        out_specs=pl.BlockSpec((block, width), lambda i: (i, 0)),
        out_shape=jax.ShapeDtypeStruct((taken, width), jnp.bfloat16),
    )(place, rows, gain, grads, *cots, *after)


def outer_kernel(groups, sums, *refs):
    arrays = sum(groups)
    cots, columns, terms = refs[:arrays], refs[arrays:2 * arrays], refs[2 * arrays:2 * arrays + sums]
    total, at = None, 0
    for size in groups:
        column, cot = columns[at][...], cots[at][...]
        for more in range(at + 1, at + size):
            column, cot = column + columns[more][...], cot + cots[more][...]
        at += size
        product = lax.dot_general(
            column, cot, (((0,), (0,)), ((), ())), preferred_element_type=jnp.float32
        )
        total = product if total is None else total + product
    for term in terms:
        total += term[...].astype(jnp.float32)
    refs[-1][...] = total.astype(refs[-1].dtype)


def outer(groups, cot_width, half, before, dtype):
    payloads = [payload for group in groups for payload in group]
    wide = payloads[0].shape[1]
    width = (wide - cot_width) // CORES
    block = math.gcd(math.gcd(width, 256), cot_width)
    first = (cot_width + half * width) // block
    out_spec = pl.BlockSpec((block, cot_width), lambda i: (i, 0))
    tokens = sum(payload.shape[0] for payload in payloads)
    return call(
        functools.partial(outer_kernel, [len(group) for group in groups], len(before)), "outer",
        2 * tokens * width * cot_width, 2 * tokens * width + 4 * width * cot_width,
        grid=(width // block,),
        in_specs=[pl.BlockSpec((payload.shape[0], cot_width), lambda i: (0, 0)) for payload in payloads]
        + [pl.BlockSpec((payload.shape[0], block), lambda i: (0, first + i)) for payload in payloads]
        + [out_spec] * len(before),
        out_specs=out_spec,
        out_shape=jax.ShapeDtypeStruct((width, cot_width), dtype),
    )(*payloads, *payloads, *before)


def shards(
    new_input,
    new_gain,
    queries,
    new_keys,
    context_grad,
    segment_ids,
    frozen_input,
    frozen_gain,
    output_grad,
    kv_grad,
    kv_weight,
):
    chips = lax.axis_size("dp") // CORES
    sections = lax.axis_size("pipe")
    tokens, kv_width = new_keys.shape[1:]
    at = lax.axis_index("dp")
    place = jnp.stack([at // CORES, at % CORES]).astype(jnp.int32)
    middle = chips // 2
    near = [by for by in range(1, chips) if by != middle]
    spread = tokens * 3 // 8

    rows = [kv_grad[0]] + [along_chips(kv_grad[0], chips - by, 1) for by in range(1, chips)]
    other_weight = swap_cores(kv_weight[0])
    value_cot = attend(queries[0], new_keys[0], context_grad[0], segment_ids)

    apply = functools.partial(normalize, place, new_input[0], new_gain, value_cot, chips)
    shared = apply([middle], 0, spread, [other_weight])[0]
    brought = [between_lines(shared, section, 0) for section in range(1, sections)]
    joint = stack_rows([shared] + brought, rows[1:])
    moved = on_line(joint, middle, 0)
    returned = [moved[:spread]] + [
        between_lines(moved[section * spread:(section + 1) * spread], 0, section) for section in range(1, sections)
    ]

    parts = project(rows, kv_weight[0], other_weight, [joint])
    arrived = [parts[0]] + [along_chips(parts[by], by, 1) for by in range(1, chips)]
    kept = apply([middle], spread, tokens - spread, [parts[0]])
    blocks = apply([0] + near, 0, tokens, kept)

    input_cot = norm_backward(
        place, arrived, frozen_input[0], frozen_gain, output_grad[0], [blocks[0]] + returned[1:]
    )
    cot_below = from_behind(input_cot, "pipe", -1)

    columns = [blocks[0]] + [along_chips(block, by) for block, by in zip(blocks[1:], near)]
    last = along_chips(kept[0], middle)

    groups = [[column] for column in columns] + [returned]
    sums = [outer(groups, kv_width, half, [], jnp.float32) for half in range(CORES)]
    given = outer([[last]], kv_width, 1, [sums[1]], jnp.bfloat16)
    taken = swap_cores(given)
    grad = outer([[last]], kv_width, 0, [sums[0], taken], jnp.float32)
    return (cot_below[None], grad[None])


def solution(mesh):
    placed = (
        P("pipe", "dp", None),
        P("pipe", None),
        P("pipe", "dp", None),
        P("pipe", "dp", None),
        P("pipe", "dp", None),
        P("pipe", "dp"),
        P("pipe", "dp", None),
        P("pipe", None),
        P("pipe", "dp", None),
        P("pipe", "dp", None),
        P("pipe", "dp", None),
    )
    return jax.shard_map(
        shards,
        mesh=mesh,
        in_specs=placed,
        out_specs=(P("pipe", "dp", None), P("pipe", "dp", None)),
        check_vma=False,
    )
```

```python
import functools
import math

import jax
import jax.numpy as jnp
from jax import lax
from jax.experimental import pallas as pl
from jax.experimental.pallas import tpu as pltpu
from jax.sharding import PartitionSpec as P

HEAD = 128
CORES = 2
MIB = 1 << 20

norm_eps = 1e-05
masked_value = -1e30

whole = pl.BlockSpec(memory_space=pl.ANY)
scalars = pl.BlockSpec(memory_space=pltpu.SMEM)


def from_behind(array, axis, by):
    length = lax.axis_size(axis)
    pairs = [(i, i + by) for i in range(length) if 0 <= i + by < length]
    return lax.ppermute(array, axis, pairs)


def along_chips(array, by, first=0):
    length = lax.axis_size("dp")
    pairs = [
        (line * length + i, line * length + (i + by * CORES) % length)
        for line in range(first, lax.axis_size("pipe")) for i in range(length)
    ]
    return lax.ppermute(array, ("pipe", "dp"), pairs)


def between_lines(array, source, target):
    length = lax.axis_size("dp")
    pairs = [(source * length + i, target * length + i) for i in range(length)]
    return lax.ppermute(array, ("pipe", "dp"), pairs)


def on_line(array, by, line):
    length = lax.axis_size("dp")
    pairs = [(line * length + i, line * length + (i + by * CORES) % length) for i in range(length)]
    return lax.ppermute(array, ("pipe", "dp"), pairs)


def swap_cores(array):
    length = lax.axis_size("dp")
    return lax.ppermute(array, "dp", [(i, i ^ 1) for i in range(length)])


def call(body, name, flops, nbytes, vmem=24, **kwargs):
    return pl.pallas_call(
        body,
        name=name,
        compiler_params=pltpu.CompilerParams(vmem_limit_bytes=vmem * MIB),
        cost_estimate=pl.CostEstimate(flops=flops, bytes_accessed=nbytes, transcendentals=0),
        **kwargs,
    )


def part_columns(chip, half, core, width):
    owner = chip * CORES + (core if half == 0 else CORES - 1 - core)
    return pl.ds(pl.multiple_of(owner * width, width), width)


def norm_kernel(chips, ahead, place_ref, x_ref, gain_ref, cot_ref, *rest):
    out_refs = rest[-len(ahead):]
    chip, core = place_ref[0], place_ref[1]
    values = x_ref[...].astype(jnp.float32)
    inverse = lax.rsqrt(jnp.mean(values * values, axis=-1, keepdims=True) + norm_eps)
    front = cot_ref.shape[1]
    width = (out_refs[0].shape[1] - front) // CORES
    for by, out_ref in zip(ahead, out_refs):
        to = lax.rem(chip + by, chips)
        out_ref[:, :front] = cot_ref[...]
        for half in range(CORES):
            cols = part_columns(to, half, core, width)
            out_ref[:, front + half * width:front + (half + 1) * width] = (
                x_ref[:, cols].astype(jnp.float32) * inverse * gain_ref[:, cols].astype(jnp.float32)
            ).astype(out_ref.dtype)


def normalize(place, rows, gain, cot, chips, ahead, start, count, after):
    width = rows.shape[1]
    front = cot.shape[1]
    block = math.gcd(math.gcd(start, count), 32)
    first = start // block
    out_width = front + width // chips
    return list(call(
        functools.partial(norm_kernel, chips, ahead), "norm_forward",
        4 * count * width, 2 * count * width + 2 * count * out_width * len(ahead),
        grid=(count // block,),
        in_specs=[
            scalars,
            pl.BlockSpec((block, width), lambda i: (first + i, 0)),
            pl.BlockSpec((1, width), lambda i: (0, 0)),
            pl.BlockSpec((block, front), lambda i: (first + i, 0)),
        ] + [whole] * len(after),
        out_specs=[pl.BlockSpec((block, out_width), lambda i: (i, 0))] * len(ahead),
        out_shape=[jax.ShapeDtypeStruct((count, out_width), jnp.bfloat16)] * len(ahead),
    )(place, rows, gain, cot, *after))


def stack_kernel(count, *refs):
    at = 0
    for ref in refs[:count]:
        refs[-1][at:at + ref.shape[0]] = ref[...]
        at += ref.shape[0]


def stack_rows(arrays, after):
    width = arrays[0].shape[1]
    tall = sum(array.shape[0] for array in arrays)
    return call(
        functools.partial(stack_kernel, len(arrays)), "stack_rows", 0, 4 * tall * width,
        grid=(1,),
        in_specs=[pl.BlockSpec(array.shape, lambda i: (0, 0)) for array in arrays] + [whole] * len(after),
        out_specs=pl.BlockSpec((tall, width), lambda i: (0, 0)),
        out_shape=jax.ShapeDtypeStruct((tall, width), arrays[0].dtype),
    )(*arrays, *after)


def attend_kernel(query_ref, key_ref, grad_ref, row_seg_ref, col_seg_ref, out_ref):
    tokens = key_ref.shape[0]
    group = query_ref.shape[1] // HEAD
    at_query = lax.broadcasted_iota(jnp.int32, (tokens, tokens), 0)
    at_key = lax.broadcasted_iota(jnp.int32, (tokens, tokens), 1)
    visible = (col_seg_ref[...] == row_seg_ref[...]) & (at_key <= at_query)
    keys = key_ref[...]
    total = jnp.zeros((tokens, HEAD), jnp.float32)
    for head in range(group):
        cols = slice(head * HEAD, (head + 1) * HEAD)
        scores = lax.dot_general(
            query_ref[:, cols], keys, (((1,), (1,)), ((), ())),
            preferred_element_type=jnp.float32,
        ) / math.sqrt(HEAD)
        masked = jnp.where(visible, scores, masked_value)
        highest = jnp.max(masked, axis=-1, keepdims=True)
        weights = jnp.where(visible, jnp.exp(masked - highest), 0.0)
        attention = (weights / jnp.sum(weights, axis=-1, keepdims=True)).astype(jnp.bfloat16)
        total += lax.dot_general(
            attention, grad_ref[:, cols], (((0,), (0,)), ((), ())),
            preferred_element_type=jnp.float32,
        )
    out_ref[...] = total.astype(out_ref.dtype)


def attend(queries, keys, grads, segments):
    tokens, kv_width = keys.shape
    heads = kv_width // HEAD
    wide = queries.shape[1] // heads
    return call(
        attend_kernel, "attend",
        4 * tokens * tokens * queries.shape[1], 4 * tokens * queries.shape[1],
        grid=(heads,),
        in_specs=[
            pl.BlockSpec((tokens, wide), lambda i: (0, i)),
            pl.BlockSpec((tokens, HEAD), lambda i: (0, i)),
            pl.BlockSpec((tokens, wide), lambda i: (0, i)),
            pl.BlockSpec((1, tokens), lambda i: (0, 0)),
            pl.BlockSpec((tokens, 1), lambda i: (0, 0)),
        ],
        out_specs=pl.BlockSpec((tokens, HEAD), lambda i: (0, i)),
        out_shape=jax.ShapeDtypeStruct((tokens, kv_width), jnp.bfloat16),
    )(queries, keys, grads, segments, segments.reshape(tokens, 1))


def project_kernel(chips, steps, own_ref, other_ref, *rest):
    row_refs, out_refs, gathered = rest[:chips], rest[-chips - 1:-1], rest[-1]
    taken, depth = row_refs[0].shape
    step = pl.program_id(0)

    @pl.when(step == 0)
    def _():
        for by in range(chips):
            gathered[by] = row_refs[by][...]

    def multiply(weight_ref):
        product = lax.dot_general(
            gathered[...].reshape(chips * taken, depth), weight_ref[...], (((1,), (1,)), ((), ())),
            preferred_element_type=jnp.float32,
        ).astype(jnp.bfloat16)
        for by in range(chips):
            out_refs[by][...] = product[by * taken:(by + 1) * taken]

    @pl.when(step < steps)
    def _():
        multiply(own_ref)

    @pl.when(step >= steps)
    def _():
        multiply(other_ref)


def project(rows, own, other, after):
    chips = len(rows)
    taken, depth = rows[0].shape
    width = own.shape[0]
    block = min(width, 256)
    steps = width // block
    return call(
        functools.partial(project_kernel, chips, steps), "project",
        4 * chips * taken * depth * width, 2 * (chips * taken * (depth + 2 * width) + 2 * width * depth),
        grid=(CORES * steps,),
        in_specs=[
            pl.BlockSpec((block, depth), lambda i: (jnp.minimum(i, steps - 1), 0)),
            pl.BlockSpec((block, depth), lambda i: (jnp.maximum(i - steps, 0), 0)),
        ] + [pl.BlockSpec((taken, depth), lambda i: (0, 0))] * chips + [whole] * len(after),
        out_specs=[pl.BlockSpec((taken, block), lambda i: (0, i))] * chips,
        out_shape=[jax.ShapeDtypeStruct((taken, CORES * width), jnp.bfloat16)] * chips,
        scratch_shapes=[pltpu.VMEM((chips, taken, depth), jnp.bfloat16)],
    )(own, other, *rows, *after)


def backward_kernel(chips, place_ref, x_ref, gain_ref, grad_ref, *rest):
    cot_refs, out_ref = rest[:chips], rest[-1]
    chip, core = place_ref[0], place_ref[1]
    values = x_ref[...].astype(jnp.float32)
    width = cot_refs[0].shape[1] // CORES
    inverse = lax.rsqrt(jnp.mean(values * values, axis=-1, keepdims=True) + norm_eps)
    inner = jnp.zeros_like(inverse)

    def parts():
        for by, cot_ref in enumerate(cot_refs):
            source = lax.rem(chip + chips - by, chips)
            for half in range(CORES):
                cols = part_columns(source, half, core, width)
                cot = cot_ref[:, half * width:(half + 1) * width].astype(jnp.float32)
                yield cols, gain_ref[:, cols].astype(jnp.float32) * cot

    for cols, scaled in parts():
        inner += jnp.sum(x_ref[:, cols].astype(jnp.float32) * scaled, axis=-1, keepdims=True)
    factor = inverse * inverse * inverse * (inner / x_ref.shape[1])
    for cols, scaled in parts():
        out_ref[:, cols] = (
            grad_ref[:, cols].astype(jnp.float32)
            + inverse * scaled
            - x_ref[:, cols].astype(jnp.float32) * factor
        ).astype(out_ref.dtype)


def norm_backward(place, cots, rows, gain, grads, after):
    tokens, width = rows.shape
    taken, part_width = cots[0].shape
    block = min(taken, 32)
    return call(
        functools.partial(backward_kernel, len(cots)), "norm_backward",
        10 * taken * width, 8 * taken * width,
        grid=(taken // block,),
        in_specs=[
            scalars,
            pl.BlockSpec((block, width), lambda i: (i, 0)),
            pl.BlockSpec((1, width), lambda i: (0, 0)),
            pl.BlockSpec((block, width), lambda i: (i, 0)),
        ] + [pl.BlockSpec((block, part_width), lambda i: (i, 0))] * len(cots) + [whole] * len(after),
        out_specs=pl.BlockSpec((block, width), lambda i: (i, 0)),
        out_shape=jax.ShapeDtypeStruct((taken, width), jnp.bfloat16),
    )(place, rows, gain, grads, *cots, *after)


def outer_kernel(groups, sums, *refs):
    arrays = sum(groups)
    cots, columns, terms = refs[:arrays], refs[arrays:2 * arrays], refs[2 * arrays:2 * arrays + sums]
    total, at = None, 0
    for size in groups:
        column, cot = columns[at][...], cots[at][...]
        for more in range(at + 1, at + size):
            column, cot = column + columns[more][...], cot + cots[more][...]
        at += size
        product = lax.dot_general(
            column, cot, (((0,), (0,)), ((), ())), preferred_element_type=jnp.float32
        )
        total = product if total is None else total + product
    for term in terms:
        total += term[...].astype(jnp.float32)
    refs[-1][...] = total.astype(refs[-1].dtype)


def outer(groups, cot_width, half, before, dtype):
    payloads = [payload for group in groups for payload in group]
    wide = payloads[0].shape[1]
    width = (wide - cot_width) // CORES
    block = math.gcd(math.gcd(width, 256), cot_width)
    first = (cot_width + half * width) // block
    out_spec = pl.BlockSpec((block, cot_width), lambda i: (i, 0))
    tokens = sum(payload.shape[0] for payload in payloads)
    return call(
        functools.partial(outer_kernel, [len(group) for group in groups], len(before)), "outer",
        2 * tokens * width * cot_width, 2 * tokens * width + 4 * width * cot_width,
        grid=(width // block,),
        in_specs=[pl.BlockSpec((payload.shape[0], cot_width), lambda i: (0, 0)) for payload in payloads]
        + [pl.BlockSpec((payload.shape[0], block), lambda i: (0, first + i)) for payload in payloads]
        + [out_spec] * len(before),
        out_specs=out_spec,
        out_shape=jax.ShapeDtypeStruct((width, cot_width), dtype),
    )(*payloads, *payloads, *before)


def shards(
    new_input,
    new_gain,
    queries,
    new_keys,
    context_grad,
    segment_ids,
    frozen_input,
    frozen_gain,
    output_grad,
    kv_grad,
    kv_weight,
):
    chips = lax.axis_size("dp") // CORES
    sections = lax.axis_size("pipe")
    tokens, kv_width = new_keys.shape[1:]
    at = lax.axis_index("dp")
    place = jnp.stack([at // CORES, at % CORES]).astype(jnp.int32)
    middle = chips // 2
    near = [by for by in range(1, chips) if by != middle]
    spread = tokens // 4

    rows = [kv_grad[0]] + [along_chips(kv_grad[0], chips - by, 1) for by in range(1, chips)]
    other_weight = swap_cores(kv_weight[0])
    value_cot = attend(queries[0], new_keys[0], context_grad[0], segment_ids)

    apply = functools.partial(normalize, place, new_input[0], new_gain, value_cot, chips)
    shared = apply([middle], 0, spread, [other_weight])[0]
    brought = [between_lines(shared, section, 0) for section in range(1, sections)]
    early = apply([0] + near[:1], 0, tokens, rows[1:])
    columns = [early[0]] + [along_chips(block, by) for block, by in zip(early[1:], near)]
    joint = stack_rows([shared] + brought, early[:1])
    moved = on_line(joint, middle, 0)
    returned = [moved[:spread]] + [
        between_lines(moved[section * spread:(section + 1) * spread], 0, section) for section in range(1, sections)
    ]

    parts = project(rows, kv_weight[0], other_weight, [joint])
    arrived = [parts[0]] + [along_chips(parts[by], by, 1) for by in range(1, chips)]
    kept = apply([middle], spread, tokens - spread, [parts[0]])
    late = apply(near[1:], 0, tokens, kept)

    input_cot = norm_backward(
        place, arrived, frozen_input[0], frozen_gain, output_grad[0], late[:1] + returned[1:] + columns[1:]
    )
    cot_below = from_behind(input_cot, "pipe", -1)

    columns += [along_chips(block, by) for block, by in zip(late, near[1:])]
    last = along_chips(kept[0], middle)

    groups = [[column] for column in columns] + [returned]
    sums = [outer(groups, kv_width, half, [], jnp.float32) for half in range(CORES)]
    given = outer([[last]], kv_width, 1, [sums[1]], jnp.bfloat16)
    taken = swap_cores(given)
    grad = outer([[last]], kv_width, 0, [sums[0], taken], jnp.float32)
    return (cot_below[None], grad[None])


def solution(mesh):
    placed = (
        P("pipe", "dp", None),
        P("pipe", None),
        P("pipe", "dp", None),
        P("pipe", "dp", None),
        P("pipe", "dp", None),
        P("pipe", "dp"),
        P("pipe", "dp", None),
        P("pipe", None),
        P("pipe", "dp", None),
        P("pipe", "dp", None),
        P("pipe", "dp", None),
    )
    return jax.shard_map(
        shards,
        mesh=mesh,
        in_specs=placed,
        out_specs=(P("pipe", "dp", None), P("pipe", "dp", None)),
        check_vma=False,
    )
```

```python
import functools
import math

import jax
import jax.numpy as jnp
from jax import lax
from jax.experimental import pallas as pl
from jax.experimental.pallas import tpu as pltpu
from jax.sharding import PartitionSpec as P

HEAD = 128
CORES = 2
MIB = 1 << 20

norm_eps = 1e-05
masked_value = -1e30

whole = pl.BlockSpec(memory_space=pl.ANY)
scalars = pl.BlockSpec(memory_space=pltpu.SMEM)


def from_behind(array, axis, by):
    length = lax.axis_size(axis)
    pairs = [(i, i + by) for i in range(length) if 0 <= i + by < length]
    return lax.ppermute(array, axis, pairs)


def along_chips(array, by, first=0):
    length = lax.axis_size("dp")
    pairs = [
        (line * length + i, line * length + ((i + by * CORES) % length if line >= first else i ^ 1))
        for line in range(lax.axis_size("pipe")) for i in range(length)
    ]
    return lax.ppermute(array, ("pipe", "dp"), pairs)


def between_lines(array, source, target):
    length = lax.axis_size("dp")
    pairs = [(source * length + i, target * length + i) for i in range(length)]
    return lax.ppermute(array, ("pipe", "dp"), pairs)


def on_line(array, by, line):
    length = lax.axis_size("dp")
    pairs = [(line * length + i, line * length + (i + by * CORES) % length) for i in range(length)]
    return lax.ppermute(array, ("pipe", "dp"), pairs)


def swap_cores(array):
    length = lax.axis_size("dp")
    return lax.ppermute(array, "dp", [(i, i ^ 1) for i in range(length)])


def call(body, name, flops, nbytes, vmem=24, **kwargs):
    return pl.pallas_call(
        body,
        name=name,
        compiler_params=pltpu.CompilerParams(vmem_limit_bytes=vmem * MIB),
        cost_estimate=pl.CostEstimate(flops=flops, bytes_accessed=nbytes, transcendentals=0),
        **kwargs,
    )


def part_columns(chip, half, core, width):
    owner = chip * CORES + (core if half == 0 else CORES - 1 - core)
    return pl.ds(pl.multiple_of(owner * width, width), width)


def norm_kernel(chips, ahead, place_ref, x_ref, gain_ref, cot_ref, *rest):
    out_refs = rest[-len(ahead):]
    chip, core = place_ref[0], place_ref[1]
    values = x_ref[...].astype(jnp.float32)
    inverse = lax.rsqrt(jnp.mean(values * values, axis=-1, keepdims=True) + norm_eps)
    front = cot_ref.shape[1]
    width = (out_refs[0].shape[1] - front) // CORES
    for by, out_ref in zip(ahead, out_refs):
        to = lax.rem(chip + by, chips)
        out_ref[:, :front] = cot_ref[...]
        for half in range(CORES):
            cols = part_columns(to, half, core, width)
            out_ref[:, front + half * width:front + (half + 1) * width] = (
                x_ref[:, cols].astype(jnp.float32) * inverse * gain_ref[:, cols].astype(jnp.float32)
            ).astype(out_ref.dtype)


def normalize(place, rows, gain, cot, chips, ahead, start, count, after):
    width = rows.shape[1]
    front = cot.shape[1]
    block = math.gcd(math.gcd(start, count), 32)
    first = start // block
    out_width = front + width // chips
    return list(call(
        functools.partial(norm_kernel, chips, ahead), "norm_forward",
        4 * count * width, 2 * count * width + 2 * count * out_width * len(ahead),
        grid=(count // block,),
        in_specs=[
            scalars,
            pl.BlockSpec((block, width), lambda i: (first + i, 0)),
            pl.BlockSpec((1, width), lambda i: (0, 0)),
            pl.BlockSpec((block, front), lambda i: (first + i, 0)),
        ] + [whole] * len(after),
        out_specs=[pl.BlockSpec((block, out_width), lambda i: (i, 0))] * len(ahead),
        out_shape=[jax.ShapeDtypeStruct((count, out_width), jnp.bfloat16)] * len(ahead),
    )(place, rows, gain, cot, *after))


def stack_kernel(count, *refs):
    at = 0
    for ref in refs[:count]:
        refs[-1][at:at + ref.shape[0]] = ref[...]
        at += ref.shape[0]


def stack_rows(arrays, after):
    width = arrays[0].shape[1]
    tall = sum(array.shape[0] for array in arrays)
    return call(
        functools.partial(stack_kernel, len(arrays)), "stack_rows", 0, 4 * tall * width,
        grid=(1,),
        in_specs=[pl.BlockSpec(array.shape, lambda i: (0, 0)) for array in arrays] + [whole] * len(after),
        out_specs=pl.BlockSpec((tall, width), lambda i: (0, 0)),
        out_shape=jax.ShapeDtypeStruct((tall, width), arrays[0].dtype),
    )(*arrays, *after)


def attend_kernel(query_ref, key_ref, grad_ref, row_seg_ref, col_seg_ref, out_ref):
    tokens = key_ref.shape[0]
    group = query_ref.shape[1] // HEAD
    at_query = lax.broadcasted_iota(jnp.int32, (tokens, tokens), 0)
    at_key = lax.broadcasted_iota(jnp.int32, (tokens, tokens), 1)
    visible = (col_seg_ref[...] == row_seg_ref[...]) & (at_key <= at_query)
    keys = key_ref[...]
    total = jnp.zeros((tokens, HEAD), jnp.float32)
    for head in range(group):
        cols = slice(head * HEAD, (head + 1) * HEAD)
        scores = lax.dot_general(
            query_ref[:, cols], keys, (((1,), (1,)), ((), ())),
            preferred_element_type=jnp.float32,
        ) / math.sqrt(HEAD)
        masked = jnp.where(visible, scores, masked_value)
        highest = jnp.max(masked, axis=-1, keepdims=True)
        weights = jnp.where(visible, jnp.exp(masked - highest), 0.0)
        attention = (weights / jnp.sum(weights, axis=-1, keepdims=True)).astype(jnp.bfloat16)
        total += lax.dot_general(
            attention, grad_ref[:, cols], (((0,), (0,)), ((), ())),
            preferred_element_type=jnp.float32,
        )
    out_ref[...] = total.astype(out_ref.dtype)


def attend(queries, keys, grads, segments):
    tokens, kv_width = keys.shape
    heads = kv_width // HEAD
    wide = queries.shape[1] // heads
    return call(
        attend_kernel, "attend",
        4 * tokens * tokens * queries.shape[1], 4 * tokens * queries.shape[1],
        grid=(heads,),
        in_specs=[
            pl.BlockSpec((tokens, wide), lambda i: (0, i)),
            pl.BlockSpec((tokens, HEAD), lambda i: (0, i)),
            pl.BlockSpec((tokens, wide), lambda i: (0, i)),
            pl.BlockSpec((1, tokens), lambda i: (0, 0)),
            pl.BlockSpec((tokens, 1), lambda i: (0, 0)),
        ],
        out_specs=pl.BlockSpec((tokens, HEAD), lambda i: (0, i)),
        out_shape=jax.ShapeDtypeStruct((tokens, kv_width), jnp.bfloat16),
    )(queries, keys, grads, segments, segments.reshape(tokens, 1))


def project_kernel(chips, steps, own_ref, other_ref, *rest):
    row_refs, out_refs, gathered = rest[:chips], rest[-chips - 1:-1], rest[-1]
    taken, depth = row_refs[0].shape
    step = pl.program_id(0)

    @pl.when(step == 0)
    def _():
        for by in range(chips):
            gathered[by] = row_refs[by][...]

    def multiply(weight_ref):
        product = lax.dot_general(
            gathered[...].reshape(chips * taken, depth), weight_ref[...], (((1,), (1,)), ((), ())),
            preferred_element_type=jnp.float32,
        ).astype(jnp.bfloat16)
        for by in range(chips):
            out_refs[by][...] = product[by * taken:(by + 1) * taken]

    @pl.when(step < steps)
    def _():
        multiply(own_ref)

    @pl.when(step >= steps)
    def _():
        multiply(other_ref)


def project(rows, own, other, after):
    chips = len(rows)
    taken, depth = rows[0].shape
    width = own.shape[0]
    block = min(width, 512)
    steps = width // block
    return call(
        functools.partial(project_kernel, chips, steps), "project",
        4 * chips * taken * depth * width, 2 * (chips * taken * (depth + 2 * width) + 2 * width * depth),
        grid=(CORES * steps,),
        in_specs=[
            pl.BlockSpec((block, depth), lambda i: (jnp.minimum(i, steps - 1), 0)),
            pl.BlockSpec((block, depth), lambda i: (jnp.maximum(i - steps, 0), 0)),
        ] + [pl.BlockSpec((taken, depth), lambda i: (0, 0))] * chips + [whole] * len(after),
        out_specs=[pl.BlockSpec((taken, block), lambda i: (0, i))] * chips,
        out_shape=[jax.ShapeDtypeStruct((taken, CORES * width), jnp.bfloat16)] * chips,
        scratch_shapes=[pltpu.VMEM((chips, taken, depth), jnp.bfloat16)],
    )(own, other, *rows, *after)


def backward_kernel(chips, place_ref, x_ref, gain_ref, grad_ref, *rest):
    cot_refs, out_ref = rest[:chips], rest[-1]
    chip, core = place_ref[0], place_ref[1]
    values = x_ref[...].astype(jnp.float32)
    width = cot_refs[0].shape[1] // CORES
    inverse = lax.rsqrt(jnp.mean(values * values, axis=-1, keepdims=True) + norm_eps)
    inner = jnp.zeros_like(inverse)

    def parts():
        for by, cot_ref in enumerate(cot_refs):
            source = lax.rem(chip + chips - by, chips)
            for half in range(CORES):
                cols = part_columns(source, half, core, width)
                cot = cot_ref[:, half * width:(half + 1) * width].astype(jnp.float32)
                yield cols, gain_ref[:, cols].astype(jnp.float32) * cot

    for cols, scaled in parts():
        inner += jnp.sum(x_ref[:, cols].astype(jnp.float32) * scaled, axis=-1, keepdims=True)
    factor = inverse * inverse * inverse * (inner / x_ref.shape[1])
    for cols, scaled in parts():
        out_ref[:, cols] = (
            grad_ref[:, cols].astype(jnp.float32)
            + inverse * scaled
            - x_ref[:, cols].astype(jnp.float32) * factor
        ).astype(out_ref.dtype)


def norm_backward(place, cots, rows, gain, grads, after):
    tokens, width = rows.shape
    taken, part_width = cots[0].shape
    block = min(taken, 32)
    return call(
        functools.partial(backward_kernel, len(cots)), "norm_backward",
        10 * taken * width, 8 * taken * width,
        grid=(taken // block,),
        in_specs=[
            scalars,
            pl.BlockSpec((block, width), lambda i: (i, 0)),
            pl.BlockSpec((1, width), lambda i: (0, 0)),
            pl.BlockSpec((block, width), lambda i: (i, 0)),
        ] + [pl.BlockSpec((block, part_width), lambda i: (i, 0))] * len(cots) + [whole] * len(after),
        out_specs=pl.BlockSpec((block, width), lambda i: (i, 0)),
        out_shape=jax.ShapeDtypeStruct((taken, width), jnp.bfloat16),
    )(place, rows, gain, grads, *cots, *after)


def outer_kernel(groups, sums, *refs):
    arrays = sum(groups)
    cots, columns, terms = refs[:arrays], refs[arrays:2 * arrays], refs[2 * arrays:2 * arrays + sums]
    total, at = None, 0
    for size in groups:
        column, cot = columns[at][...], cots[at][...]
        for more in range(at + 1, at + size):
            column, cot = column + columns[more][...], cot + cots[more][...]
        at += size
        product = lax.dot_general(
            column, cot, (((0,), (0,)), ((), ())), preferred_element_type=jnp.float32
        )
        total = product if total is None else total + product
    for term in terms:
        total += term[...].astype(jnp.float32)
    refs[-1][...] = total.astype(refs[-1].dtype)


def outer(groups, cot_width, half, before, dtype):
    payloads = [payload for group in groups for payload in group]
    wide = payloads[0].shape[1]
    width = (wide - cot_width) // CORES
    block = math.gcd(math.gcd(width, 256), cot_width)
    first = (cot_width + half * width) // block
    out_spec = pl.BlockSpec((block, cot_width), lambda i: (i, 0))
    tokens = sum(payload.shape[0] for payload in payloads)
    return call(
        functools.partial(outer_kernel, [len(group) for group in groups], len(before)), "outer",
        2 * tokens * width * cot_width, 2 * tokens * width + 4 * width * cot_width,
        grid=(width // block,),
        in_specs=[pl.BlockSpec((payload.shape[0], cot_width), lambda i: (0, 0)) for payload in payloads]
        + [pl.BlockSpec((payload.shape[0], block), lambda i: (0, first + i)) for payload in payloads]
        + [out_spec] * len(before),
        out_specs=out_spec,
        out_shape=jax.ShapeDtypeStruct((width, cot_width), dtype),
    )(*payloads, *payloads, *before)


def shards(
    new_input,
    new_gain,
    queries,
    new_keys,
    context_grad,
    segment_ids,
    frozen_input,
    frozen_gain,
    output_grad,
    kv_grad,
    kv_weight,
):
    chips = lax.axis_size("dp") // CORES
    sections = lax.axis_size("pipe")
    tokens, kv_width = new_keys.shape[1:]
    at = lax.axis_index("dp")
    place = jnp.stack([at // CORES, at % CORES]).astype(jnp.int32)
    middle = chips // 2
    near = [by for by in range(1, chips) if by != middle]
    spread = tokens // 4

    rows = [kv_grad[0]] + [along_chips(kv_grad[0], chips - by, 1) for by in range(1, chips)]
    other_weight = swap_cores(kv_weight[0])
    value_cot = attend(queries[0], new_keys[0], context_grad[0], segment_ids)

    apply = functools.partial(normalize, place, new_input[0], new_gain, value_cot, chips)
    shared = apply([middle], 0, spread, [other_weight])[0]
    brought = [between_lines(shared, section, 0) for section in range(1, sections)]
    early = apply([0] + near[:1], 0, tokens, rows[1:])
    columns = [early[0]] + [along_chips(block, by) for block, by in zip(early[1:], near)]
    joint = stack_rows([shared] + brought, early[:1])
    moved = on_line(joint, middle, 0)
    returned = [moved[:spread]] + [
        between_lines(moved[section * spread:(section + 1) * spread], 0, section) for section in range(1, sections)
    ]

    parts = project(rows, kv_weight[0], other_weight, [joint])
    arrived = [parts[0]] + [along_chips(parts[by], by, 1) for by in range(1, chips)]
    kept = apply([middle], spread, tokens - spread, [parts[0]])
    late = apply(near[1:], 0, tokens, kept)

    input_cot = norm_backward(
        place, arrived, frozen_input[0], frozen_gain, output_grad[0], late[:1] + returned[1:] + columns[1:]
    )
    cot_below = from_behind(input_cot, "pipe", -1)

    columns += [along_chips(block, by) for block, by in zip(late, near[1:])]
    last = along_chips(kept[0], middle)

    groups = [[column] for column in columns] + [returned]
    sums = [outer(groups, kv_width, half, [], jnp.float32) for half in range(CORES)]
    given = outer([[last]], kv_width, 1, [sums[1]], jnp.bfloat16)
    taken = swap_cores(given)
    grad = outer([[last]], kv_width, 0, [sums[0], taken], jnp.float32)
    return (cot_below[None], grad[None])


def solution(mesh):
    placed = (
        P("pipe", "dp", None),
        P("pipe", None),
        P("pipe", "dp", None),
        P("pipe", "dp", None),
        P("pipe", "dp", None),
        P("pipe", "dp"),
        P("pipe", "dp", None),
        P("pipe", None),
        P("pipe", "dp", None),
        P("pipe", "dp", None),
        P("pipe", "dp", None),
    )
    return jax.shard_map(
        shards,
        mesh=mesh,
        in_specs=placed,
        out_specs=(P("pipe", "dp", None), P("pipe", "dp", None)),
        check_vma=False,
    )
```

```python
import functools
import math

import jax
import jax.numpy as jnp
from jax import lax
from jax.experimental import pallas as pl
from jax.experimental.pallas import tpu as pltpu
from jax.sharding import PartitionSpec as P

HEAD = 128
CORES = 2
MIB = 1 << 20

norm_eps = 1e-05
masked_value = -1e30

whole = pl.BlockSpec(memory_space=pl.ANY)
scalars = pl.BlockSpec(memory_space=pltpu.SMEM)


def from_behind(array, axis, by):
    length = lax.axis_size(axis)
    pairs = [(i, i + by) for i in range(length) if 0 <= i + by < length]
    return lax.ppermute(array, axis, pairs)


def along_chips(array, by, first=0):
    length = lax.axis_size("dp")
    pairs = [
        (line * length + i, line * length + ((i + by * CORES) % length if line >= first else i ^ 1))
        for line in range(lax.axis_size("pipe")) for i in range(length)
    ]
    return lax.ppermute(array, ("pipe", "dp"), pairs)


def between_lines(array, source, target):
    length = lax.axis_size("dp")
    pairs = [(source * length + i, target * length + i) for i in range(length)]
    return lax.ppermute(array, ("pipe", "dp"), pairs)


def on_line(array, by, line):
    length = lax.axis_size("dp")
    pairs = [(line * length + i, line * length + (i + by * CORES) % length) for i in range(length)]
    return lax.ppermute(array, ("pipe", "dp"), pairs)


def swap_cores(array):
    length = lax.axis_size("dp")
    return lax.ppermute(array, "dp", [(i, i ^ 1) for i in range(length)])


def call(body, name, flops, nbytes, vmem=24, **kwargs):
    return pl.pallas_call(
        body,
        name=name,
        compiler_params=pltpu.CompilerParams(vmem_limit_bytes=vmem * MIB),
        cost_estimate=pl.CostEstimate(flops=flops, bytes_accessed=nbytes, transcendentals=0),
        **kwargs,
    )


def part_columns(chip, half, core, width):
    owner = chip * CORES + (core if half == 0 else CORES - 1 - core)
    return pl.ds(pl.multiple_of(owner * width, width), width)


def norm_kernel(chips, ahead, place_ref, x_ref, gain_ref, cot_ref, *rest):
    out_refs = rest[-len(ahead):]
    chip, core = place_ref[0], place_ref[1]
    values = x_ref[...].astype(jnp.float32)
    inverse = lax.rsqrt(jnp.mean(values * values, axis=-1, keepdims=True) + norm_eps)
    front = cot_ref.shape[1]
    width = (out_refs[0].shape[1] - front) // CORES
    for by, out_ref in zip(ahead, out_refs):
        to = lax.rem(chip + by, chips)
        out_ref[:, :front] = cot_ref[...]
        for half in range(CORES):
            cols = part_columns(to, half, core, width)
            out_ref[:, front + half * width:front + (half + 1) * width] = (
                x_ref[:, cols].astype(jnp.float32) * inverse * gain_ref[:, cols].astype(jnp.float32)
            ).astype(out_ref.dtype)


def normalize(place, rows, gain, cot, chips, ahead, start, count, after):
    width = rows.shape[1]
    front = cot.shape[1]
    block = math.gcd(math.gcd(start, count), 32)
    first = start // block
    out_width = front + width // chips
    return list(call(
        functools.partial(norm_kernel, chips, ahead), "norm_forward",
        4 * count * width, 2 * count * width + 2 * count * out_width * len(ahead),
        grid=(count // block,),
        in_specs=[
            scalars,
            pl.BlockSpec((block, width), lambda i: (first + i, 0)),
            pl.BlockSpec((1, width), lambda i: (0, 0)),
            pl.BlockSpec((block, front), lambda i: (first + i, 0)),
        ] + [whole] * len(after),
        out_specs=[pl.BlockSpec((block, out_width), lambda i: (i, 0))] * len(ahead),
        out_shape=[jax.ShapeDtypeStruct((count, out_width), jnp.bfloat16)] * len(ahead),
    )(place, rows, gain, cot, *after))


def stack_kernel(count, *refs):
    at = 0
    for ref in refs[:count]:
        refs[-1][at:at + ref.shape[0]] = ref[...]
        at += ref.shape[0]


def stack_rows(arrays, after):
    width = arrays[0].shape[1]
    tall = sum(array.shape[0] for array in arrays)
    return call(
        functools.partial(stack_kernel, len(arrays)), "stack_rows", 0, 4 * tall * width,
        grid=(1,),
        in_specs=[pl.BlockSpec(array.shape, lambda i: (0, 0)) for array in arrays] + [whole] * len(after),
        out_specs=pl.BlockSpec((tall, width), lambda i: (0, 0)),
        out_shape=jax.ShapeDtypeStruct((tall, width), arrays[0].dtype),
    )(*arrays, *after)


def attend_kernel(query_ref, key_ref, grad_ref, row_seg_ref, col_seg_ref, out_ref):
    tokens = key_ref.shape[0]
    group = query_ref.shape[1] // HEAD
    at_query = lax.broadcasted_iota(jnp.int32, (tokens, tokens), 0)
    at_key = lax.broadcasted_iota(jnp.int32, (tokens, tokens), 1)
    visible = (col_seg_ref[...] == row_seg_ref[...]) & (at_key <= at_query)
    keys = key_ref[...]
    total = jnp.zeros((tokens, HEAD), jnp.float32)
    for head in range(group):
        cols = slice(head * HEAD, (head + 1) * HEAD)
        scores = lax.dot_general(
            query_ref[:, cols], keys, (((1,), (1,)), ((), ())),
            preferred_element_type=jnp.float32,
        ) / math.sqrt(HEAD)
        masked = jnp.where(visible, scores, masked_value)
        highest = jnp.max(masked, axis=-1, keepdims=True)
        weights = jnp.where(visible, jnp.exp(masked - highest), 0.0)
        attention = (weights / jnp.sum(weights, axis=-1, keepdims=True)).astype(jnp.bfloat16)
        total += lax.dot_general(
            attention, grad_ref[:, cols], (((0,), (0,)), ((), ())),
            preferred_element_type=jnp.float32,
        )
    out_ref[...] = total.astype(out_ref.dtype)


def attend(queries, keys, grads, segments):
    tokens, kv_width = keys.shape
    heads = kv_width // HEAD
    wide = queries.shape[1] // heads
    return call(
        attend_kernel, "attend",
        4 * tokens * tokens * queries.shape[1], 4 * tokens * queries.shape[1],
        grid=(heads,),
        in_specs=[
            pl.BlockSpec((tokens, wide), lambda i: (0, i)),
            pl.BlockSpec((tokens, HEAD), lambda i: (0, i)),
            pl.BlockSpec((tokens, wide), lambda i: (0, i)),
            pl.BlockSpec((1, tokens), lambda i: (0, 0)),
            pl.BlockSpec((tokens, 1), lambda i: (0, 0)),
        ],
        out_specs=pl.BlockSpec((tokens, HEAD), lambda i: (0, i)),
        out_shape=jax.ShapeDtypeStruct((tokens, kv_width), jnp.bfloat16),
    )(queries, keys, grads, segments, segments.reshape(tokens, 1))


def project_kernel(chips, steps, cuts, own_ref, other_ref, *rest):
    row_refs, out_refs, gathered = rest[:chips], rest[-chips * (len(cuts) - 1) - 1:-1], rest[-1]
    taken, depth = row_refs[0].shape
    step = pl.program_id(0)

    @pl.when(step == 0)
    def _():
        for by in range(chips):
            gathered[by] = row_refs[by][...]

    def multiply(weight_ref):
        product = lax.dot_general(
            gathered[...].reshape(chips * taken, depth), weight_ref[...], (((1,), (1,)), ((), ())),
            preferred_element_type=jnp.float32,
        ).astype(jnp.bfloat16)
        for part, (start, end) in enumerate(zip(cuts, cuts[1:])):
            for by in range(chips):
                out_refs[part * chips + by][...] = product[by * taken + start:by * taken + end]

    @pl.when(step < steps)
    def _():
        multiply(own_ref)

    @pl.when(step >= steps)
    def _():
        multiply(other_ref)


def project(rows, own, other, cuts, after):
    chips = len(rows)
    taken, depth = rows[0].shape
    width = own.shape[0]
    block = min(width, 512)
    steps = width // block
    counts = [end - start for start, end in zip(cuts, cuts[1:]) for by in range(chips)]
    results = list(call(
        functools.partial(project_kernel, chips, steps, cuts), "project",
        4 * chips * taken * depth * width, 2 * (chips * taken * (depth + 2 * width) + 2 * width * depth),
        grid=(CORES * steps,),
        in_specs=[
            pl.BlockSpec((block, depth), lambda i: (jnp.minimum(i, steps - 1), 0)),
            pl.BlockSpec((block, depth), lambda i: (jnp.maximum(i - steps, 0), 0)),
        ] + [pl.BlockSpec((taken, depth), lambda i: (0, 0))] * chips + [whole] * len(after),
        out_specs=[pl.BlockSpec((count, block), lambda i: (0, i)) for count in counts],
        out_shape=[jax.ShapeDtypeStruct((count, CORES * width), jnp.bfloat16) for count in counts],
        scratch_shapes=[pltpu.VMEM((chips, taken, depth), jnp.bfloat16)],
    )(own, other, *rows, *after))
    return [results[at:at + chips] for at in range(0, len(results), chips)]


def backward_kernel(chips, place_ref, x_ref, gain_ref, grad_ref, *rest):
    cot_refs, out_ref = rest[:chips], rest[-1]
    chip, core = place_ref[0], place_ref[1]
    values = x_ref[...].astype(jnp.float32)
    width = cot_refs[0].shape[1] // CORES
    inverse = lax.rsqrt(jnp.mean(values * values, axis=-1, keepdims=True) + norm_eps)
    inner = jnp.zeros_like(inverse)

    def parts():
        for by, cot_ref in enumerate(cot_refs):
            source = lax.rem(chip + chips - by, chips)
            for half in range(CORES):
                cols = part_columns(source, half, core, width)
                cot = cot_ref[:, half * width:(half + 1) * width].astype(jnp.float32)
                yield cols, gain_ref[:, cols].astype(jnp.float32) * cot

    for cols, scaled in parts():
        inner += jnp.sum(x_ref[:, cols].astype(jnp.float32) * scaled, axis=-1, keepdims=True)
    factor = inverse * inverse * inverse * (inner / x_ref.shape[1])
    for cols, scaled in parts():
        out_ref[:, cols] = (
            grad_ref[:, cols].astype(jnp.float32)
            + inverse * scaled
            - x_ref[:, cols].astype(jnp.float32) * factor
        ).astype(out_ref.dtype)


def norm_backward(place, cots, rows, gain, grads, start, after):
    tokens, width = rows.shape
    taken, part_width = cots[0].shape
    block = math.gcd(math.gcd(start, taken), 32)
    first = start // block
    return call(
        functools.partial(backward_kernel, len(cots)), "norm_backward",
        10 * taken * width, 8 * taken * width,
        grid=(taken // block,),
        in_specs=[
            scalars,
            pl.BlockSpec((block, width), lambda i: (first + i, 0)),
            pl.BlockSpec((1, width), lambda i: (0, 0)),
            pl.BlockSpec((block, width), lambda i: (first + i, 0)),
        ] + [pl.BlockSpec((block, part_width), lambda i: (i, 0))] * len(cots) + [whole] * len(after),
        out_specs=pl.BlockSpec((block, width), lambda i: (i, 0)),
        out_shape=jax.ShapeDtypeStruct((taken, width), jnp.bfloat16),
    )(place, rows, gain, grads, *cots, *after)


def outer_kernel(groups, sums, halves, *refs):
    arrays = sum(groups)
    cots, columns, terms = refs[:arrays], refs[arrays:2 * arrays], refs[2 * arrays:2 * arrays + sums]
    total, at = None, 0
    for size in groups:
        column, cot = columns[at][...], cots[at][...]
        for more in range(at + 1, at + size):
            column, cot = column + columns[more][...], cot + cots[more][...]
        at += size
        product = lax.dot_general(
            column, cot, (((0,), (0,)), ((), ())), preferred_element_type=jnp.float32
        )
        total = product if total is None else total + product
    for term in terms:
        total += term[...].astype(jnp.float32)
    if halves:
        lower, upper = refs[2 * arrays + sums:2 * arrays + sums + 2]
        in_lower = pl.program_id(0) < pl.num_programs(0) // 2
        total += jnp.where(in_lower, lower[...], upper[...]).astype(jnp.float32)
    refs[-1][...] = total.astype(refs[-1].dtype)


def outer(groups, cot_width, half, before, dtype, part=0, parts=1, halves=(), after=()):
    payloads = [payload for group in groups for payload in group]
    wide = payloads[0].shape[1]
    width = (wide - cot_width) // CORES
    block = math.gcd(math.gcd(width // 2, 256), cot_width)
    steps = width // parts // block
    skip = part * steps
    first = (cot_width + half * width) // block + skip
    middle = steps // 2
    tokens = sum(payload.shape[0] for payload in payloads)
    return call(
        functools.partial(outer_kernel, [len(group) for group in groups], len(before), len(halves)), "outer",
        2 * tokens * width * cot_width, 2 * tokens * width + 4 * width * cot_width,
        grid=(steps,),
        in_specs=[pl.BlockSpec((payload.shape[0], cot_width), lambda i: (0, 0)) for payload in payloads]
        + [pl.BlockSpec((payload.shape[0], block), lambda i: (0, first + i)) for payload in payloads]
        + [pl.BlockSpec((block, cot_width), lambda i: (skip + i, 0)) for term in before]
        + [
            pl.BlockSpec((block, cot_width), lambda i: (jnp.minimum(i, middle - 1), 0)),
            pl.BlockSpec((block, cot_width), lambda i: (jnp.maximum(i - middle, 0), 0)),
        ][:len(halves)]
        + [whole] * len(after),
        out_specs=pl.BlockSpec((block, cot_width), lambda i: (i, 0)),
        out_shape=jax.ShapeDtypeStruct((width // parts, cot_width), dtype),
    )(*payloads, *payloads, *before, *halves, *after)


def shards(
    new_input,
    new_gain,
    queries,
    new_keys,
    context_grad,
    segment_ids,
    frozen_input,
    frozen_gain,
    output_grad,
    kv_grad,
    kv_weight,
):
    chips = lax.axis_size("dp") // CORES
    sections = lax.axis_size("pipe")
    tokens, kv_width = new_keys.shape[1:]
    at = lax.axis_index("dp")
    place = jnp.stack([at // CORES, at % CORES]).astype(jnp.int32)
    middle = chips // 2
    near = [by for by in range(1, chips) if by != middle]
    spread = tokens // 4

    rows = [kv_grad[0]] + [along_chips(kv_grad[0], chips - by, 1) for by in range(1, chips)]
    other_weight = swap_cores(kv_weight[0])
    value_cot = attend(queries[0], new_keys[0], context_grad[0], segment_ids)

    apply = functools.partial(normalize, place, new_input[0], new_gain, value_cot, chips)
    shared = apply([middle], 0, spread, [other_weight])[0]
    brought = [between_lines(shared, section, 0) for section in range(1, sections)]
    early = apply([0] + near[:1], 0, tokens, rows[1:])
    columns = [early[0]] + [along_chips(block, by) for block, by in zip(early[1:], near)]
    joint = stack_rows([shared] + brought, early[:1])
    moved = on_line(joint, middle, 0)
    returned = [moved[:spread]] + [
        between_lines(moved[section * spread:(section + 1) * spread], 0, section) for section in range(1, sections)
    ]

    cuts = [0, tokens * 5 // 8, tokens]
    parts = project(rows, kv_weight[0], other_weight, cuts, [joint])
    arrived = [
        [part[0]] + [along_chips(part[by], by, 1) for by in range(1, chips)] for part in parts
    ]
    backward = functools.partial(norm_backward, place, rows=frozen_input[0], gain=frozen_gain, grads=output_grad[0])
    above = backward(arrived[0], start=cuts[0], after=columns[1:])
    kept = apply([middle], spread, tokens - spread, [above] + arrived[1][1:])
    late = apply(near[1:], 0, tokens, kept)
    above = [above, backward(arrived[1], start=cuts[1], after=late[:1] + returned[1:])]
    below = [from_behind(half, "pipe", -1) for half in above]
    cot_below = stack_rows(below, [])

    columns += [along_chips(block, by) for block, by in zip(late, near[1:])]
    last = along_chips(kept[0], middle)

    groups = [[column] for column in columns] + [returned]
    sums = [outer(groups, kv_width, half, [], jnp.float32, after=above[1:]) for half in range(CORES)]
    given = [outer([[last]], kv_width, 1, [sums[1]], jnp.bfloat16, part, 2) for part in range(2)]
    taken = [swap_cores(part) for part in given]
    grad = outer([[last]], kv_width, 0, [sums[0]], jnp.float32, halves=taken, after=[cot_below])
    return (cot_below[None], grad[None])


def solution(mesh):
    placed = (
        P("pipe", "dp", None),
        P("pipe", None),
        P("pipe", "dp", None),
        P("pipe", "dp", None),
        P("pipe", "dp", None),
        P("pipe", "dp"),
        P("pipe", "dp", None),
        P("pipe", None),
        P("pipe", "dp", None),
        P("pipe", "dp", None),
        P("pipe", "dp", None),
    )
    return jax.shard_map(
        shards,
        mesh=mesh,
        in_specs=placed,
        out_specs=(P("pipe", "dp", None), P("pipe", "dp", None)),
        check_vma=False,
    )
```

```python
import functools
import math

import jax
import jax.numpy as jnp
from jax import lax
from jax.experimental import pallas as pl
from jax.experimental.pallas import tpu as pltpu
from jax.sharding import PartitionSpec as P

HEAD = 128
CORES = 2
MIB = 1 << 20

norm_eps = 1e-05
masked_value = -1e30

whole = pl.BlockSpec(memory_space=pl.ANY)
scalars = pl.BlockSpec(memory_space=pltpu.SMEM)


def from_behind(array, axis, by):
    length = lax.axis_size(axis)
    pairs = [(i, i + by) for i in range(length) if 0 <= i + by < length]
    return lax.ppermute(array, axis, pairs)


def along_chips(array, by, first=0):
    length = lax.axis_size("dp")
    pairs = [
        (line * length + i, line * length + ((i + by * CORES) % length if line >= first else i ^ 1))
        for line in range(lax.axis_size("pipe")) for i in range(length)
    ]
    return lax.ppermute(array, ("pipe", "dp"), pairs)


def between_lines(array, source, target):
    length = lax.axis_size("dp")
    pairs = [(source * length + i, target * length + i) for i in range(length)]
    return lax.ppermute(array, ("pipe", "dp"), pairs)


def on_line(array, by, line):
    length = lax.axis_size("dp")
    pairs = [(line * length + i, line * length + (i + by * CORES) % length) for i in range(length)]
    return lax.ppermute(array, ("pipe", "dp"), pairs)


def swap_cores(array):
    length = lax.axis_size("dp")
    return lax.ppermute(array, "dp", [(i, i ^ 1) for i in range(length)])


def call(body, name, flops, nbytes, vmem=24, **kwargs):
    return pl.pallas_call(
        body,
        name=name,
        compiler_params=pltpu.CompilerParams(vmem_limit_bytes=vmem * MIB),
        cost_estimate=pl.CostEstimate(flops=flops, bytes_accessed=nbytes, transcendentals=0),
        **kwargs,
    )


def part_columns(chip, half, core, width):
    owner = chip * CORES + (core if half == 0 else CORES - 1 - core)
    return pl.ds(pl.multiple_of(owner * width, width), width)


def norm_kernel(chips, ahead, place_ref, x_ref, gain_ref, cot_ref, *rest):
    out_refs = rest[-len(ahead):]
    chip, core = place_ref[0], place_ref[1]
    values = x_ref[...].astype(jnp.float32)
    inverse = lax.rsqrt(jnp.mean(values * values, axis=-1, keepdims=True) + norm_eps)
    front = cot_ref.shape[1]
    width = (out_refs[0].shape[1] - front) // CORES
    for by, out_ref in zip(ahead, out_refs):
        to = lax.rem(chip + by, chips)
        out_ref[:, :front] = cot_ref[...]
        for half in range(CORES):
            cols = part_columns(to, half, core, width)
            out_ref[:, front + half * width:front + (half + 1) * width] = (
                x_ref[:, cols].astype(jnp.float32) * inverse * gain_ref[:, cols].astype(jnp.float32)
            ).astype(out_ref.dtype)


def normalize(place, rows, gain, cot, chips, ahead, start, count, after):
    width = rows.shape[1]
    front = cot.shape[1]
    block = math.gcd(math.gcd(start, count), 32)
    first = start // block
    out_width = front + width // chips
    return list(call(
        functools.partial(norm_kernel, chips, ahead), "norm_forward",
        4 * count * width, 2 * count * width + 2 * count * out_width * len(ahead),
        grid=(count // block,),
        in_specs=[
            scalars,
            pl.BlockSpec((block, width), lambda i: (first + i, 0)),
            pl.BlockSpec((1, width), lambda i: (0, 0)),
            pl.BlockSpec((block, front), lambda i: (first + i, 0)),
        ] + [whole] * len(after),
        out_specs=[pl.BlockSpec((block, out_width), lambda i: (i, 0))] * len(ahead),
        out_shape=[jax.ShapeDtypeStruct((count, out_width), jnp.bfloat16)] * len(ahead),
    )(place, rows, gain, cot, *after))


def stack_kernel(count, *refs):
    at = 0
    for ref in refs[:count]:
        refs[-1][at:at + ref.shape[0]] = ref[...]
        at += ref.shape[0]


def stack_rows(arrays, after):
    width = arrays[0].shape[1]
    tall = sum(array.shape[0] for array in arrays)
    return call(
        functools.partial(stack_kernel, len(arrays)), "stack_rows", 0, 4 * tall * width,
        grid=(1,),
        in_specs=[pl.BlockSpec(array.shape, lambda i: (0, 0)) for array in arrays] + [whole] * len(after),
        out_specs=pl.BlockSpec((tall, width), lambda i: (0, 0)),
        out_shape=jax.ShapeDtypeStruct((tall, width), arrays[0].dtype),
    )(*arrays, *after)


def attend_kernel(query_ref, key_ref, grad_ref, row_seg_ref, col_seg_ref, out_ref):
    tokens = key_ref.shape[0]
    group = query_ref.shape[1] // HEAD
    at_query = lax.broadcasted_iota(jnp.int32, (tokens, tokens), 0)
    at_key = lax.broadcasted_iota(jnp.int32, (tokens, tokens), 1)
    visible = (col_seg_ref[...] == row_seg_ref[...]) & (at_key <= at_query)
    keys = key_ref[...]
    total = jnp.zeros((tokens, HEAD), jnp.float32)
    for head in range(group):
        cols = slice(head * HEAD, (head + 1) * HEAD)
        scores = lax.dot_general(
            query_ref[:, cols], keys, (((1,), (1,)), ((), ())),
            preferred_element_type=jnp.float32,
        ) / math.sqrt(HEAD)
        masked = jnp.where(visible, scores, masked_value)
        highest = jnp.max(masked, axis=-1, keepdims=True)
        weights = jnp.where(visible, jnp.exp(masked - highest), 0.0)
        attention = (weights / jnp.sum(weights, axis=-1, keepdims=True)).astype(jnp.bfloat16)
        total += lax.dot_general(
            attention, grad_ref[:, cols], (((0,), (0,)), ((), ())),
            preferred_element_type=jnp.float32,
        )
    out_ref[...] = total.astype(out_ref.dtype)


def attend(queries, keys, grads, segments):
    tokens, kv_width = keys.shape
    heads = kv_width // HEAD
    wide = queries.shape[1] // heads
    return call(
        attend_kernel, "attend",
        4 * tokens * tokens * queries.shape[1], 4 * tokens * queries.shape[1],
        grid=(heads,),
        in_specs=[
            pl.BlockSpec((tokens, wide), lambda i: (0, i)),
            pl.BlockSpec((tokens, HEAD), lambda i: (0, i)),
            pl.BlockSpec((tokens, wide), lambda i: (0, i)),
            pl.BlockSpec((1, tokens), lambda i: (0, 0)),
            pl.BlockSpec((tokens, 1), lambda i: (0, 0)),
        ],
        out_specs=pl.BlockSpec((tokens, HEAD), lambda i: (0, i)),
        out_shape=jax.ShapeDtypeStruct((tokens, kv_width), jnp.bfloat16),
    )(queries, keys, grads, segments, segments.reshape(tokens, 1))


def project_kernel(chips, steps, cuts, own_ref, other_ref, *rest):
    row_refs, out_refs, gathered = rest[:chips], rest[-chips * (len(cuts) - 1) - 1:-1], rest[-1]
    taken, depth = row_refs[0].shape
    step = pl.program_id(0)

    @pl.when(step == 0)
    def _():
        for by in range(chips):
            gathered[by] = row_refs[by][...]

    def multiply(weight_ref):
        product = lax.dot_general(
            gathered[...].reshape(chips * taken, depth), weight_ref[...], (((1,), (1,)), ((), ())),
            preferred_element_type=jnp.float32,
        ).astype(jnp.bfloat16)
        for part, (start, end) in enumerate(zip(cuts, cuts[1:])):
            for by in range(chips):
                out_refs[part * chips + by][...] = product[by * taken + start:by * taken + end]

    @pl.when(step < steps)
    def _():
        multiply(own_ref)

    @pl.when(step >= steps)
    def _():
        multiply(other_ref)


def project(rows, own, other, cuts, after):
    chips = len(rows)
    taken, depth = rows[0].shape
    width = own.shape[0]
    block = min(width, 512)
    steps = width // block
    counts = [end - start for start, end in zip(cuts, cuts[1:]) for by in range(chips)]
    results = list(call(
        functools.partial(project_kernel, chips, steps, cuts), "project",
        4 * chips * taken * depth * width, 2 * (chips * taken * (depth + 2 * width) + 2 * width * depth),
        grid=(CORES * steps,),
        in_specs=[
            pl.BlockSpec((block, depth), lambda i: (jnp.minimum(i, steps - 1), 0)),
            pl.BlockSpec((block, depth), lambda i: (jnp.maximum(i - steps, 0), 0)),
        ] + [pl.BlockSpec((taken, depth), lambda i: (0, 0))] * chips + [whole] * len(after),
        out_specs=[pl.BlockSpec((count, block), lambda i: (0, i)) for count in counts],
        out_shape=[jax.ShapeDtypeStruct((count, CORES * width), jnp.bfloat16) for count in counts],
        scratch_shapes=[pltpu.VMEM((chips, taken, depth), jnp.bfloat16)],
    )(own, other, *rows, *after))
    return [results[at:at + chips] for at in range(0, len(results), chips)]


def backward_kernel(chips, place_ref, x_ref, gain_ref, grad_ref, *rest):
    cot_refs, out_ref = rest[:chips], rest[-1]
    chip, core = place_ref[0], place_ref[1]
    values = x_ref[...].astype(jnp.float32)
    width = cot_refs[0].shape[1] // CORES
    inverse = lax.rsqrt(jnp.mean(values * values, axis=-1, keepdims=True) + norm_eps)
    inner = jnp.zeros_like(inverse)

    def parts():
        for by, cot_ref in enumerate(cot_refs):
            source = lax.rem(chip + chips - by, chips)
            for half in range(CORES):
                cols = part_columns(source, half, core, width)
                cot = cot_ref[:, half * width:(half + 1) * width].astype(jnp.float32)
                yield cols, gain_ref[:, cols].astype(jnp.float32) * cot

    for cols, scaled in parts():
        inner += jnp.sum(x_ref[:, cols].astype(jnp.float32) * scaled, axis=-1, keepdims=True)
    factor = inverse * inverse * inverse * (inner / x_ref.shape[1])
    for cols, scaled in parts():
        out_ref[:, cols] = (
            grad_ref[:, cols].astype(jnp.float32)
            + inverse * scaled
            - x_ref[:, cols].astype(jnp.float32) * factor
        ).astype(out_ref.dtype)


def norm_backward(place, cots, rows, gain, grads, start, after):
    tokens, width = rows.shape
    taken, part_width = cots[0].shape
    block = math.gcd(math.gcd(start, taken), 32)
    first = start // block
    return call(
        functools.partial(backward_kernel, len(cots)), "norm_backward",
        10 * taken * width, 8 * taken * width,
        grid=(taken // block,),
        in_specs=[
            scalars,
            pl.BlockSpec((block, width), lambda i: (first + i, 0)),
            pl.BlockSpec((1, width), lambda i: (0, 0)),
            pl.BlockSpec((block, width), lambda i: (first + i, 0)),
        ] + [pl.BlockSpec((block, part_width), lambda i: (i, 0))] * len(cots) + [whole] * len(after),
        out_specs=pl.BlockSpec((block, width), lambda i: (i, 0)),
        out_shape=jax.ShapeDtypeStruct((taken, width), jnp.bfloat16),
    )(place, rows, gain, grads, *cots, *after)


def outer_kernel(groups, sums, halves, *refs):
    arrays = sum(groups)
    cots, columns, terms = refs[:arrays], refs[arrays:2 * arrays], refs[2 * arrays:2 * arrays + sums]
    total, at = None, 0
    for size in groups:
        column, cot = columns[at][...], cots[at][...]
        for more in range(at + 1, at + size):
            column, cot = column + columns[more][...], cot + cots[more][...]
        at += size
        product = lax.dot_general(
            column, cot, (((0,), (0,)), ((), ())), preferred_element_type=jnp.float32
        )
        total = product if total is None else total + product
    for term in terms:
        total += term[...].astype(jnp.float32)
    if halves:
        lower, upper = refs[2 * arrays + sums:2 * arrays + sums + 2]
        in_lower = pl.program_id(0) < pl.num_programs(0) // 2
        total += jnp.where(in_lower, lower[...], upper[...]).astype(jnp.float32)
    refs[-1][...] = total.astype(refs[-1].dtype)


def outer(groups, cot_width, half, before, dtype, part=0, parts=1, halves=(), after=()):
    payloads = [payload for group in groups for payload in group]
    wide = payloads[0].shape[1]
    width = (wide - cot_width) // CORES
    block = math.gcd(math.gcd(width // 2, 256), cot_width)
    steps = width // parts // block
    skip = part * steps
    first = (cot_width + half * width) // block + skip
    middle = steps // 2
    tokens = sum(payload.shape[0] for payload in payloads)
    return call(
        functools.partial(outer_kernel, [len(group) for group in groups], len(before), len(halves)), "outer",
        2 * tokens * width * cot_width, 2 * tokens * width + 4 * width * cot_width,
        grid=(steps,),
        in_specs=[pl.BlockSpec((payload.shape[0], cot_width), lambda i: (0, 0)) for payload in payloads]
        + [pl.BlockSpec((payload.shape[0], block), lambda i: (0, first + i)) for payload in payloads]
        + [pl.BlockSpec((block, cot_width), lambda i: (skip + i, 0)) for term in before]
        + [
            pl.BlockSpec((block, cot_width), lambda i: (jnp.minimum(i, middle - 1), 0)),
            pl.BlockSpec((block, cot_width), lambda i: (jnp.maximum(i - middle, 0), 0)),
        ][:len(halves)]
        + [whole] * len(after),
        out_specs=pl.BlockSpec((block, cot_width), lambda i: (i, 0)),
        out_shape=jax.ShapeDtypeStruct((width // parts, cot_width), dtype),
    )(*payloads, *payloads, *before, *halves, *after)


def shards(
    new_input,
    new_gain,
    queries,
    new_keys,
    context_grad,
    segment_ids,
    frozen_input,
    frozen_gain,
    output_grad,
    kv_grad,
    kv_weight,
):
    chips = lax.axis_size("dp") // CORES
    sections = lax.axis_size("pipe")
    tokens, kv_width = new_keys.shape[1:]
    at = lax.axis_index("dp")
    place = jnp.stack([at // CORES, at % CORES]).astype(jnp.int32)
    middle = chips // 2
    near = [by for by in range(1, chips) if by != middle]
    spread = tokens // 4

    rows = [kv_grad[0]] + [along_chips(kv_grad[0], chips - by, 1) for by in range(1, chips)]
    other_weight = swap_cores(kv_weight[0])
    value_cot = attend(queries[0], new_keys[0], context_grad[0], segment_ids)

    apply = functools.partial(normalize, place, new_input[0], new_gain, value_cot, chips)
    shared = apply([middle], 0, spread, [other_weight])[0]
    brought = [between_lines(shared, section, 0) for section in range(1, sections)]
    early = apply([0] + near[:1], 0, tokens, rows[1:])
    columns = [early[0]] + [along_chips(block, by) for block, by in zip(early[1:], near)]
    joint = stack_rows([shared] + brought, early[:1])
    moved = on_line(joint, middle, 0)
    returned = [moved[:spread]] + [
        between_lines(moved[section * spread:(section + 1) * spread], 0, section) for section in range(1, sections)
    ]

    cuts = [0, tokens * 5 // 8, tokens]
    parts = project(rows, kv_weight[0], other_weight, cuts, [joint])
    arrived = [
        [part[0]] + [along_chips(part[by], by, 1) for by in range(1, chips)] for part in parts
    ]
    backward = functools.partial(norm_backward, place, rows=frozen_input[0], gain=frozen_gain, grads=output_grad[0])
    above = backward(arrived[0], start=cuts[0], after=columns[1:])
    kept = apply([middle], spread, tokens - spread, [above] + [arrived[1][by] for by in near])
    late = apply(near[1:], 0, tokens, kept)
    above = [above, backward(arrived[1], start=cuts[1], after=late[:1])]
    below = [from_behind(half, "pipe", -1) for half in above]
    cot_below = stack_rows(below, [])

    columns += [along_chips(block, by) for block, by in zip(late, near[1:])]
    last = along_chips(kept[0], middle)

    groups = [[column] for column in columns] + [returned]
    sums = [outer(groups, kv_width, half, [], jnp.float32, after=above[1:]) for half in range(CORES)]
    given = [outer([[last]], kv_width, 1, sums[1:], jnp.bfloat16, part, 2, after=sums[:1]) for part in range(2)]
    taken = [swap_cores(part) for part in given]
    grad = outer([[last]], kv_width, 0, [sums[0]], jnp.float32, halves=taken, after=[cot_below])
    return (cot_below[None], grad[None])


def solution(mesh):
    placed = (
        P("pipe", "dp", None),
        P("pipe", None),
        P("pipe", "dp", None),
        P("pipe", "dp", None),
        P("pipe", "dp", None),
        P("pipe", "dp"),
        P("pipe", "dp", None),
        P("pipe", None),
        P("pipe", "dp", None),
        P("pipe", "dp", None),
        P("pipe", "dp", None),
    )
    return jax.shard_map(
        shards,
        mesh=mesh,
        in_specs=placed,
        out_specs=(P("pipe", "dp", None), P("pipe", "dp", None)),
        check_vma=False,
    )
```

```python
import functools
import math

import jax
import jax.numpy as jnp
from jax import lax
from jax.experimental import pallas as pl
from jax.experimental.pallas import tpu as pltpu
from jax.sharding import PartitionSpec as P

HEAD = 128
CORES = 2
MIB = 1 << 20

norm_eps = 1e-05
masked_value = -1e30

whole = pl.BlockSpec(memory_space=pl.ANY)
scalars = pl.BlockSpec(memory_space=pltpu.SMEM)


def from_behind(array, axis, by):
    length = lax.axis_size(axis)
    pairs = [(i, i + by) for i in range(length) if 0 <= i + by < length]
    return lax.ppermute(array, axis, pairs)


def along_chips(array, by, first=0):
    length = lax.axis_size("dp")
    pairs = [
        (line * length + i, line * length + ((i + by * CORES) % length if line >= first else i ^ 1))
        for line in range(lax.axis_size("pipe")) for i in range(length)
    ]
    return lax.ppermute(array, ("pipe", "dp"), pairs)


def between_lines(array, source, target):
    length = lax.axis_size("dp")
    pairs = [(source * length + i, target * length + i) for i in range(length)]
    return lax.ppermute(array, ("pipe", "dp"), pairs)


def on_line(array, by, line):
    length = lax.axis_size("dp")
    pairs = [(line * length + i, line * length + (i + by * CORES) % length) for i in range(length)]
    return lax.ppermute(array, ("pipe", "dp"), pairs)


def swap_cores(array):
    length = lax.axis_size("dp")
    return lax.ppermute(array, "dp", [(i, i ^ 1) for i in range(length)])


def call(body, name, flops, nbytes, vmem=24, **kwargs):
    return pl.pallas_call(
        body,
        name=name,
        compiler_params=pltpu.CompilerParams(vmem_limit_bytes=vmem * MIB),
        cost_estimate=pl.CostEstimate(flops=flops, bytes_accessed=nbytes, transcendentals=0),
        **kwargs,
    )


def part_columns(chip, half, core, width):
    owner = chip * CORES + (core if half == 0 else CORES - 1 - core)
    return pl.ds(pl.multiple_of(owner * width, width), width)


def norm_kernel(chips, ahead, place_ref, x_ref, gain_ref, cot_ref, *rest):
    out_refs = rest[-len(ahead):]
    chip, core = place_ref[0], place_ref[1]
    values = x_ref[...].astype(jnp.float32)
    inverse = lax.rsqrt(jnp.mean(values * values, axis=-1, keepdims=True) + norm_eps)
    front = cot_ref.shape[1]
    width = (out_refs[0].shape[1] - front) // CORES
    for by, out_ref in zip(ahead, out_refs):
        to = lax.rem(chip + by, chips)
        out_ref[:, :front] = cot_ref[...]
        for half in range(CORES):
            cols = part_columns(to, half, core, width)
            out_ref[:, front + half * width:front + (half + 1) * width] = (
                x_ref[:, cols].astype(jnp.float32) * inverse * gain_ref[:, cols].astype(jnp.float32)
            ).astype(out_ref.dtype)


def normalize(place, rows, gain, cot, chips, ahead, start, count, after):
    width = rows.shape[1]
    front = cot.shape[1]
    block = math.gcd(math.gcd(start, count), 32)
    first = start // block
    out_width = front + width // chips
    return list(call(
        functools.partial(norm_kernel, chips, ahead), "norm_forward",
        4 * count * width, 2 * count * width + 2 * count * out_width * len(ahead),
        grid=(count // block,),
        in_specs=[
            scalars,
            pl.BlockSpec((block, width), lambda i: (first + i, 0)),
            pl.BlockSpec((1, width), lambda i: (0, 0)),
            pl.BlockSpec((block, front), lambda i: (first + i, 0)),
        ] + [whole] * len(after),
        out_specs=[pl.BlockSpec((block, out_width), lambda i: (i, 0))] * len(ahead),
        out_shape=[jax.ShapeDtypeStruct((count, out_width), jnp.bfloat16)] * len(ahead),
    )(place, rows, gain, cot, *after))


def stack_kernel(count, *refs):
    at = 0
    for ref in refs[:count]:
        refs[-1][at:at + ref.shape[0]] = ref[...]
        at += ref.shape[0]


def stack_rows(arrays, after):
    width = arrays[0].shape[1]
    tall = sum(array.shape[0] for array in arrays)
    return call(
        functools.partial(stack_kernel, len(arrays)), "stack_rows", 0, 4 * tall * width,
        grid=(1,),
        in_specs=[pl.BlockSpec(array.shape, lambda i: (0, 0)) for array in arrays] + [whole] * len(after),
        out_specs=pl.BlockSpec((tall, width), lambda i: (0, 0)),
        out_shape=jax.ShapeDtypeStruct((tall, width), arrays[0].dtype),
    )(*arrays, *after)


def attend_kernel(query_ref, key_ref, grad_ref, row_seg_ref, col_seg_ref, out_ref):
    tokens = key_ref.shape[0]
    group = query_ref.shape[1] // HEAD
    at_query = lax.broadcasted_iota(jnp.int32, (tokens, tokens), 0)
    at_key = lax.broadcasted_iota(jnp.int32, (tokens, tokens), 1)
    visible = (col_seg_ref[...] == row_seg_ref[...]) & (at_key <= at_query)
    keys = key_ref[...]
    total = jnp.zeros((tokens, HEAD), jnp.float32)
    for head in range(group):
        cols = slice(head * HEAD, (head + 1) * HEAD)
        scores = lax.dot_general(
            query_ref[:, cols], keys, (((1,), (1,)), ((), ())),
            preferred_element_type=jnp.float32,
        ) / math.sqrt(HEAD)
        masked = jnp.where(visible, scores, masked_value)
        highest = jnp.max(masked, axis=-1, keepdims=True)
        weights = jnp.where(visible, jnp.exp(masked - highest), 0.0)
        attention = (weights / jnp.sum(weights, axis=-1, keepdims=True)).astype(jnp.bfloat16)
        total += lax.dot_general(
            attention, grad_ref[:, cols], (((0,), (0,)), ((), ())),
            preferred_element_type=jnp.float32,
        )
    out_ref[...] = total.astype(out_ref.dtype)


def attend(queries, keys, grads, segments):
    tokens, kv_width = keys.shape
    heads = kv_width // HEAD
    wide = queries.shape[1] // heads
    return call(
        attend_kernel, "attend",
        4 * tokens * tokens * queries.shape[1], 4 * tokens * queries.shape[1],
        grid=(heads,),
        in_specs=[
            pl.BlockSpec((tokens, wide), lambda i: (0, i)),
            pl.BlockSpec((tokens, HEAD), lambda i: (0, i)),
            pl.BlockSpec((tokens, wide), lambda i: (0, i)),
            pl.BlockSpec((1, tokens), lambda i: (0, 0)),
            pl.BlockSpec((tokens, 1), lambda i: (0, 0)),
        ],
        out_specs=pl.BlockSpec((tokens, HEAD), lambda i: (0, i)),
        out_shape=jax.ShapeDtypeStruct((tokens, kv_width), jnp.bfloat16),
    )(queries, keys, grads, segments, segments.reshape(tokens, 1))


def project_kernel(chips, steps, cuts, own_ref, other_ref, *rest):
    row_refs, out_refs, gathered = rest[:chips], rest[-chips * (len(cuts) - 1) - 1:-1], rest[-1]
    taken, depth = row_refs[0].shape
    step = pl.program_id(0)

    @pl.when(step == 0)
    def _():
        for by in range(chips):
            gathered[by] = row_refs[by][...]

    def multiply(weight_ref):
        product = lax.dot_general(
            gathered[...].reshape(chips * taken, depth), weight_ref[...], (((1,), (1,)), ((), ())),
            preferred_element_type=jnp.float32,
        ).astype(jnp.bfloat16)
        for part, (start, end) in enumerate(zip(cuts, cuts[1:])):
            for by in range(chips):
                out_refs[part * chips + by][...] = product[by * taken + start:by * taken + end]

    @pl.when(step < steps)
    def _():
        multiply(own_ref)

    @pl.when(step >= steps)
    def _():
        multiply(other_ref)


def project(rows, own, other, cuts, after):
    chips = len(rows)
    taken, depth = rows[0].shape
    width = own.shape[0]
    block = min(width, 512)
    steps = width // block
    counts = [end - start for start, end in zip(cuts, cuts[1:]) for by in range(chips)]
    results = list(call(
        functools.partial(project_kernel, chips, steps, cuts), "project",
        4 * chips * taken * depth * width, 2 * (chips * taken * (depth + 2 * width) + 2 * width * depth),
        grid=(CORES * steps,),
        in_specs=[
            pl.BlockSpec((block, depth), lambda i: (jnp.minimum(i, steps - 1), 0)),
            pl.BlockSpec((block, depth), lambda i: (jnp.maximum(i - steps, 0), 0)),
        ] + [pl.BlockSpec((taken, depth), lambda i: (0, 0))] * chips + [whole] * len(after),
        out_specs=[pl.BlockSpec((count, block), lambda i: (0, i)) for count in counts],
        out_shape=[jax.ShapeDtypeStruct((count, CORES * width), jnp.bfloat16) for count in counts],
        scratch_shapes=[pltpu.VMEM((chips, taken, depth), jnp.bfloat16)],
    )(own, other, *rows, *after))
    return [results[at:at + chips] for at in range(0, len(results), chips)]


def backward_kernel(chips, place_ref, x_ref, gain_ref, grad_ref, *rest):
    cot_refs, out_ref = rest[:chips], rest[-1]
    chip, core = place_ref[0], place_ref[1]
    values = x_ref[...].astype(jnp.float32)
    width = cot_refs[0].shape[1] // CORES
    inverse = lax.rsqrt(jnp.mean(values * values, axis=-1, keepdims=True) + norm_eps)
    inner = jnp.zeros_like(inverse)

    def parts():
        for by, cot_ref in enumerate(cot_refs):
            source = lax.rem(chip + chips - by, chips)
            for half in range(CORES):
                cols = part_columns(source, half, core, width)
                cot = cot_ref[:, half * width:(half + 1) * width].astype(jnp.float32)
                yield cols, gain_ref[:, cols].astype(jnp.float32) * cot

    for cols, scaled in parts():
        inner += jnp.sum(x_ref[:, cols].astype(jnp.float32) * scaled, axis=-1, keepdims=True)
    factor = inverse * inverse * inverse * (inner / x_ref.shape[1])
    for cols, scaled in parts():
        out_ref[:, cols] = (
            grad_ref[:, cols].astype(jnp.float32)
            + inverse * scaled
            - x_ref[:, cols].astype(jnp.float32) * factor
        ).astype(out_ref.dtype)


def norm_backward(place, cots, rows, gain, grads, start, after):
    tokens, width = rows.shape
    taken, part_width = cots[0].shape
    block = math.gcd(math.gcd(start, taken), 32)
    first = start // block
    return call(
        functools.partial(backward_kernel, len(cots)), "norm_backward",
        10 * taken * width, 8 * taken * width,
        grid=(taken // block,),
        in_specs=[
            scalars,
            pl.BlockSpec((block, width), lambda i: (first + i, 0)),
            pl.BlockSpec((1, width), lambda i: (0, 0)),
            pl.BlockSpec((block, width), lambda i: (first + i, 0)),
        ] + [pl.BlockSpec((block, part_width), lambda i: (i, 0))] * len(cots) + [whole] * len(after),
        out_specs=pl.BlockSpec((block, width), lambda i: (i, 0)),
        out_shape=jax.ShapeDtypeStruct((taken, width), jnp.bfloat16),
    )(place, rows, gain, grads, *cots, *after)


def outer_kernel(groups, sums, halves, *refs):
    arrays = sum(groups)
    cots, columns, terms = refs[:arrays], refs[arrays:2 * arrays], refs[2 * arrays:2 * arrays + sums]
    total, at = None, 0
    for size in groups:
        column, cot = columns[at][...], cots[at][...]
        for more in range(at + 1, at + size):
            column, cot = column + columns[more][...], cot + cots[more][...]
        at += size
        product = lax.dot_general(
            column, cot, (((0,), (0,)), ((), ())), preferred_element_type=jnp.float32
        )
        total = product if total is None else total + product
    for term in terms:
        total += term[...].astype(jnp.float32)
    if halves:
        lower, upper = refs[2 * arrays + sums:2 * arrays + sums + 2]
        in_lower = pl.program_id(0) < pl.num_programs(0) // 2
        total += jnp.where(in_lower, lower[...], upper[...]).astype(jnp.float32)
    refs[-1][...] = total.astype(refs[-1].dtype)


def outer(groups, cot_width, half, before, dtype, part=0, parts=1, halves=(), after=()):
    payloads = [payload for group in groups for payload in group]
    wide = payloads[0].shape[1]
    width = (wide - cot_width) // CORES
    block = math.gcd(math.gcd(width // 2, 256), cot_width)
    steps = width // parts // block
    skip = part * steps
    first = (cot_width + half * width) // block + skip
    middle = steps // 2
    tokens = sum(payload.shape[0] for payload in payloads)
    return call(
        functools.partial(outer_kernel, [len(group) for group in groups], len(before), len(halves)), "outer",
        2 * tokens * width * cot_width, 2 * tokens * width + 4 * width * cot_width,
        grid=(steps,),
        in_specs=[pl.BlockSpec((payload.shape[0], cot_width), lambda i: (0, 0)) for payload in payloads]
        + [pl.BlockSpec((payload.shape[0], block), lambda i: (0, first + i)) for payload in payloads]
        + [pl.BlockSpec((block, cot_width), lambda i: (skip + i, 0)) for term in before]
        + [
            pl.BlockSpec((block, cot_width), lambda i: (jnp.minimum(i, middle - 1), 0)),
            pl.BlockSpec((block, cot_width), lambda i: (jnp.maximum(i - middle, 0), 0)),
        ][:len(halves)]
        + [whole] * len(after),
        out_specs=pl.BlockSpec((block, cot_width), lambda i: (i, 0)),
        out_shape=jax.ShapeDtypeStruct((width // parts, cot_width), dtype),
    )(*payloads, *payloads, *before, *halves, *after)


def shards(
    new_input,
    new_gain,
    queries,
    new_keys,
    context_grad,
    segment_ids,
    frozen_input,
    frozen_gain,
    output_grad,
    kv_grad,
    kv_weight,
):
    chips = lax.axis_size("dp") // CORES
    sections = lax.axis_size("pipe")
    tokens, kv_width = new_keys.shape[1:]
    at = lax.axis_index("dp")
    place = jnp.stack([at // CORES, at % CORES]).astype(jnp.int32)
    middle = chips // 2
    near = [by for by in range(1, chips) if by != middle]
    spread = tokens * 3 // 8

    rows = [kv_grad[0]] + [along_chips(kv_grad[0], chips - by, 1) for by in range(1, chips)]
    other_weight = swap_cores(kv_weight[0])
    value_cot = attend(queries[0], new_keys[0], context_grad[0], segment_ids)

    apply = functools.partial(normalize, place, new_input[0], new_gain, value_cot, chips)
    shared = apply([middle], 0, spread, [other_weight])[0]
    brought = [between_lines(shared, section, 0) for section in range(1, sections)]
    early = apply([0] + near[:1], 0, tokens, rows[1:])
    columns = [early[0]] + [along_chips(block, by) for block, by in zip(early[1:], near)]
    joint = stack_rows([shared] + brought, early[:1])
    moved = on_line(joint, middle, 0)
    returned = [moved[:spread]] + [
        between_lines(moved[section * spread:(section + 1) * spread], 0, section) for section in range(1, sections)
    ]

    cuts = [0, tokens * 5 // 8, tokens]
    parts = project(rows, kv_weight[0], other_weight, cuts, [joint])
    arrived = [
        [part[0]] + [along_chips(part[by], by, 1) for by in range(1, chips)] for part in parts
    ]
    backward = functools.partial(norm_backward, place, rows=frozen_input[0], gain=frozen_gain, grads=output_grad[0])
    above = backward(arrived[0], start=cuts[0], after=columns[1:])
    kept = apply([middle], spread, tokens - spread, [above] + [arrived[1][by] for by in near])
    late = apply(near[1:], 0, tokens, kept)
    above = [above, backward(arrived[1], start=cuts[1], after=late[:1])]
    below = [from_behind(half, "pipe", -1) for half in above]
    cot_below = stack_rows(below, [])

    groups = [[column] for column in columns] + [returned]
    last = [[along_chips(block, by)] for block, by in zip(late + kept, near[1:] + [middle])]
    sums = [outer(groups, kv_width, half, [], jnp.float32, after=above[1:]) for half in range(CORES)]
    given = [
        outer(last, kv_width, 1, sums[1:], jnp.bfloat16, part, 2, after=sums[:1]) for part in range(2)
    ]
    taken = [swap_cores(part) for part in given]
    grad = outer(last, kv_width, 0, sums[:1], jnp.float32, halves=taken, after=[cot_below])
    return (cot_below[None], grad[None])


def solution(mesh):
    placed = (
        P("pipe", "dp", None),
        P("pipe", None),
        P("pipe", "dp", None),
        P("pipe", "dp", None),
        P("pipe", "dp", None),
        P("pipe", "dp"),
        P("pipe", "dp", None),
        P("pipe", None),
        P("pipe", "dp", None),
        P("pipe", "dp", None),
        P("pipe", "dp", None),
    )
    return jax.shard_map(
        shards,
        mesh=mesh,
        in_specs=placed,
        out_specs=(P("pipe", "dp", None), P("pipe", "dp", None)),
        check_vma=False,
    )
```

```python
import functools
import math

import jax
import jax.numpy as jnp
from jax import lax
from jax.experimental import pallas as pl
from jax.experimental.pallas import tpu as pltpu
from jax.sharding import PartitionSpec as P

HEAD = 128
CORES = 2
MIB = 1 << 20

norm_eps = 1e-05
masked_value = -1e30

whole = pl.BlockSpec(memory_space=pl.ANY)
scalars = pl.BlockSpec(memory_space=pltpu.SMEM)


def from_behind(array, axis, by):
    length = lax.axis_size(axis)
    pairs = [(i, i + by) for i in range(length) if 0 <= i + by < length]
    return lax.ppermute(array, axis, pairs)


def along_chips(array, by, first=0):
    length = lax.axis_size("dp")
    pairs = [
        (line * length + i, line * length + ((i + by * CORES) % length if line >= first else i ^ 1))
        for line in range(lax.axis_size("pipe")) for i in range(length)
    ]
    return lax.ppermute(array, ("pipe", "dp"), pairs)


def between_lines(array, source, target):
    length = lax.axis_size("dp")
    pairs = [(source * length + i, target * length + i) for i in range(length)]
    return lax.ppermute(array, ("pipe", "dp"), pairs)


def on_line(array, by, line):
    length = lax.axis_size("dp")
    pairs = [(line * length + i, line * length + (i + by * CORES) % length) for i in range(length)]
    return lax.ppermute(array, ("pipe", "dp"), pairs)


def swap_cores(array):
    length = lax.axis_size("dp")
    return lax.ppermute(array, "dp", [(i, i ^ 1) for i in range(length)])


def call(body, name, flops, nbytes, vmem=24, **kwargs):
    return pl.pallas_call(
        body,
        name=name,
        compiler_params=pltpu.CompilerParams(vmem_limit_bytes=vmem * MIB),
        cost_estimate=pl.CostEstimate(flops=flops, bytes_accessed=nbytes, transcendentals=0),
        **kwargs,
    )


def part_columns(chip, half, core, width):
    owner = chip * CORES + (core if half == 0 else CORES - 1 - core)
    return pl.ds(pl.multiple_of(owner * width, width), width)


def norm_kernel(chips, ahead, place_ref, x_ref, gain_ref, cot_ref, *rest):
    out_refs = rest[-len(ahead):]
    chip, core = place_ref[0], place_ref[1]
    values = x_ref[...].astype(jnp.float32)
    inverse = lax.rsqrt(jnp.mean(values * values, axis=-1, keepdims=True) + norm_eps)
    front = cot_ref.shape[1]
    width = (out_refs[0].shape[1] - front) // CORES
    for by, out_ref in zip(ahead, out_refs):
        to = lax.rem(chip + by, chips)
        out_ref[:, :front] = cot_ref[...]
        for half in range(CORES):
            cols = part_columns(to, half, core, width)
            out_ref[:, front + half * width:front + (half + 1) * width] = (
                x_ref[:, cols].astype(jnp.float32) * inverse * gain_ref[:, cols].astype(jnp.float32)
            ).astype(out_ref.dtype)


def normalize(place, rows, gain, cot, chips, ahead, start, count, after):
    width = rows.shape[1]
    front = cot.shape[1]
    block = math.gcd(math.gcd(start, count), 32)
    first = start // block
    out_width = front + width // chips
    return list(call(
        functools.partial(norm_kernel, chips, ahead), "norm_forward",
        4 * count * width, 2 * count * width + 2 * count * out_width * len(ahead),
        grid=(count // block,),
        in_specs=[
            scalars,
            pl.BlockSpec((block, width), lambda i: (first + i, 0)),
            pl.BlockSpec((1, width), lambda i: (0, 0)),
            pl.BlockSpec((block, front), lambda i: (first + i, 0)),
        ] + [whole] * len(after),
        out_specs=[pl.BlockSpec((block, out_width), lambda i: (i, 0))] * len(ahead),
        out_shape=[jax.ShapeDtypeStruct((count, out_width), jnp.bfloat16)] * len(ahead),
    )(place, rows, gain, cot, *after))


def stack_kernel(count, *refs):
    at = 0
    for ref in refs[:count]:
        refs[-1][at:at + ref.shape[0]] = ref[...]
        at += ref.shape[0]


def stack_rows(arrays, after):
    width = arrays[0].shape[1]
    tall = sum(array.shape[0] for array in arrays)
    return call(
        functools.partial(stack_kernel, len(arrays)), "stack_rows", 0, 4 * tall * width,
        grid=(1,),
        in_specs=[pl.BlockSpec(array.shape, lambda i: (0, 0)) for array in arrays] + [whole] * len(after),
        out_specs=pl.BlockSpec((tall, width), lambda i: (0, 0)),
        out_shape=jax.ShapeDtypeStruct((tall, width), arrays[0].dtype),
    )(*arrays, *after)


def attend_kernel(query_ref, key_ref, grad_ref, row_seg_ref, col_seg_ref, out_ref):
    tokens = key_ref.shape[0]
    group = query_ref.shape[1] // HEAD
    at_query = lax.broadcasted_iota(jnp.int32, (tokens, tokens), 0)
    at_key = lax.broadcasted_iota(jnp.int32, (tokens, tokens), 1)
    visible = (col_seg_ref[...] == row_seg_ref[...]) & (at_key <= at_query)
    keys = key_ref[...]
    total = jnp.zeros((tokens, HEAD), jnp.float32)
    for head in range(group):
        cols = slice(head * HEAD, (head + 1) * HEAD)
        scores = lax.dot_general(
            query_ref[:, cols], keys, (((1,), (1,)), ((), ())),
            preferred_element_type=jnp.float32,
        ) / math.sqrt(HEAD)
        masked = jnp.where(visible, scores, masked_value)
        highest = jnp.max(masked, axis=-1, keepdims=True)
        weights = jnp.where(visible, jnp.exp(masked - highest), 0.0)
        attention = (weights / jnp.sum(weights, axis=-1, keepdims=True)).astype(jnp.bfloat16)
        total += lax.dot_general(
            attention, grad_ref[:, cols], (((0,), (0,)), ((), ())),
            preferred_element_type=jnp.float32,
        )
    out_ref[...] = total.astype(out_ref.dtype)


def attend(queries, keys, grads, segments):
    tokens, kv_width = keys.shape
    heads = kv_width // HEAD
    wide = queries.shape[1] // heads
    return call(
        attend_kernel, "attend",
        4 * tokens * tokens * queries.shape[1], 4 * tokens * queries.shape[1],
        grid=(heads,),
        in_specs=[
            pl.BlockSpec((tokens, wide), lambda i: (0, i)),
            pl.BlockSpec((tokens, HEAD), lambda i: (0, i)),
            pl.BlockSpec((tokens, wide), lambda i: (0, i)),
            pl.BlockSpec((1, tokens), lambda i: (0, 0)),
            pl.BlockSpec((tokens, 1), lambda i: (0, 0)),
        ],
        out_specs=pl.BlockSpec((tokens, HEAD), lambda i: (0, i)),
        out_shape=jax.ShapeDtypeStruct((tokens, kv_width), jnp.bfloat16),
    )(queries, keys, grads, segments, segments.reshape(tokens, 1))


def project_kernel(chips, steps, cuts, own_ref, other_ref, *rest):
    row_refs, out_refs, gathered = rest[:chips], rest[-chips * (len(cuts) - 1) - 1:-1], rest[-1]
    taken, depth = row_refs[0].shape
    step = pl.program_id(0)

    @pl.when(step == 0)
    def _():
        for by in range(chips):
            gathered[by] = row_refs[by][...]

    def multiply(weight_ref):
        product = lax.dot_general(
            gathered[...].reshape(chips * taken, depth), weight_ref[...], (((1,), (1,)), ((), ())),
            preferred_element_type=jnp.float32,
        ).astype(jnp.bfloat16)
        for part, (start, end) in enumerate(zip(cuts, cuts[1:])):
            for by in range(chips):
                out_refs[part * chips + by][...] = product[by * taken + start:by * taken + end]

    @pl.when(step < steps)
    def _():
        multiply(own_ref)

    @pl.when(step >= steps)
    def _():
        multiply(other_ref)


def project(rows, own, other, cuts, after):
    chips = len(rows)
    taken, depth = rows[0].shape
    width = own.shape[0]
    block = min(width, 512)
    steps = width // block
    counts = [end - start for start, end in zip(cuts, cuts[1:]) for by in range(chips)]
    results = list(call(
        functools.partial(project_kernel, chips, steps, cuts), "project",
        4 * chips * taken * depth * width, 2 * (chips * taken * (depth + 2 * width) + 2 * width * depth),
        grid=(CORES * steps,),
        in_specs=[
            pl.BlockSpec((block, depth), lambda i: (jnp.minimum(i, steps - 1), 0)),
            pl.BlockSpec((block, depth), lambda i: (jnp.maximum(i - steps, 0), 0)),
        ] + [pl.BlockSpec((taken, depth), lambda i: (0, 0))] * chips + [whole] * len(after),
        out_specs=[pl.BlockSpec((count, block), lambda i: (0, i)) for count in counts],
        out_shape=[jax.ShapeDtypeStruct((count, CORES * width), jnp.bfloat16) for count in counts],
        scratch_shapes=[pltpu.VMEM((chips, taken, depth), jnp.bfloat16)],
    )(own, other, *rows, *after))
    return [results[at:at + chips] for at in range(0, len(results), chips)]


def backward_kernel(chips, place_ref, x_ref, gain_ref, grad_ref, *rest):
    cot_refs, out_ref = rest[:chips], rest[-1]
    chip, core = place_ref[0], place_ref[1]
    values = x_ref[...].astype(jnp.float32)
    width = cot_refs[0].shape[1] // CORES
    inverse = lax.rsqrt(jnp.mean(values * values, axis=-1, keepdims=True) + norm_eps)
    inner = jnp.zeros_like(inverse)

    def parts():
        for by, cot_ref in enumerate(cot_refs):
            source = lax.rem(chip + chips - by, chips)
            for half in range(CORES):
                cols = part_columns(source, half, core, width)
                cot = cot_ref[:, half * width:(half + 1) * width].astype(jnp.float32)
                yield cols, gain_ref[:, cols].astype(jnp.float32) * cot

    for cols, scaled in parts():
        inner += jnp.sum(x_ref[:, cols].astype(jnp.float32) * scaled, axis=-1, keepdims=True)
    factor = inverse * inverse * inverse * (inner / x_ref.shape[1])
    for cols, scaled in parts():
        out_ref[:, cols] = (
            grad_ref[:, cols].astype(jnp.float32)
            + inverse * scaled
            - x_ref[:, cols].astype(jnp.float32) * factor
        ).astype(out_ref.dtype)


def norm_backward(place, cots, rows, gain, grads, start, after):
    tokens, width = rows.shape
    taken, part_width = cots[0].shape
    block = math.gcd(math.gcd(start, taken), 32)
    first = start // block
    return call(
        functools.partial(backward_kernel, len(cots)), "norm_backward",
        10 * taken * width, 8 * taken * width,
        grid=(taken // block,),
        in_specs=[
            scalars,
            pl.BlockSpec((block, width), lambda i: (first + i, 0)),
            pl.BlockSpec((1, width), lambda i: (0, 0)),
            pl.BlockSpec((block, width), lambda i: (first + i, 0)),
        ] + [pl.BlockSpec((block, part_width), lambda i: (i, 0))] * len(cots) + [whole] * len(after),
        out_specs=pl.BlockSpec((block, width), lambda i: (i, 0)),
        out_shape=jax.ShapeDtypeStruct((taken, width), jnp.bfloat16),
    )(place, rows, gain, grads, *cots, *after)


def outer_kernel(groups, sums, halves, *refs):
    arrays = sum(groups)
    cots, columns, terms = refs[:arrays], refs[arrays:2 * arrays], refs[2 * arrays:2 * arrays + sums]
    total, at = None, 0
    for size in groups:
        column, cot = columns[at][...], cots[at][...]
        for more in range(at + 1, at + size):
            column, cot = column + columns[more][...], cot + cots[more][...]
        at += size
        product = lax.dot_general(
            column, cot, (((0,), (0,)), ((), ())), preferred_element_type=jnp.float32
        )
        total = product if total is None else total + product
    for term in terms:
        total += term[...].astype(jnp.float32)
    if halves:
        lower, upper = refs[2 * arrays + sums:2 * arrays + sums + 2]
        in_lower = pl.program_id(0) < pl.num_programs(0) // 2
        total += jnp.where(in_lower, lower[...], upper[...]).astype(jnp.float32)
    refs[-1][...] = total.astype(refs[-1].dtype)


def outer(groups, cot_width, half, before, dtype, part=0, parts=1, halves=(), after=()):
    payloads = [payload for group in groups for payload in group]
    wide = payloads[0].shape[1]
    width = (wide - cot_width) // CORES
    block = math.gcd(math.gcd(width // 2, 256), cot_width)
    steps = width // parts // block
    skip = part * steps
    first = (cot_width + half * width) // block + skip
    middle = steps // 2
    tokens = sum(payload.shape[0] for payload in payloads)
    return call(
        functools.partial(outer_kernel, [len(group) for group in groups], len(before), len(halves)), "outer",
        2 * tokens * width * cot_width, 2 * tokens * width + 4 * width * cot_width,
        grid=(steps,),
        in_specs=[pl.BlockSpec((payload.shape[0], cot_width), lambda i: (0, 0)) for payload in payloads]
        + [pl.BlockSpec((payload.shape[0], block), lambda i: (0, first + i)) for payload in payloads]
        + [pl.BlockSpec((block, cot_width), lambda i: (skip + i, 0)) for term in before]
        + [
            pl.BlockSpec((block, cot_width), lambda i: (jnp.minimum(i, middle - 1), 0)),
            pl.BlockSpec((block, cot_width), lambda i: (jnp.maximum(i - middle, 0), 0)),
        ][:len(halves)]
        + [whole] * len(after),
        out_specs=pl.BlockSpec((block, cot_width), lambda i: (i, 0)),
        out_shape=jax.ShapeDtypeStruct((width // parts, cot_width), dtype),
    )(*payloads, *payloads, *before, *halves, *after)


def shards(
    new_input,
    new_gain,
    queries,
    new_keys,
    context_grad,
    segment_ids,
    frozen_input,
    frozen_gain,
    output_grad,
    kv_grad,
    kv_weight,
):
    chips = lax.axis_size("dp") // CORES
    sections = lax.axis_size("pipe")
    tokens, kv_width = new_keys.shape[1:]
    at = lax.axis_index("dp")
    place = jnp.stack([at // CORES, at % CORES]).astype(jnp.int32)
    middle = chips // 2
    near = [by for by in range(1, chips) if by != middle]
    spread = tokens // 4

    rows = [kv_grad[0]] + [along_chips(kv_grad[0], chips - by, 1) for by in range(1, chips)]
    other_weight = swap_cores(kv_weight[0])
    value_cot = attend(queries[0], new_keys[0], context_grad[0], segment_ids)

    apply = functools.partial(normalize, place, new_input[0], new_gain, value_cot, chips)
    shared = apply([middle], 0, spread, [other_weight])[0]
    brought = [between_lines(shared, section, 0) for section in range(1, sections)]
    early = apply([0] + near[:1], 0, tokens, rows[1:])
    columns = [early[0]] + [along_chips(block, by) for block, by in zip(early[1:], near)]
    joint = stack_rows([shared] + brought, early[:1])
    moved = on_line(joint, middle, 0)
    returned = [moved[:spread]] + [
        between_lines(moved[section * spread:(section + 1) * spread], 0, section) for section in range(1, sections)
    ]

    cuts = [0, tokens * 5 // 8, tokens]
    parts = project(rows, kv_weight[0], other_weight, cuts, [joint])
    arrived = [
        [part[0]] + [along_chips(part[by], by, 1) for by in range(1, chips)] for part in parts
    ]
    backward = functools.partial(norm_backward, place, rows=frozen_input[0], gain=frozen_gain, grads=output_grad[0])
    above = backward(arrived[0], start=cuts[0], after=columns[1:])
    kept = apply([middle], spread, tokens - spread, [above] + [arrived[1][by] for by in near])
    late = apply(near[1:], 0, tokens, kept)
    above = [above, backward(arrived[1], start=cuts[1], after=late[:1])]
    below = [from_behind(half, "pipe", -1) for half in above]
    cot_below = stack_rows(below, [])

    groups = [[column] for column in columns] + [returned]
    last = [[along_chips(block, by)] for block, by in zip(late + kept, near[1:] + [middle])]
    sums = [outer(groups, kv_width, half, [], jnp.float32, after=above[1:]) for half in range(CORES)]
    given = [
        outer(last, kv_width, 1, sums[1:], jnp.bfloat16, part, 2, after=sums[:1]) for part in range(2)
    ]
    taken = [swap_cores(part) for part in given]
    grad = outer(last, kv_width, 0, sums[:1], jnp.float32, halves=taken, after=[cot_below])
    return (cot_below[None], grad[None])


def solution(mesh):
    placed = (
        P("pipe", "dp", None),
        P("pipe", None),
        P("pipe", "dp", None),
        P("pipe", "dp", None),
        P("pipe", "dp", None),
        P("pipe", "dp"),
        P("pipe", "dp", None),
        P("pipe", None),
        P("pipe", "dp", None),
        P("pipe", "dp", None),
        P("pipe", "dp", None),
    )
    return jax.shard_map(
        shards,
        mesh=mesh,
        in_specs=placed,
        out_specs=(P("pipe", "dp", None), P("pipe", "dp", None)),
        check_vma=False,
    )
```

```python
import functools
import math

import jax
import jax.numpy as jnp
from jax import lax
from jax.experimental import pallas as pl
from jax.experimental.pallas import tpu as pltpu
from jax.sharding import PartitionSpec as P

HEAD = 128
CORES = 2
MIB = 1 << 20

norm_eps = 1e-05
masked_value = -1e30

whole = pl.BlockSpec(memory_space=pl.ANY)
scalars = pl.BlockSpec(memory_space=pltpu.SMEM)


def from_behind(array, axis, by):
    length = lax.axis_size(axis)
    pairs = [(i, i + by) for i in range(length) if 0 <= i + by < length]
    return lax.ppermute(array, axis, pairs)


def along_chips(array, by):
    length = lax.axis_size("dp")
    return lax.ppermute(array, "dp", [(i, (i + by * CORES) % length) for i in range(length)])


def swap_cores(array):
    length = lax.axis_size("dp")
    return lax.ppermute(array, "dp", [(i, i ^ 1) for i in range(length)])


def call(body, name, flops, nbytes, vmem=24, **kwargs):
    return pl.pallas_call(
        body,
        name=name,
        compiler_params=pltpu.CompilerParams(vmem_limit_bytes=vmem * MIB),
        cost_estimate=pl.CostEstimate(flops=flops, bytes_accessed=nbytes, transcendentals=0),
        **kwargs,
    )


def part_columns(chip, half, core, width):
    owner = chip * CORES + (core if half == 0 else CORES - 1 - core)
    return pl.ds(pl.multiple_of(owner * width, width), width)


def norm_kernel(chips, ahead, place_ref, x_ref, gain_ref, cot_ref, *rest):
    out_refs = rest[-len(ahead):]
    chip, core = place_ref[0], place_ref[1]
    values = x_ref[...].astype(jnp.float32)
    inverse = lax.rsqrt(jnp.mean(values * values, axis=-1, keepdims=True) + norm_eps)
    front = cot_ref.shape[1]
    width = (out_refs[0].shape[1] - front) // CORES
    for by, out_ref in zip(ahead, out_refs):
        to = lax.rem(chip + by, chips)
        out_ref[:, :front] = cot_ref[...]
        for half in range(CORES):
            cols = part_columns(to, half, core, width)
            out_ref[:, front + half * width:front + (half + 1) * width] = (
                x_ref[:, cols].astype(jnp.float32) * inverse * gain_ref[:, cols].astype(jnp.float32)
            ).astype(out_ref.dtype)


def normalize(place, rows, gain, cot, chips, ahead, start, count, after):
    width = rows.shape[1]
    front = cot.shape[1]
    block = math.gcd(math.gcd(start, count), 32)
    first = start // block
    out_width = front + width // chips
    return list(call(
        functools.partial(norm_kernel, chips, ahead), "norm_forward",
        4 * count * width, 2 * count * width + 2 * count * out_width * len(ahead),
        grid=(count // block,),
        in_specs=[
            scalars,
            pl.BlockSpec((block, width), lambda i: (first + i, 0)),
            pl.BlockSpec((1, width), lambda i: (0, 0)),
            pl.BlockSpec((block, front), lambda i: (first + i, 0)),
        ] + [whole] * len(after),
        out_specs=[pl.BlockSpec((block, out_width), lambda i: (i, 0))] * len(ahead),
        out_shape=[jax.ShapeDtypeStruct((count, out_width), jnp.bfloat16)] * len(ahead),
    )(place, rows, gain, cot, *after))


def stack_kernel(count, *refs):
    at = 0
    for ref in refs[:count]:
        refs[-1][at:at + ref.shape[0]] = ref[...]
        at += ref.shape[0]


def stack_rows(arrays, after):
    width = arrays[0].shape[1]
    tall = sum(array.shape[0] for array in arrays)
    return call(
        functools.partial(stack_kernel, len(arrays)), "stack_rows", 0, 4 * tall * width,
        grid=(1,),
        in_specs=[pl.BlockSpec(array.shape, lambda i: (0, 0)) for array in arrays] + [whole] * len(after),
        out_specs=pl.BlockSpec((tall, width), lambda i: (0, 0)),
        out_shape=jax.ShapeDtypeStruct((tall, width), arrays[0].dtype),
    )(*arrays, *after)


def attend_kernel(query_ref, key_ref, grad_ref, row_seg_ref, col_seg_ref, out_ref):
    tokens = key_ref.shape[0]
    group = query_ref.shape[1] // HEAD
    at_query = lax.broadcasted_iota(jnp.int32, (tokens, tokens), 0)
    at_key = lax.broadcasted_iota(jnp.int32, (tokens, tokens), 1)
    visible = (col_seg_ref[...] == row_seg_ref[...]) & (at_key <= at_query)
    keys = key_ref[...]
    total = jnp.zeros((tokens, HEAD), jnp.float32)
    for head in range(group):
        cols = slice(head * HEAD, (head + 1) * HEAD)
        scores = lax.dot_general(
            query_ref[:, cols], keys, (((1,), (1,)), ((), ())),
            preferred_element_type=jnp.float32,
        ) / math.sqrt(HEAD)
        masked = jnp.where(visible, scores, masked_value)
        highest = jnp.max(masked, axis=-1, keepdims=True)
        weights = jnp.where(visible, jnp.exp(masked - highest), 0.0)
        attention = (weights / jnp.sum(weights, axis=-1, keepdims=True)).astype(jnp.bfloat16)
        total += lax.dot_general(
            attention, grad_ref[:, cols], (((0,), (0,)), ((), ())),
            preferred_element_type=jnp.float32,
        )
    out_ref[...] = total.astype(out_ref.dtype)


def attend(queries, keys, grads, segments):
    tokens, kv_width = keys.shape
    heads = kv_width // HEAD
    wide = queries.shape[1] // heads
    return call(
        attend_kernel, "attend",
        4 * tokens * tokens * queries.shape[1], 4 * tokens * queries.shape[1],
        grid=(heads,),
        in_specs=[
            pl.BlockSpec((tokens, wide), lambda i: (0, i)),
            pl.BlockSpec((tokens, HEAD), lambda i: (0, i)),
            pl.BlockSpec((tokens, wide), lambda i: (0, i)),
            pl.BlockSpec((1, tokens), lambda i: (0, 0)),
            pl.BlockSpec((tokens, 1), lambda i: (0, 0)),
        ],
        out_specs=pl.BlockSpec((tokens, HEAD), lambda i: (0, i)),
        out_shape=jax.ShapeDtypeStruct((tokens, kv_width), jnp.bfloat16),
    )(queries, keys, grads, segments, segments.reshape(tokens, 1))


def project_kernel(chips, steps, cuts, own_ref, other_ref, *rest):
    row_refs, out_refs, gathered = rest[:chips], rest[-chips * (len(cuts) - 1) - 1:-1], rest[-1]
    taken, depth = row_refs[0].shape
    step = pl.program_id(0)

    @pl.when(step == 0)
    def _():
        for by in range(chips):
            gathered[by] = row_refs[by][...]

    def multiply(weight_ref):
        product = lax.dot_general(
            gathered[...].reshape(chips * taken, depth), weight_ref[...], (((1,), (1,)), ((), ())),
            preferred_element_type=jnp.float32,
        ).astype(jnp.bfloat16)
        for part, (start, end) in enumerate(zip(cuts, cuts[1:])):
            for by in range(chips):
                out_refs[part * chips + by][...] = product[by * taken + start:by * taken + end]

    @pl.when(step < steps)
    def _():
        multiply(own_ref)

    @pl.when(step >= steps)
    def _():
        multiply(other_ref)


def project(rows, own, other, cuts, after):
    chips = len(rows)
    taken, depth = rows[0].shape
    width = own.shape[0]
    block = min(width, 512)
    steps = width // block
    counts = [end - start for start, end in zip(cuts, cuts[1:]) for by in range(chips)]
    results = list(call(
        functools.partial(project_kernel, chips, steps, cuts), "project",
        4 * chips * taken * depth * width, 2 * (chips * taken * (depth + 2 * width) + 2 * width * depth),
        grid=(CORES * steps,),
        in_specs=[
            pl.BlockSpec((block, depth), lambda i: (jnp.minimum(i, steps - 1), 0)),
            pl.BlockSpec((block, depth), lambda i: (jnp.maximum(i - steps, 0), 0)),
        ] + [pl.BlockSpec((taken, depth), lambda i: (0, 0))] * chips + [whole] * len(after),
        out_specs=[pl.BlockSpec((count, block), lambda i: (0, i)) for count in counts],
        out_shape=[jax.ShapeDtypeStruct((count, CORES * width), jnp.bfloat16) for count in counts],
        scratch_shapes=[pltpu.VMEM((chips, taken, depth), jnp.bfloat16)],
    )(own, other, *rows, *after))
    return [results[at:at + chips] for at in range(0, len(results), chips)]


def backward_kernel(chips, place_ref, x_ref, gain_ref, grad_ref, *rest):
    cot_refs, out_ref = rest[:chips], rest[-1]
    chip, core = place_ref[0], place_ref[1]
    values = x_ref[...].astype(jnp.float32)
    width = cot_refs[0].shape[1] // CORES
    inverse = lax.rsqrt(jnp.mean(values * values, axis=-1, keepdims=True) + norm_eps)
    inner = jnp.zeros_like(inverse)

    def parts():
        for by, cot_ref in enumerate(cot_refs):
            source = lax.rem(chip + chips - by, chips)
            for half in range(CORES):
                cols = part_columns(source, half, core, width)
                cot = cot_ref[:, half * width:(half + 1) * width].astype(jnp.float32)
                yield cols, gain_ref[:, cols].astype(jnp.float32) * cot

    for cols, scaled in parts():
        inner += jnp.sum(x_ref[:, cols].astype(jnp.float32) * scaled, axis=-1, keepdims=True)
    factor = inverse * inverse * inverse * (inner / x_ref.shape[1])
    for cols, scaled in parts():
        out_ref[:, cols] = (
            grad_ref[:, cols].astype(jnp.float32)
            + inverse * scaled
            - x_ref[:, cols].astype(jnp.float32) * factor
        ).astype(out_ref.dtype)


def norm_backward(place, cots, rows, gain, grads, start, after):
    tokens, width = rows.shape
    taken, part_width = cots[0].shape
    block = math.gcd(math.gcd(start, taken), 32)
    first = start // block
    return call(
        functools.partial(backward_kernel, len(cots)), "norm_backward",
        10 * taken * width, 8 * taken * width,
        grid=(taken // block,),
        in_specs=[
            scalars,
            pl.BlockSpec((block, width), lambda i: (first + i, 0)),
            pl.BlockSpec((1, width), lambda i: (0, 0)),
            pl.BlockSpec((block, width), lambda i: (first + i, 0)),
        ] + [pl.BlockSpec((block, part_width), lambda i: (i, 0))] * len(cots) + [whole] * len(after),
        out_specs=pl.BlockSpec((block, width), lambda i: (i, 0)),
        out_shape=jax.ShapeDtypeStruct((taken, width), jnp.bfloat16),
    )(place, rows, gain, grads, *cots, *after)


def outer_kernel(groups, sums, halves, *refs):
    arrays = sum(groups)
    cots, columns, terms = refs[:arrays], refs[arrays:2 * arrays], refs[2 * arrays:2 * arrays + sums]
    total, at = None, 0
    for size in groups:
        column, cot = columns[at][...], cots[at][...]
        for more in range(at + 1, at + size):
            column, cot = column + columns[more][...], cot + cots[more][...]
        at += size
        product = lax.dot_general(
            column, cot, (((0,), (0,)), ((), ())), preferred_element_type=jnp.float32
        )
        total = product if total is None else total + product
    for term in terms:
        total += term[...].astype(jnp.float32)
    if halves:
        lower, upper = refs[2 * arrays + sums:2 * arrays + sums + 2]
        in_lower = pl.program_id(0) < pl.num_programs(0) // 2
        total += jnp.where(in_lower, lower[...], upper[...]).astype(jnp.float32)
    refs[-1][...] = total.astype(refs[-1].dtype)


def outer(groups, cot_width, half, before, dtype, part=0, parts=1, halves=(), after=()):
    payloads = [payload for group in groups for payload in group]
    wide = payloads[0].shape[1]
    width = (wide - cot_width) // CORES
    block = math.gcd(math.gcd(width // 2, 256), cot_width)
    steps = width // parts // block
    skip = part * steps
    first = (cot_width + half * width) // block + skip
    middle = steps // 2
    tokens = sum(payload.shape[0] for payload in payloads)
    return call(
        functools.partial(outer_kernel, [len(group) for group in groups], len(before), len(halves)), "outer",
        2 * tokens * width * cot_width, 2 * tokens * width + 4 * width * cot_width,
        grid=(steps,),
        in_specs=[pl.BlockSpec((payload.shape[0], cot_width), lambda i: (0, 0)) for payload in payloads]
        + [pl.BlockSpec((payload.shape[0], block), lambda i: (0, first + i)) for payload in payloads]
        + [pl.BlockSpec((block, cot_width), lambda i: (skip + i, 0)) for term in before]
        + [
            pl.BlockSpec((block, cot_width), lambda i: (jnp.minimum(i, middle - 1), 0)),
            pl.BlockSpec((block, cot_width), lambda i: (jnp.maximum(i - middle, 0), 0)),
        ][:len(halves)]
        + [whole] * len(after),
        out_specs=pl.BlockSpec((block, cot_width), lambda i: (i, 0)),
        out_shape=jax.ShapeDtypeStruct((width // parts, cot_width), dtype),
    )(*payloads, *payloads, *before, *halves, *after)


def shards(
    new_input,
    new_gain,
    queries,
    new_keys,
    context_grad,
    segment_ids,
    frozen_input,
    frozen_gain,
    output_grad,
    kv_grad,
    kv_weight,
):
    chips = lax.axis_size("dp") // CORES
    tokens, kv_width = new_keys.shape[1:]
    at = lax.axis_index("dp")
    place = jnp.stack([at // CORES, at % CORES]).astype(jnp.int32)
    middle = chips // 2
    near = [by for by in range(1, chips) if by != middle]

    rows = [kv_grad[0]] + [along_chips(kv_grad[0], chips - by) for by in range(1, chips)]
    other_weight = swap_cores(kv_weight[0])
    value_cot = attend(queries[0], new_keys[0], context_grad[0], segment_ids)

    apply = functools.partial(normalize, place, new_input[0], new_gain, value_cot, chips)
    early = apply([0] + near[:1], 0, tokens, rows[1:])
    columns = [early[0]] + [along_chips(block, by) for block, by in zip(early[1:], near)]

    cuts = [0, tokens * 5 // 8, tokens]
    parts = project(rows, kv_weight[0], other_weight, cuts, early[:1])
    arrived = [[part[0]] + [along_chips(part[by], by) for by in range(1, chips)] for part in parts]
    backward = functools.partial(norm_backward, place, rows=frozen_input[0], gain=frozen_gain, grads=output_grad[0])
    above = backward(arrived[0], start=cuts[0], after=columns[1:])
    late = apply(near[1:] + [middle], 0, tokens, [above] + arrived[1][1:])
    above = [above, backward(arrived[1], start=cuts[1], after=late[:1])]
    below = [from_behind(half, "pipe", -1) for half in above]
    cot_below = stack_rows(below, [])

    last = [[along_chips(block, by)] for block, by in zip(late, near[1:] + [middle])]
    groups = [[column] for column in columns]
    sums = [outer(groups, kv_width, half, [], jnp.float32, after=above[1:]) for half in range(CORES)]
    given = [
        outer(last, kv_width, 1, sums[1:], jnp.bfloat16, part, 2, after=sums[:1]) for part in range(2)
    ]
    taken = [swap_cores(part) for part in given]
    grad = outer(last, kv_width, 0, sums[:1], jnp.float32, halves=taken, after=[cot_below])
    return (cot_below[None], grad[None])


def solution(mesh):
    placed = (
        P("pipe", "dp", None),
        P("pipe", None),
        P("pipe", "dp", None),
        P("pipe", "dp", None),
        P("pipe", "dp", None),
        P("pipe", "dp"),
        P("pipe", "dp", None),
        P("pipe", None),
        P("pipe", "dp", None),
        P("pipe", "dp", None),
        P("pipe", "dp", None),
    )
    return jax.shard_map(
        shards,
        mesh=mesh,
        in_specs=placed,
        out_specs=(P("pipe", "dp", None), P("pipe", "dp", None)),
        check_vma=False,
    )
```

```python
import functools
import math

import jax
import jax.numpy as jnp
from jax import lax
from jax.experimental import pallas as pl
from jax.experimental.pallas import tpu as pltpu
from jax.sharding import PartitionSpec as P

HEAD = 128
CORES = 2
MIB = 1 << 20

norm_eps = 1e-05
masked_value = -1e30

whole = pl.BlockSpec(memory_space=pl.ANY)
scalars = pl.BlockSpec(memory_space=pltpu.SMEM)


def from_behind(array, axis, by):
    length = lax.axis_size(axis)
    pairs = [(i, i + by) for i in range(length) if 0 <= i + by < length]
    return lax.ppermute(array, axis, pairs)


def along_chips(array, by, first=0):
    length = lax.axis_size("dp")
    pairs = [
        (line * length + i, line * length + ((i + by * CORES) % length if line >= first else i ^ 1))
        for line in range(lax.axis_size("pipe")) for i in range(length)
    ]
    return lax.ppermute(array, ("pipe", "dp"), pairs)


def between_lines(array, source, target):
    length = lax.axis_size("dp")
    pairs = [(source * length + i, target * length + i) for i in range(length)]
    return lax.ppermute(array, ("pipe", "dp"), pairs)


def on_line(array, by, line):
    length = lax.axis_size("dp")
    pairs = [(line * length + i, line * length + (i + by * CORES) % length) for i in range(length)]
    return lax.ppermute(array, ("pipe", "dp"), pairs)


def swap_cores(array):
    length = lax.axis_size("dp")
    return lax.ppermute(array, "dp", [(i, i ^ 1) for i in range(length)])


def call(body, name, flops, nbytes, vmem=24, **kwargs):
    return pl.pallas_call(
        body,
        name=name,
        compiler_params=pltpu.CompilerParams(vmem_limit_bytes=vmem * MIB),
        cost_estimate=pl.CostEstimate(flops=flops, bytes_accessed=nbytes, transcendentals=0),
        **kwargs,
    )


def part_columns(chip, half, core, width):
    owner = chip * CORES + (core if half == 0 else CORES - 1 - core)
    return pl.ds(pl.multiple_of(owner * width, width), width)


def norm_kernel(chips, ahead, place_ref, x_ref, gain_ref, cot_ref, *rest):
    out_refs = rest[-len(ahead):]
    chip, core = place_ref[0], place_ref[1]
    values = x_ref[...].astype(jnp.float32)
    inverse = lax.rsqrt(jnp.mean(values * values, axis=-1, keepdims=True) + norm_eps)
    front = cot_ref.shape[1]
    width = (out_refs[0].shape[1] - front) // CORES
    for by, out_ref in zip(ahead, out_refs):
        to = lax.rem(chip + by, chips)
        out_ref[:, :front] = cot_ref[...]
        for half in range(CORES):
            cols = part_columns(to, half, core, width)
            out_ref[:, front + half * width:front + (half + 1) * width] = (
                x_ref[:, cols].astype(jnp.float32) * inverse * gain_ref[:, cols].astype(jnp.float32)
            ).astype(out_ref.dtype)


def normalize(place, rows, gain, cot, chips, ahead, start, count, after):
    width = rows.shape[1]
    front = cot.shape[1]
    block = math.gcd(math.gcd(start, count), 32)
    first = start // block
    out_width = front + width // chips
    return list(call(
        functools.partial(norm_kernel, chips, ahead), "norm_forward",
        4 * count * width, 2 * count * width + 2 * count * out_width * len(ahead),
        grid=(count // block,),
        in_specs=[
            scalars,
            pl.BlockSpec((block, width), lambda i: (first + i, 0)),
            pl.BlockSpec((1, width), lambda i: (0, 0)),
            pl.BlockSpec((block, front), lambda i: (first + i, 0)),
        ] + [whole] * len(after),
        out_specs=[pl.BlockSpec((block, out_width), lambda i: (i, 0))] * len(ahead),
        out_shape=[jax.ShapeDtypeStruct((count, out_width), jnp.bfloat16)] * len(ahead),
    )(place, rows, gain, cot, *after))


def stack_kernel(count, *refs):
    at = 0
    for ref in refs[:count]:
        refs[-1][at:at + ref.shape[0]] = ref[...]
        at += ref.shape[0]


def stack_rows(arrays, after):
    width = arrays[0].shape[1]
    tall = sum(array.shape[0] for array in arrays)
    return call(
        functools.partial(stack_kernel, len(arrays)), "stack_rows", 0, 4 * tall * width,
        grid=(1,),
        in_specs=[pl.BlockSpec(array.shape, lambda i: (0, 0)) for array in arrays] + [whole] * len(after),
        out_specs=pl.BlockSpec((tall, width), lambda i: (0, 0)),
        out_shape=jax.ShapeDtypeStruct((tall, width), arrays[0].dtype),
    )(*arrays, *after)


def attend_kernel(query_ref, key_ref, grad_ref, row_seg_ref, col_seg_ref, out_ref):
    tokens = key_ref.shape[0]
    group = query_ref.shape[1] // HEAD
    at_query = lax.broadcasted_iota(jnp.int32, (tokens, tokens), 0)
    at_key = lax.broadcasted_iota(jnp.int32, (tokens, tokens), 1)
    visible = (col_seg_ref[...] == row_seg_ref[...]) & (at_key <= at_query)
    keys = key_ref[...]
    total = jnp.zeros((tokens, HEAD), jnp.float32)
    for head in range(group):
        cols = slice(head * HEAD, (head + 1) * HEAD)
        scores = lax.dot_general(
            query_ref[:, cols], keys, (((1,), (1,)), ((), ())),
            preferred_element_type=jnp.float32,
        ) / math.sqrt(HEAD)
        masked = jnp.where(visible, scores, masked_value)
        highest = jnp.max(masked, axis=-1, keepdims=True)
        weights = jnp.where(visible, jnp.exp(masked - highest), 0.0)
        attention = (weights / jnp.sum(weights, axis=-1, keepdims=True)).astype(jnp.bfloat16)
        total += lax.dot_general(
            attention, grad_ref[:, cols], (((0,), (0,)), ((), ())),
            preferred_element_type=jnp.float32,
        )
    out_ref[...] = total.astype(out_ref.dtype)


def attend(queries, keys, grads, segments):
    tokens, kv_width = keys.shape
    heads = kv_width // HEAD
    wide = queries.shape[1] // heads
    return call(
        attend_kernel, "attend",
        4 * tokens * tokens * queries.shape[1], 4 * tokens * queries.shape[1],
        grid=(heads,),
        in_specs=[
            pl.BlockSpec((tokens, wide), lambda i: (0, i)),
            pl.BlockSpec((tokens, HEAD), lambda i: (0, i)),
            pl.BlockSpec((tokens, wide), lambda i: (0, i)),
            pl.BlockSpec((1, tokens), lambda i: (0, 0)),
            pl.BlockSpec((tokens, 1), lambda i: (0, 0)),
        ],
        out_specs=pl.BlockSpec((tokens, HEAD), lambda i: (0, i)),
        out_shape=jax.ShapeDtypeStruct((tokens, kv_width), jnp.bfloat16),
    )(queries, keys, grads, segments, segments.reshape(tokens, 1))


def project_kernel(chips, steps, cuts, own_ref, other_ref, *rest):
    row_refs, out_refs, gathered = rest[:chips], rest[-chips * (len(cuts) - 1) - 1:-1], rest[-1]
    taken, depth = row_refs[0].shape
    step = pl.program_id(0)

    @pl.when(step == 0)
    def _():
        for by in range(chips):
            gathered[by] = row_refs[by][...]

    def multiply(weight_ref):
        product = lax.dot_general(
            gathered[...].reshape(chips * taken, depth), weight_ref[...], (((1,), (1,)), ((), ())),
            preferred_element_type=jnp.float32,
        ).astype(jnp.bfloat16)
        for part, (start, end) in enumerate(zip(cuts, cuts[1:])):
            for by in range(chips):
                out_refs[part * chips + by][...] = product[by * taken + start:by * taken + end]

    @pl.when(step < steps)
    def _():
        multiply(own_ref)

    @pl.when(step >= steps)
    def _():
        multiply(other_ref)


def project(rows, own, other, cuts, after):
    chips = len(rows)
    taken, depth = rows[0].shape
    width = own.shape[0]
    block = min(width, 512)
    steps = width // block
    counts = [end - start for start, end in zip(cuts, cuts[1:]) for by in range(chips)]
    results = list(call(
        functools.partial(project_kernel, chips, steps, cuts), "project",
        4 * chips * taken * depth * width, 2 * (chips * taken * (depth + 2 * width) + 2 * width * depth),
        grid=(CORES * steps,),
        in_specs=[
            pl.BlockSpec((block, depth), lambda i: (jnp.minimum(i, steps - 1), 0)),
            pl.BlockSpec((block, depth), lambda i: (jnp.maximum(i - steps, 0), 0)),
        ] + [pl.BlockSpec((taken, depth), lambda i: (0, 0))] * chips + [whole] * len(after),
        out_specs=[pl.BlockSpec((count, block), lambda i: (0, i)) for count in counts],
        out_shape=[jax.ShapeDtypeStruct((count, CORES * width), jnp.bfloat16) for count in counts],
        scratch_shapes=[pltpu.VMEM((chips, taken, depth), jnp.bfloat16)],
    )(own, other, *rows, *after))
    return [results[at:at + chips] for at in range(0, len(results), chips)]


def backward_kernel(chips, place_ref, x_ref, gain_ref, grad_ref, *rest):
    cot_refs, out_ref = rest[:chips], rest[-1]
    chip, core = place_ref[0], place_ref[1]
    values = x_ref[...].astype(jnp.float32)
    width = cot_refs[0].shape[1] // CORES
    inverse = lax.rsqrt(jnp.mean(values * values, axis=-1, keepdims=True) + norm_eps)
    inner = jnp.zeros_like(inverse)

    def parts():
        for by, cot_ref in enumerate(cot_refs):
            source = lax.rem(chip + chips - by, chips)
            for half in range(CORES):
                cols = part_columns(source, half, core, width)
                cot = cot_ref[:, half * width:(half + 1) * width].astype(jnp.float32)
                yield cols, gain_ref[:, cols].astype(jnp.float32) * cot

    for cols, scaled in parts():
        inner += jnp.sum(x_ref[:, cols].astype(jnp.float32) * scaled, axis=-1, keepdims=True)
    factor = inverse * inverse * inverse * (inner / x_ref.shape[1])
    for cols, scaled in parts():
        out_ref[:, cols] = (
            grad_ref[:, cols].astype(jnp.float32)
            + inverse * scaled
            - x_ref[:, cols].astype(jnp.float32) * factor
        ).astype(out_ref.dtype)


def norm_backward(place, cots, rows, gain, grads, start, after):
    tokens, width = rows.shape
    taken, part_width = cots[0].shape
    block = math.gcd(math.gcd(start, taken), 32)
    first = start // block
    return call(
        functools.partial(backward_kernel, len(cots)), "norm_backward",
        10 * taken * width, 8 * taken * width,
        grid=(taken // block,),
        in_specs=[
            scalars,
            pl.BlockSpec((block, width), lambda i: (first + i, 0)),
            pl.BlockSpec((1, width), lambda i: (0, 0)),
            pl.BlockSpec((block, width), lambda i: (first + i, 0)),
        ] + [pl.BlockSpec((block, part_width), lambda i: (i, 0))] * len(cots) + [whole] * len(after),
        out_specs=pl.BlockSpec((block, width), lambda i: (i, 0)),
        out_shape=jax.ShapeDtypeStruct((taken, width), jnp.bfloat16),
    )(place, rows, gain, grads, *cots, *after)


def outer_kernel(groups, sums, halves, *refs):
    arrays = sum(groups)
    cots, columns, terms = refs[:arrays], refs[arrays:2 * arrays], refs[2 * arrays:2 * arrays + sums]
    total, at = None, 0
    for size in groups:
        column, cot = columns[at][...], cots[at][...]
        for more in range(at + 1, at + size):
            column, cot = column + columns[more][...], cot + cots[more][...]
        at += size
        product = lax.dot_general(
            column, cot, (((0,), (0,)), ((), ())), preferred_element_type=jnp.float32
        )
        total = product if total is None else total + product
    for term in terms:
        total += term[...].astype(jnp.float32)
    if halves:
        lower, upper = refs[2 * arrays + sums:2 * arrays + sums + 2]
        in_lower = pl.program_id(0) < pl.num_programs(0) // 2
        total += jnp.where(in_lower, lower[...], upper[...]).astype(jnp.float32)
    refs[-1][...] = total.astype(refs[-1].dtype)


def outer(groups, cot_width, half, before, dtype, part=0, parts=1, halves=(), after=()):
    payloads = [payload for group in groups for payload in group]
    wide = payloads[0].shape[1]
    width = (wide - cot_width) // CORES
    block = math.gcd(math.gcd(width // 2, 256), cot_width)
    steps = width // parts // block
    skip = part * steps
    first = (cot_width + half * width) // block + skip
    middle = steps // 2
    tokens = sum(payload.shape[0] for payload in payloads)
    return call(
        functools.partial(outer_kernel, [len(group) for group in groups], len(before), len(halves)), "outer",
        2 * tokens * width * cot_width, 2 * tokens * width + 4 * width * cot_width,
        grid=(steps,),
        in_specs=[pl.BlockSpec((payload.shape[0], cot_width), lambda i: (0, 0)) for payload in payloads]
        + [pl.BlockSpec((payload.shape[0], block), lambda i: (0, first + i)) for payload in payloads]
        + [pl.BlockSpec((block, cot_width), lambda i: (skip + i, 0)) for term in before]
        + [
            pl.BlockSpec((block, cot_width), lambda i: (jnp.minimum(i, middle - 1), 0)),
            pl.BlockSpec((block, cot_width), lambda i: (jnp.maximum(i - middle, 0), 0)),
        ][:len(halves)]
        + [whole] * len(after),
        out_specs=pl.BlockSpec((block, cot_width), lambda i: (i, 0)),
        out_shape=jax.ShapeDtypeStruct((width // parts, cot_width), dtype),
    )(*payloads, *payloads, *before, *halves, *after)


def shards(
    new_input,
    new_gain,
    queries,
    new_keys,
    context_grad,
    segment_ids,
    frozen_input,
    frozen_gain,
    output_grad,
    kv_grad,
    kv_weight,
):
    chips = lax.axis_size("dp") // CORES
    sections = lax.axis_size("pipe")
    tokens, kv_width = new_keys.shape[1:]
    at = lax.axis_index("dp")
    place = jnp.stack([at // CORES, at % CORES]).astype(jnp.int32)
    middle = chips // 2
    near = [by for by in range(1, chips) if by != middle]
    spread = tokens // 4

    rows = [kv_grad[0]] + [along_chips(kv_grad[0], chips - by, 1) for by in range(1, chips)]
    other_weight = swap_cores(kv_weight[0])
    value_cot = attend(queries[0], new_keys[0], context_grad[0], segment_ids)

    apply = functools.partial(normalize, place, new_input[0], new_gain, value_cot, chips)
    shared = apply([middle], 0, spread, [other_weight])[0]
    brought = [between_lines(shared, section, 0) for section in range(1, sections)]
    early = apply([0] + near[:1], 0, tokens, rows[1:])
    columns = [early[0]] + [along_chips(block, by) for block, by in zip(early[1:], near)]
    joint = stack_rows([shared] + brought, early[:1])
    moved = on_line(joint, middle, 0)
    returned = [moved[:spread]] + [
        between_lines(moved[section * spread:(section + 1) * spread], 0, section) for section in range(1, sections)
    ]

    cuts = [0, tokens * 5 // 8, tokens]
    parts = project(rows, kv_weight[0], other_weight, cuts, [joint])
    arrived = [
        [part[0]] + [along_chips(part[by], by, 1) for by in range(1, chips)] for part in parts
    ]
    backward = functools.partial(norm_backward, place, rows=frozen_input[0], gain=frozen_gain, grads=output_grad[0])
    above = backward(arrived[0], start=cuts[0], after=columns[1:])
    kept = apply([middle], spread, tokens - spread, [above] + [arrived[1][by] for by in near])
    late = apply(near[1:], 0, tokens, kept)
    above = [above, backward(arrived[1], start=cuts[1], after=late[:1])]
    below = [from_behind(half, "pipe", -1) for half in above]
    cot_below = stack_rows(below, [])

    groups = [[column] for column in columns] + [returned]
    last = [[along_chips(block, by)] for block, by in zip(late + kept, near[1:] + [middle])]
    sums = [outer(groups, kv_width, half, [], jnp.float32, after=above[1:]) for half in range(CORES)]
    given = [
        outer(last, kv_width, 1, sums[1:], jnp.bfloat16, part, 2, after=sums[:1]) for part in range(2)
    ]
    taken = [swap_cores(part) for part in given]
    grad = outer(last, kv_width, 0, sums[:1], jnp.float32, halves=taken)
    return (cot_below[None], grad[None])


def solution(mesh):
    placed = (
        P("pipe", "dp", None),
        P("pipe", None),
        P("pipe", "dp", None),
        P("pipe", "dp", None),
        P("pipe", "dp", None),
        P("pipe", "dp"),
        P("pipe", "dp", None),
        P("pipe", None),
        P("pipe", "dp", None),
        P("pipe", "dp", None),
        P("pipe", "dp", None),
    )
    return jax.shard_map(
        shards,
        mesh=mesh,
        in_specs=placed,
        out_specs=(P("pipe", "dp", None), P("pipe", "dp", None)),
        check_vma=False,
    )
```

```python
import functools
import math

import jax
import jax.numpy as jnp
from jax import lax
from jax.experimental import pallas as pl
from jax.experimental.pallas import tpu as pltpu
from jax.sharding import PartitionSpec as P

HEAD = 128
CORES = 2
MIB = 1 << 20

norm_eps = 1e-05
masked_value = -1e30

whole = pl.BlockSpec(memory_space=pl.ANY)
scalars = pl.BlockSpec(memory_space=pltpu.SMEM)


def from_behind(array, axis, by):
    length = lax.axis_size(axis)
    pairs = [(i, i + by) for i in range(length) if 0 <= i + by < length]
    return lax.ppermute(array, axis, pairs)


def along_chips(array, by, first=0):
    length = lax.axis_size("dp")
    pairs = [
        (line * length + i, line * length + ((i + by * CORES) % length if line >= first else i ^ 1))
        for line in range(lax.axis_size("pipe")) for i in range(length)
    ]
    return lax.ppermute(array, ("pipe", "dp"), pairs)


def between_lines(array, source, target):
    length = lax.axis_size("dp")
    pairs = [(source * length + i, target * length + i) for i in range(length)]
    return lax.ppermute(array, ("pipe", "dp"), pairs)


def on_line(array, by, line):
    length = lax.axis_size("dp")
    pairs = [(line * length + i, line * length + (i + by * CORES) % length) for i in range(length)]
    return lax.ppermute(array, ("pipe", "dp"), pairs)


def swap_cores(array):
    length = lax.axis_size("dp")
    return lax.ppermute(array, "dp", [(i, i ^ 1) for i in range(length)])


def call(body, name, flops, nbytes, vmem=24, **kwargs):
    return pl.pallas_call(
        body,
        name=name,
        compiler_params=pltpu.CompilerParams(vmem_limit_bytes=vmem * MIB),
        cost_estimate=pl.CostEstimate(flops=flops, bytes_accessed=nbytes, transcendentals=0),
        **kwargs,
    )


def part_columns(chip, half, core, width):
    owner = chip * CORES + (core if half == 0 else CORES - 1 - core)
    return pl.ds(pl.multiple_of(owner * width, width), width)


def norm_kernel(chips, ahead, place_ref, x_ref, gain_ref, cot_ref, *rest):
    out_refs = rest[-len(ahead):]
    chip, core = place_ref[0], place_ref[1]
    values = x_ref[...].astype(jnp.float32)
    inverse = lax.rsqrt(jnp.mean(values * values, axis=-1, keepdims=True) + norm_eps)
    front = cot_ref.shape[1]
    width = (out_refs[0].shape[1] - front) // CORES
    for by, out_ref in zip(ahead, out_refs):
        to = lax.rem(chip + by, chips)
        out_ref[:, :front] = cot_ref[...]
        for half in range(CORES):
            cols = part_columns(to, half, core, width)
            out_ref[:, front + half * width:front + (half + 1) * width] = (
                x_ref[:, cols].astype(jnp.float32) * inverse * gain_ref[:, cols].astype(jnp.float32)
            ).astype(out_ref.dtype)


def normalize(place, rows, gain, cot, chips, ahead, start, count, after):
    width = rows.shape[1]
    front = cot.shape[1]
    block = math.gcd(math.gcd(start, count), 32)
    first = start // block
    out_width = front + width // chips
    return list(call(
        functools.partial(norm_kernel, chips, ahead), "norm_forward",
        4 * count * width, 2 * count * width + 2 * count * out_width * len(ahead),
        grid=(count // block,),
        in_specs=[
            scalars,
            pl.BlockSpec((block, width), lambda i: (first + i, 0)),
            pl.BlockSpec((1, width), lambda i: (0, 0)),
            pl.BlockSpec((block, front), lambda i: (first + i, 0)),
        ] + [whole] * len(after),
        out_specs=[pl.BlockSpec((block, out_width), lambda i: (i, 0))] * len(ahead),
        out_shape=[jax.ShapeDtypeStruct((count, out_width), jnp.bfloat16)] * len(ahead),
    )(place, rows, gain, cot, *after))


def stack_kernel(count, *refs):
    at = 0
    for ref in refs[:count]:
        refs[-1][at:at + ref.shape[0]] = ref[...]
        at += ref.shape[0]


def stack_rows(arrays, after):
    width = arrays[0].shape[1]
    tall = sum(array.shape[0] for array in arrays)
    return call(
        functools.partial(stack_kernel, len(arrays)), "stack_rows", 0, 4 * tall * width,
        grid=(1,),
        in_specs=[pl.BlockSpec(array.shape, lambda i: (0, 0)) for array in arrays] + [whole] * len(after),
        out_specs=pl.BlockSpec((tall, width), lambda i: (0, 0)),
        out_shape=jax.ShapeDtypeStruct((tall, width), arrays[0].dtype),
    )(*arrays, *after)


def attend_kernel(query_ref, key_ref, grad_ref, row_seg_ref, col_seg_ref, out_ref):
    tokens = key_ref.shape[0]
    group = query_ref.shape[1] // HEAD
    at_query = lax.broadcasted_iota(jnp.int32, (tokens, tokens), 0)
    at_key = lax.broadcasted_iota(jnp.int32, (tokens, tokens), 1)
    visible = (col_seg_ref[...] == row_seg_ref[...]) & (at_key <= at_query)
    keys = key_ref[...]
    total = jnp.zeros((tokens, HEAD), jnp.float32)
    for head in range(group):
        cols = slice(head * HEAD, (head + 1) * HEAD)
        scores = lax.dot_general(
            query_ref[:, cols], keys, (((1,), (1,)), ((), ())),
            preferred_element_type=jnp.float32,
        ) / math.sqrt(HEAD)
        masked = jnp.where(visible, scores, masked_value)
        highest = jnp.max(masked, axis=-1, keepdims=True)
        weights = jnp.where(visible, jnp.exp(masked - highest), 0.0)
        attention = (weights / jnp.sum(weights, axis=-1, keepdims=True)).astype(jnp.bfloat16)
        total += lax.dot_general(
            attention, grad_ref[:, cols], (((0,), (0,)), ((), ())),
            preferred_element_type=jnp.float32,
        )
    out_ref[...] = total.astype(out_ref.dtype)


def attend(queries, keys, grads, segments):
    tokens, kv_width = keys.shape
    heads = kv_width // HEAD
    wide = queries.shape[1] // heads
    return call(
        attend_kernel, "attend",
        4 * tokens * tokens * queries.shape[1], 4 * tokens * queries.shape[1],
        grid=(heads,),
        in_specs=[
            pl.BlockSpec((tokens, wide), lambda i: (0, i)),
            pl.BlockSpec((tokens, HEAD), lambda i: (0, i)),
            pl.BlockSpec((tokens, wide), lambda i: (0, i)),
            pl.BlockSpec((1, tokens), lambda i: (0, 0)),
            pl.BlockSpec((tokens, 1), lambda i: (0, 0)),
        ],
        out_specs=pl.BlockSpec((tokens, HEAD), lambda i: (0, i)),
        out_shape=jax.ShapeDtypeStruct((tokens, kv_width), jnp.bfloat16),
    )(queries, keys, grads, segments, segments.reshape(tokens, 1))


def project_kernel(chips, steps, cuts, own_ref, other_ref, *rest):
    row_refs, out_refs, gathered = rest[:chips], rest[-chips * (len(cuts) - 1) - 1:-1], rest[-1]
    taken, depth = row_refs[0].shape
    step = pl.program_id(0)

    @pl.when(step == 0)
    def _():
        for by in range(chips):
            gathered[by] = row_refs[by][...]

    def multiply(weight_ref):
        product = lax.dot_general(
            gathered[...].reshape(chips * taken, depth), weight_ref[...], (((1,), (1,)), ((), ())),
            preferred_element_type=jnp.float32,
        ).astype(jnp.bfloat16)
        for part, (start, end) in enumerate(zip(cuts, cuts[1:])):
            for by in range(chips):
                out_refs[part * chips + by][...] = product[by * taken + start:by * taken + end]

    @pl.when(step < steps)
    def _():
        multiply(own_ref)

    @pl.when(step >= steps)
    def _():
        multiply(other_ref)


def project(rows, own, other, cuts, after):
    chips = len(rows)
    taken, depth = rows[0].shape
    width = own.shape[0]
    block = min(width, 512)
    steps = width // block
    counts = [end - start for start, end in zip(cuts, cuts[1:]) for by in range(chips)]
    results = list(call(
        functools.partial(project_kernel, chips, steps, cuts), "project",
        4 * chips * taken * depth * width, 2 * (chips * taken * (depth + 2 * width) + 2 * width * depth),
        grid=(CORES * steps,),
        in_specs=[
            pl.BlockSpec((block, depth), lambda i: (jnp.minimum(i, steps - 1), 0)),
            pl.BlockSpec((block, depth), lambda i: (jnp.maximum(i - steps, 0), 0)),
        ] + [pl.BlockSpec((taken, depth), lambda i: (0, 0))] * chips + [whole] * len(after),
        out_specs=[pl.BlockSpec((count, block), lambda i: (0, i)) for count in counts],
        out_shape=[jax.ShapeDtypeStruct((count, CORES * width), jnp.bfloat16) for count in counts],
        scratch_shapes=[pltpu.VMEM((chips, taken, depth), jnp.bfloat16)],
    )(own, other, *rows, *after))
    return [results[at:at + chips] for at in range(0, len(results), chips)]


def backward_kernel(chips, place_ref, x_ref, gain_ref, grad_ref, *rest):
    cot_refs, out_ref = rest[:chips], rest[-1]
    chip, core = place_ref[0], place_ref[1]
    values = x_ref[...].astype(jnp.float32)
    width = cot_refs[0].shape[1] // CORES
    inverse = lax.rsqrt(jnp.mean(values * values, axis=-1, keepdims=True) + norm_eps)
    inner = jnp.zeros_like(inverse)

    def parts():
        for by, cot_ref in enumerate(cot_refs):
            source = lax.rem(chip + chips - by, chips)
            for half in range(CORES):
                cols = part_columns(source, half, core, width)
                cot = cot_ref[:, half * width:(half + 1) * width].astype(jnp.float32)
                yield cols, gain_ref[:, cols].astype(jnp.float32) * cot

    for cols, scaled in parts():
        inner += jnp.sum(x_ref[:, cols].astype(jnp.float32) * scaled, axis=-1, keepdims=True)
    factor = inverse * inverse * inverse * (inner / x_ref.shape[1])
    for cols, scaled in parts():
        out_ref[:, cols] = (
            grad_ref[:, cols].astype(jnp.float32)
            + inverse * scaled
            - x_ref[:, cols].astype(jnp.float32) * factor
        ).astype(out_ref.dtype)


def norm_backward(place, cots, rows, gain, grads, start, after):
    tokens, width = rows.shape
    taken, part_width = cots[0].shape
    block = math.gcd(math.gcd(start, taken), 32)
    first = start // block
    return call(
        functools.partial(backward_kernel, len(cots)), "norm_backward",
        10 * taken * width, 8 * taken * width,
        grid=(taken // block,),
        in_specs=[
            scalars,
            pl.BlockSpec((block, width), lambda i: (first + i, 0)),
            pl.BlockSpec((1, width), lambda i: (0, 0)),
            pl.BlockSpec((block, width), lambda i: (first + i, 0)),
        ] + [pl.BlockSpec((block, part_width), lambda i: (i, 0))] * len(cots) + [whole] * len(after),
        out_specs=pl.BlockSpec((block, width), lambda i: (i, 0)),
        out_shape=jax.ShapeDtypeStruct((taken, width), jnp.bfloat16),
    )(place, rows, gain, grads, *cots, *after)


def outer_kernel(groups, sums, halves, *refs):
    arrays = sum(groups)
    cots, columns, terms = refs[:arrays], refs[arrays:2 * arrays], refs[2 * arrays:2 * arrays + sums]
    total, at = None, 0
    for size in groups:
        column, cot = columns[at][...], cots[at][...]
        for more in range(at + 1, at + size):
            column, cot = column + columns[more][...], cot + cots[more][...]
        at += size
        product = lax.dot_general(
            column, cot, (((0,), (0,)), ((), ())), preferred_element_type=jnp.float32
        )
        total = product if total is None else total + product
    for term in terms:
        total += term[...].astype(jnp.float32)
    if halves:
        lower, upper = refs[2 * arrays + sums:2 * arrays + sums + 2]
        in_lower = pl.program_id(0) < pl.num_programs(0) // 2
        total += jnp.where(in_lower, lower[...], upper[...]).astype(jnp.float32)
    refs[-1][...] = total.astype(refs[-1].dtype)


def outer(groups, cot_width, half, before, dtype, part=0, parts=1, halves=(), after=()):
    payloads = [payload for group in groups for payload in group]
    wide = payloads[0].shape[1]
    width = (wide - cot_width) // CORES
    block = math.gcd(math.gcd(width // 2, 256), cot_width)
    steps = width // parts // block
    skip = part * steps
    first = (cot_width + half * width) // block + skip
    middle = steps // 2
    tokens = sum(payload.shape[0] for payload in payloads)
    return call(
        functools.partial(outer_kernel, [len(group) for group in groups], len(before), len(halves)), "outer",
        2 * tokens * width * cot_width, 2 * tokens * width + 4 * width * cot_width,
        grid=(steps,),
        in_specs=[pl.BlockSpec((payload.shape[0], cot_width), lambda i: (0, 0)) for payload in payloads]
        + [pl.BlockSpec((payload.shape[0], block), lambda i: (0, first + i)) for payload in payloads]
        + [pl.BlockSpec((block, cot_width), lambda i: (skip + i, 0)) for term in before]
        + [
            pl.BlockSpec((block, cot_width), lambda i: (jnp.minimum(i, middle - 1), 0)),
            pl.BlockSpec((block, cot_width), lambda i: (jnp.maximum(i - middle, 0), 0)),
        ][:len(halves)]
        + [whole] * len(after),
        out_specs=pl.BlockSpec((block, cot_width), lambda i: (i, 0)),
        out_shape=jax.ShapeDtypeStruct((width // parts, cot_width), dtype),
    )(*payloads, *payloads, *before, *halves, *after)


def shards(
    new_input,
    new_gain,
    queries,
    new_keys,
    context_grad,
    segment_ids,
    frozen_input,
    frozen_gain,
    output_grad,
    kv_grad,
    kv_weight,
):
    chips = lax.axis_size("dp") // CORES
    sections = lax.axis_size("pipe")
    tokens, kv_width = new_keys.shape[1:]
    at = lax.axis_index("dp")
    place = jnp.stack([at // CORES, at % CORES]).astype(jnp.int32)
    middle = chips // 2
    near = [by for by in range(1, chips) if by != middle]
    spread = tokens // 8

    rows = [kv_grad[0]] + [along_chips(kv_grad[0], chips - by, 1) for by in range(1, chips)]
    other_weight = swap_cores(kv_weight[0])
    value_cot = attend(queries[0], new_keys[0], context_grad[0], segment_ids)

    apply = functools.partial(normalize, place, new_input[0], new_gain, value_cot, chips)
    shared = apply([middle], 0, spread, [other_weight])[0]
    brought = [between_lines(shared, section, 0) for section in range(1, sections)]
    early = apply([0] + near[:1], 0, tokens, rows[1:])
    columns = [early[0]] + [along_chips(block, by) for block, by in zip(early[1:], near)]
    joint = stack_rows([shared] + brought, early[:1])
    moved = on_line(joint, middle, 0)
    returned = [moved[:spread]] + [
        between_lines(moved[section * spread:(section + 1) * spread], 0, section) for section in range(1, sections)
    ]

    cuts = [0, tokens * 5 // 8, tokens]
    parts = project(rows, kv_weight[0], other_weight, cuts, [joint])
    arrived = [
        [part[0]] + [along_chips(part[by], by, 1) for by in range(1, chips)] for part in parts
    ]
    backward = functools.partial(norm_backward, place, rows=frozen_input[0], gain=frozen_gain, grads=output_grad[0])
    above = backward(arrived[0], start=cuts[0], after=columns[1:])
    kept = apply([middle], spread, tokens - spread, [above] + [arrived[1][by] for by in near])
    late = apply(near[1:], 0, tokens, kept)
    above = [above, backward(arrived[1], start=cuts[1], after=late[:1])]
    below = [from_behind(half, "pipe", -1) for half in above]
    cot_below = stack_rows(below, [])

    groups = [[column] for column in columns] + [returned]
    last = [[along_chips(block, by)] for block, by in zip(late + kept, near[1:] + [middle])]
    sums = [outer(groups, kv_width, half, [], jnp.float32, after=above[1:]) for half in range(CORES)]
    given = [
        outer(last, kv_width, 1, sums[1:], jnp.bfloat16, part, 2, after=sums[:1]) for part in range(2)
    ]
    taken = [swap_cores(part) for part in given]
    grad = outer(last, kv_width, 0, sums[:1], jnp.float32, halves=taken)
    return (cot_below[None], grad[None])


def solution(mesh):
    placed = (
        P("pipe", "dp", None),
        P("pipe", None),
        P("pipe", "dp", None),
        P("pipe", "dp", None),
        P("pipe", "dp", None),
        P("pipe", "dp"),
        P("pipe", "dp", None),
        P("pipe", None),
        P("pipe", "dp", None),
        P("pipe", "dp", None),
        P("pipe", "dp", None),
    )
    return jax.shard_map(
        shards,
        mesh=mesh,
        in_specs=placed,
        out_specs=(P("pipe", "dp", None), P("pipe", "dp", None)),
        check_vma=False,
    )
```

```python
import functools
import math

import jax
import jax.numpy as jnp
from jax import lax
from jax.experimental import pallas as pl
from jax.experimental.pallas import tpu as pltpu
from jax.sharding import PartitionSpec as P

HEAD = 128
CORES = 2
MIB = 1 << 20

norm_eps = 1e-05
masked_value = -1e30

whole = pl.BlockSpec(memory_space=pl.ANY)
scalars = pl.BlockSpec(memory_space=pltpu.SMEM)


def from_behind(array, axis, by):
    length = lax.axis_size(axis)
    pairs = [(i, i + by) for i in range(length) if 0 <= i + by < length]
    return lax.ppermute(array, axis, pairs)


def along_chips(array, by, first=0):
    length = lax.axis_size("dp")
    pairs = [
        (line * length + i, line * length + ((i + by * CORES) % length if line >= first else i ^ 1))
        for line in range(lax.axis_size("pipe")) for i in range(length)
    ]
    return lax.ppermute(array, ("pipe", "dp"), pairs)


def between_lines(array, source, target):
    length = lax.axis_size("dp")
    pairs = [(source * length + i, target * length + i) for i in range(length)]
    return lax.ppermute(array, ("pipe", "dp"), pairs)


def on_line(array, by, line):
    length = lax.axis_size("dp")
    pairs = [(line * length + i, line * length + (i + by * CORES) % length) for i in range(length)]
    return lax.ppermute(array, ("pipe", "dp"), pairs)


def swap_cores(array):
    length = lax.axis_size("dp")
    return lax.ppermute(array, "dp", [(i, i ^ 1) for i in range(length)])


def call(body, name, flops, nbytes, vmem=24, **kwargs):
    return pl.pallas_call(
        body,
        name=name,
        compiler_params=pltpu.CompilerParams(vmem_limit_bytes=vmem * MIB),
        cost_estimate=pl.CostEstimate(flops=flops, bytes_accessed=nbytes, transcendentals=0),
        **kwargs,
    )


def part_columns(chip, half, core, width):
    owner = chip * CORES + (core if half == 0 else CORES - 1 - core)
    return pl.ds(pl.multiple_of(owner * width, width), width)


def norm_kernel(chips, ahead, place_ref, x_ref, gain_ref, cot_ref, *rest):
    out_refs = rest[-len(ahead):]
    chip, core = place_ref[0], place_ref[1]
    values = x_ref[...].astype(jnp.float32)
    inverse = lax.rsqrt(jnp.mean(values * values, axis=-1, keepdims=True) + norm_eps)
    front = cot_ref.shape[1]
    width = (out_refs[0].shape[1] - front) // CORES
    for by, out_ref in zip(ahead, out_refs):
        to = lax.rem(chip + by, chips)
        out_ref[:, :front] = cot_ref[...]
        for half in range(CORES):
            cols = part_columns(to, half, core, width)
            out_ref[:, front + half * width:front + (half + 1) * width] = (
                x_ref[:, cols].astype(jnp.float32) * inverse * gain_ref[:, cols].astype(jnp.float32)
            ).astype(out_ref.dtype)


def normalize(place, rows, gain, cot, chips, ahead, start, count, after):
    width = rows.shape[1]
    front = cot.shape[1]
    block = math.gcd(math.gcd(start, count), 32)
    first = start // block
    out_width = front + width // chips
    return list(call(
        functools.partial(norm_kernel, chips, ahead), "norm_forward",
        4 * count * width, 2 * count * width + 2 * count * out_width * len(ahead),
        grid=(count // block,),
        in_specs=[
            scalars,
            pl.BlockSpec((block, width), lambda i: (first + i, 0)),
            pl.BlockSpec((1, width), lambda i: (0, 0)),
            pl.BlockSpec((block, front), lambda i: (first + i, 0)),
        ] + [whole] * len(after),
        out_specs=[pl.BlockSpec((block, out_width), lambda i: (i, 0))] * len(ahead),
        out_shape=[jax.ShapeDtypeStruct((count, out_width), jnp.bfloat16)] * len(ahead),
    )(place, rows, gain, cot, *after))


def stack_kernel(count, *refs):
    at = 0
    for ref in refs[:count]:
        refs[-1][at:at + ref.shape[0]] = ref[...]
        at += ref.shape[0]


def stack_rows(arrays, after):
    width = arrays[0].shape[1]
    tall = sum(array.shape[0] for array in arrays)
    return call(
        functools.partial(stack_kernel, len(arrays)), "stack_rows", 0, 4 * tall * width,
        grid=(1,),
        in_specs=[pl.BlockSpec(array.shape, lambda i: (0, 0)) for array in arrays] + [whole] * len(after),
        out_specs=pl.BlockSpec((tall, width), lambda i: (0, 0)),
        out_shape=jax.ShapeDtypeStruct((tall, width), arrays[0].dtype),
    )(*arrays, *after)


def join_kernel(count, *refs):
    out_ref, semaphores = refs[-2], refs[-1]
    at, copies = 0, []
    for index, ref in enumerate(refs[:count]):
        tall = ref.shape[0]
        copies.append(pltpu.make_async_copy(ref, out_ref.at[at:at + tall], semaphores.at[index]))
        at += tall
    for copy in copies:
        copy.start()
    for copy in copies:
        copy.wait()


def join_rows(arrays):
    width = arrays[0].shape[1]
    tall = sum(array.shape[0] for array in arrays)
    return call(
        functools.partial(join_kernel, len(arrays)), "join_rows", 0, 4 * tall * width,
        in_specs=[whole] * len(arrays),
        out_specs=pl.BlockSpec(memory_space=pltpu.HBM),
        out_shape=jax.ShapeDtypeStruct((tall, width), arrays[0].dtype),
        scratch_shapes=[pltpu.SemaphoreType.DMA((len(arrays),))],
    )(*arrays)


def attend_kernel(query_ref, key_ref, grad_ref, row_seg_ref, col_seg_ref, out_ref):
    tokens = key_ref.shape[0]
    group = query_ref.shape[1] // HEAD
    at_query = lax.broadcasted_iota(jnp.int32, (tokens, tokens), 0)
    at_key = lax.broadcasted_iota(jnp.int32, (tokens, tokens), 1)
    visible = (col_seg_ref[...] == row_seg_ref[...]) & (at_key <= at_query)
    keys = key_ref[...]
    total = jnp.zeros((tokens, HEAD), jnp.float32)
    for head in range(group):
        cols = slice(head * HEAD, (head + 1) * HEAD)
        scores = lax.dot_general(
            query_ref[:, cols], keys, (((1,), (1,)), ((), ())),
            preferred_element_type=jnp.float32,
        ) / math.sqrt(HEAD)
        masked = jnp.where(visible, scores, masked_value)
        highest = jnp.max(masked, axis=-1, keepdims=True)
        weights = jnp.where(visible, jnp.exp(masked - highest), 0.0)
        attention = (weights / jnp.sum(weights, axis=-1, keepdims=True)).astype(jnp.bfloat16)
        total += lax.dot_general(
            attention, grad_ref[:, cols], (((0,), (0,)), ((), ())),
            preferred_element_type=jnp.float32,
        )
    out_ref[...] = total.astype(out_ref.dtype)


def attend(queries, keys, grads, segments):
    tokens, kv_width = keys.shape
    heads = kv_width // HEAD
    wide = queries.shape[1] // heads
    return call(
        attend_kernel, "attend",
        4 * tokens * tokens * queries.shape[1], 4 * tokens * queries.shape[1],
        grid=(heads,),
        in_specs=[
            pl.BlockSpec((tokens, wide), lambda i: (0, i)),
            pl.BlockSpec((tokens, HEAD), lambda i: (0, i)),
            pl.BlockSpec((tokens, wide), lambda i: (0, i)),
            pl.BlockSpec((1, tokens), lambda i: (0, 0)),
            pl.BlockSpec((tokens, 1), lambda i: (0, 0)),
        ],
        out_specs=pl.BlockSpec((tokens, HEAD), lambda i: (0, i)),
        out_shape=jax.ShapeDtypeStruct((tokens, kv_width), jnp.bfloat16),
    )(queries, keys, grads, segments, segments.reshape(tokens, 1))


def project_kernel(chips, steps, cuts, own_ref, other_ref, *rest):
    row_refs, out_refs, gathered = rest[:chips], rest[-chips * (len(cuts) - 1) - 1:-1], rest[-1]
    taken, depth = row_refs[0].shape
    step = pl.program_id(0)

    @pl.when(step == 0)
    def _():
        for by in range(chips):
            gathered[by] = row_refs[by][...]

    def multiply(weight_ref):
        product = lax.dot_general(
            gathered[...].reshape(chips * taken, depth), weight_ref[...], (((1,), (1,)), ((), ())),
            preferred_element_type=jnp.float32,
        ).astype(jnp.bfloat16)
        for part, (start, end) in enumerate(zip(cuts, cuts[1:])):
            for by in range(chips):
                out_refs[part * chips + by][...] = product[by * taken + start:by * taken + end]

    @pl.when(step < steps)
    def _():
        multiply(own_ref)

    @pl.when(step >= steps)
    def _():
        multiply(other_ref)


def project(rows, own, other, cuts, after):
    chips = len(rows)
    taken, depth = rows[0].shape
    width = own.shape[0]
    block = min(width, 512)
    steps = width // block
    counts = [end - start for start, end in zip(cuts, cuts[1:]) for by in range(chips)]
    results = list(call(
        functools.partial(project_kernel, chips, steps, cuts), "project",
        4 * chips * taken * depth * width, 2 * (chips * taken * (depth + 2 * width) + 2 * width * depth),
        grid=(CORES * steps,),
        in_specs=[
            pl.BlockSpec((block, depth), lambda i: (jnp.minimum(i, steps - 1), 0)),
            pl.BlockSpec((block, depth), lambda i: (jnp.maximum(i - steps, 0), 0)),
        ] + [pl.BlockSpec((taken, depth), lambda i: (0, 0))] * chips + [whole] * len(after),
        out_specs=[pl.BlockSpec((count, block), lambda i: (0, i)) for count in counts],
        out_shape=[jax.ShapeDtypeStruct((count, CORES * width), jnp.bfloat16) for count in counts],
        scratch_shapes=[pltpu.VMEM((chips, taken, depth), jnp.bfloat16)],
    )(own, other, *rows, *after))
    return [results[at:at + chips] for at in range(0, len(results), chips)]


def backward_kernel(chips, place_ref, x_ref, gain_ref, grad_ref, *rest):
    cot_refs, out_ref = rest[:chips], rest[-1]
    chip, core = place_ref[0], place_ref[1]
    values = x_ref[...].astype(jnp.float32)
    width = cot_refs[0].shape[1] // CORES
    inverse = lax.rsqrt(jnp.mean(values * values, axis=-1, keepdims=True) + norm_eps)
    inner = jnp.zeros_like(inverse)

    def parts():
        for by, cot_ref in enumerate(cot_refs):
            source = lax.rem(chip + chips - by, chips)
            for half in range(CORES):
                cols = part_columns(source, half, core, width)
                cot = cot_ref[:, half * width:(half + 1) * width].astype(jnp.float32)
                yield cols, gain_ref[:, cols].astype(jnp.float32) * cot

    for cols, scaled in parts():
        inner += jnp.sum(x_ref[:, cols].astype(jnp.float32) * scaled, axis=-1, keepdims=True)
    factor = inverse * inverse * inverse * (inner / x_ref.shape[1])
    for cols, scaled in parts():
        out_ref[:, cols] = (
            grad_ref[:, cols].astype(jnp.float32)
            + inverse * scaled
            - x_ref[:, cols].astype(jnp.float32) * factor
        ).astype(out_ref.dtype)


def norm_backward(place, cots, rows, gain, grads, start, after):
    tokens, width = rows.shape
    taken, part_width = cots[0].shape
    block = math.gcd(math.gcd(start, taken), 32)
    first = start // block
    return call(
        functools.partial(backward_kernel, len(cots)), "norm_backward",
        10 * taken * width, 8 * taken * width,
        grid=(taken // block,),
        in_specs=[
            scalars,
            pl.BlockSpec((block, width), lambda i: (first + i, 0)),
            pl.BlockSpec((1, width), lambda i: (0, 0)),
            pl.BlockSpec((block, width), lambda i: (first + i, 0)),
        ] + [pl.BlockSpec((block, part_width), lambda i: (i, 0))] * len(cots) + [whole] * len(after),
        out_specs=pl.BlockSpec((block, width), lambda i: (i, 0)),
        out_shape=jax.ShapeDtypeStruct((taken, width), jnp.bfloat16),
    )(place, rows, gain, grads, *cots, *after)


def outer_kernel(groups, sums, halves, *refs):
    arrays = sum(groups)
    cots, columns, terms = refs[:arrays], refs[arrays:2 * arrays], refs[2 * arrays:2 * arrays + sums]
    total, at = None, 0
    for size in groups:
        column, cot = columns[at][...], cots[at][...]
        for more in range(at + 1, at + size):
            column, cot = column + columns[more][...], cot + cots[more][...]
        at += size
        product = lax.dot_general(
            column, cot, (((0,), (0,)), ((), ())), preferred_element_type=jnp.float32
        )
        total = product if total is None else total + product
    for term in terms:
        total += term[...].astype(jnp.float32)
    if halves:
        lower, upper = refs[2 * arrays + sums:2 * arrays + sums + 2]
        in_lower = pl.program_id(0) < pl.num_programs(0) // 2
        total += jnp.where(in_lower, lower[...], upper[...]).astype(jnp.float32)
    refs[-1][...] = total.astype(refs[-1].dtype)


def outer(groups, cot_width, half, before, dtype, part=0, parts=1, halves=(), after=()):
    payloads = [payload for group in groups for payload in group]
    wide = payloads[0].shape[1]
    width = (wide - cot_width) // CORES
    block = math.gcd(math.gcd(width // 2, 256), cot_width)
    steps = width // parts // block
    skip = part * steps
    first = (cot_width + half * width) // block + skip
    middle = steps // 2
    tokens = sum(payload.shape[0] for payload in payloads)
    return call(
        functools.partial(outer_kernel, [len(group) for group in groups], len(before), len(halves)), "outer",
        2 * tokens * width * cot_width, 2 * tokens * width + 4 * width * cot_width,
        grid=(steps,),
        in_specs=[pl.BlockSpec((payload.shape[0], cot_width), lambda i: (0, 0)) for payload in payloads]
        + [pl.BlockSpec((payload.shape[0], block), lambda i: (0, first + i)) for payload in payloads]
        + [pl.BlockSpec((block, cot_width), lambda i: (skip + i, 0)) for term in before]
        + [
            pl.BlockSpec((block, cot_width), lambda i: (jnp.minimum(i, middle - 1), 0)),
            pl.BlockSpec((block, cot_width), lambda i: (jnp.maximum(i - middle, 0), 0)),
        ][:len(halves)]
        + [whole] * len(after),
        out_specs=pl.BlockSpec((block, cot_width), lambda i: (i, 0)),
        out_shape=jax.ShapeDtypeStruct((width // parts, cot_width), dtype),
    )(*payloads, *payloads, *before, *halves, *after)


def shards(
    new_input,
    new_gain,
    queries,
    new_keys,
    context_grad,
    segment_ids,
    frozen_input,
    frozen_gain,
    output_grad,
    kv_grad,
    kv_weight,
):
    chips = lax.axis_size("dp") // CORES
    sections = lax.axis_size("pipe")
    tokens, kv_width = new_keys.shape[1:]
    at = lax.axis_index("dp")
    place = jnp.stack([at // CORES, at % CORES]).astype(jnp.int32)
    middle = chips // 2
    near = [by for by in range(1, chips) if by != middle]
    spread = tokens // 4

    rows = [kv_grad[0]] + [along_chips(kv_grad[0], chips - by, 1) for by in range(1, chips)]
    other_weight = swap_cores(kv_weight[0])
    value_cot = attend(queries[0], new_keys[0], context_grad[0], segment_ids)

    apply = functools.partial(normalize, place, new_input[0], new_gain, value_cot, chips)
    shared = apply([middle], 0, spread, [other_weight])[0]
    brought = [between_lines(shared, section, 0) for section in range(1, sections)]
    early = apply([0] + near[:1], 0, tokens, rows[1:])
    columns = [early[0]] + [along_chips(block, by) for block, by in zip(early[1:], near)]
    joint = stack_rows([shared] + brought, early[:1])
    moved = on_line(joint, middle, 0)
    returned = [moved[:spread]] + [
        between_lines(moved[section * spread:(section + 1) * spread], 0, section) for section in range(1, sections)
    ]

    cuts = [0, tokens * 5 // 8, tokens]
    parts = project(rows, kv_weight[0], other_weight, cuts, [joint])
    arrived = [
        [part[0]] + [along_chips(part[by], by, 1) for by in range(1, chips)] for part in parts
    ]
    backward = functools.partial(norm_backward, place, rows=frozen_input[0], gain=frozen_gain, grads=output_grad[0])
    above = backward(arrived[0], start=cuts[0], after=columns[1:])
    kept = apply([middle], spread, tokens - spread, [above] + [arrived[1][by] for by in near])
    late = apply(near[1:], 0, tokens, kept)
    above = [above, backward(arrived[1], start=cuts[1], after=late[:1])]
    below = [from_behind(half, "pipe", -1) for half in above]
    cot_below = join_rows(below)

    groups = [[column] for column in columns] + [returned]
    last = [[along_chips(block, by)] for block, by in zip(late + kept, near[1:] + [middle])]
    sums = [outer(groups, kv_width, half, [], jnp.float32, after=above[1:]) for half in range(CORES)]
    given = [
        outer(last, kv_width, 1, sums[1:], jnp.bfloat16, part, 2, after=sums[:1]) for part in range(2)
    ]
    taken = [swap_cores(part) for part in given]
    grad = outer(last, kv_width, 0, sums[:1], jnp.float32, halves=taken)
    return (cot_below[None], grad[None])


def solution(mesh):
    placed = (
        P("pipe", "dp", None),
        P("pipe", None),
        P("pipe", "dp", None),
        P("pipe", "dp", None),
        P("pipe", "dp", None),
        P("pipe", "dp"),
        P("pipe", "dp", None),
        P("pipe", None),
        P("pipe", "dp", None),
        P("pipe", "dp", None),
        P("pipe", "dp", None),
    )
    return jax.shard_map(
        shards,
        mesh=mesh,
        in_specs=placed,
        out_specs=(P("pipe", "dp", None), P("pipe", "dp", None)),
        check_vma=False,
    )
```

```python
import functools
import math

import jax
import jax.numpy as jnp
from jax import lax
from jax.experimental import pallas as pl
from jax.experimental.pallas import tpu as pltpu
from jax.sharding import PartitionSpec as P

HEAD = 128
CORES = 2
MIB = 1 << 20

norm_eps = 1e-05
masked_value = -1e30

whole = pl.BlockSpec(memory_space=pl.ANY)
scalars = pl.BlockSpec(memory_space=pltpu.SMEM)


def from_behind(array, axis, by):
    length = lax.axis_size(axis)
    pairs = [(i, i + by) for i in range(length) if 0 <= i + by < length]
    return lax.ppermute(array, axis, pairs)


def along_chips(array, by, first=0):
    length = lax.axis_size("dp")
    pairs = [
        (line * length + i, line * length + ((i + by * CORES) % length if line >= first else i ^ 1))
        for line in range(lax.axis_size("pipe")) for i in range(length)
    ]
    return lax.ppermute(array, ("pipe", "dp"), pairs)


def between_lines(array, source, target):
    length = lax.axis_size("dp")
    pairs = [(source * length + i, target * length + i) for i in range(length)]
    return lax.ppermute(array, ("pipe", "dp"), pairs)


def on_line(array, by, line):
    length = lax.axis_size("dp")
    pairs = [(line * length + i, line * length + (i + by * CORES) % length) for i in range(length)]
    return lax.ppermute(array, ("pipe", "dp"), pairs)


def swap_cores(array):
    length = lax.axis_size("dp")
    return lax.ppermute(array, "dp", [(i, i ^ 1) for i in range(length)])


def call(body, name, flops, nbytes, vmem=24, **kwargs):
    return pl.pallas_call(
        body,
        name=name,
        compiler_params=pltpu.CompilerParams(vmem_limit_bytes=vmem * MIB),
        cost_estimate=pl.CostEstimate(flops=flops, bytes_accessed=nbytes, transcendentals=0),
        **kwargs,
    )


def part_columns(chip, half, core, width):
    owner = chip * CORES + (core if half == 0 else CORES - 1 - core)
    return pl.ds(pl.multiple_of(owner * width, width), width)


def norm_kernel(chips, ahead, place_ref, x_ref, gain_ref, cot_ref, *rest):
    out_refs = rest[-len(ahead):]
    chip, core = place_ref[0], place_ref[1]
    values = x_ref[...].astype(jnp.float32)
    inverse = lax.rsqrt(jnp.mean(values * values, axis=-1, keepdims=True) + norm_eps)
    front = cot_ref.shape[1]
    width = (out_refs[0].shape[1] - front) // CORES
    for by, out_ref in zip(ahead, out_refs):
        to = lax.rem(chip + by, chips)
        out_ref[:, :front] = cot_ref[...]
        for half in range(CORES):
            cols = part_columns(to, half, core, width)
            out_ref[:, front + half * width:front + (half + 1) * width] = (
                x_ref[:, cols].astype(jnp.float32) * inverse * gain_ref[:, cols].astype(jnp.float32)
            ).astype(out_ref.dtype)


def normalize(place, rows, gain, cot, chips, ahead, start, count, after):
    width = rows.shape[1]
    front = cot.shape[1]
    block = math.gcd(math.gcd(start, count), 32)
    first = start // block
    out_width = front + width // chips
    return list(call(
        functools.partial(norm_kernel, chips, ahead), "norm_forward",
        4 * count * width, 2 * count * width + 2 * count * out_width * len(ahead),
        grid=(count // block,),
        in_specs=[
            scalars,
            pl.BlockSpec((block, width), lambda i: (first + i, 0)),
            pl.BlockSpec((1, width), lambda i: (0, 0)),
            pl.BlockSpec((block, front), lambda i: (first + i, 0)),
        ] + [whole] * len(after),
        out_specs=[pl.BlockSpec((block, out_width), lambda i: (i, 0))] * len(ahead),
        out_shape=[jax.ShapeDtypeStruct((count, out_width), jnp.bfloat16)] * len(ahead),
    )(place, rows, gain, cot, *after))


def stack_kernel(count, *refs):
    at = 0
    for ref in refs[:count]:
        refs[-1][at:at + ref.shape[0]] = ref[...]
        at += ref.shape[0]


def stack_rows(arrays, after):
    width = arrays[0].shape[1]
    tall = sum(array.shape[0] for array in arrays)
    return call(
        functools.partial(stack_kernel, len(arrays)), "stack_rows", 0, 4 * tall * width,
        grid=(1,),
        in_specs=[pl.BlockSpec(array.shape, lambda i: (0, 0)) for array in arrays] + [whole] * len(after),
        out_specs=pl.BlockSpec((tall, width), lambda i: (0, 0)),
        out_shape=jax.ShapeDtypeStruct((tall, width), arrays[0].dtype),
    )(*arrays, *after)


def join_kernel(count, *refs):
    out_ref, semaphores = refs[-2], refs[-1]
    at, copies = 0, []
    for index, ref in enumerate(refs[:count]):
        tall = ref.shape[0]
        copies.append(pltpu.make_async_copy(ref, out_ref.at[at:at + tall], semaphores.at[index]))
        at += tall
    for copy in copies:
        copy.start()
    for copy in copies:
        copy.wait()


def join_rows(arrays):
    width = arrays[0].shape[1]
    tall = sum(array.shape[0] for array in arrays)
    return call(
        functools.partial(join_kernel, len(arrays)), "join_rows", 0, 4 * tall * width,
        in_specs=[whole] * len(arrays),
        out_specs=pl.BlockSpec(memory_space=pltpu.HBM),
        out_shape=jax.ShapeDtypeStruct((tall, width), arrays[0].dtype),
        scratch_shapes=[pltpu.SemaphoreType.DMA((len(arrays),))],
    )(*arrays)


def attend_kernel(query_ref, key_ref, grad_ref, row_seg_ref, col_seg_ref, out_ref):
    tokens = key_ref.shape[0]
    group = query_ref.shape[1] // HEAD
    at_query = lax.broadcasted_iota(jnp.int32, (tokens, tokens), 0)
    at_key = lax.broadcasted_iota(jnp.int32, (tokens, tokens), 1)
    visible = (col_seg_ref[...] == row_seg_ref[...]) & (at_key <= at_query)
    keys = key_ref[...]
    total = jnp.zeros((tokens, HEAD), jnp.float32)
    for head in range(group):
        cols = slice(head * HEAD, (head + 1) * HEAD)
        scores = lax.dot_general(
            query_ref[:, cols], keys, (((1,), (1,)), ((), ())),
            preferred_element_type=jnp.float32,
        ) / math.sqrt(HEAD)
        masked = jnp.where(visible, scores, masked_value)
        highest = jnp.max(masked, axis=-1, keepdims=True)
        weights = jnp.where(visible, jnp.exp(masked - highest), 0.0)
        attention = (weights / jnp.sum(weights, axis=-1, keepdims=True)).astype(jnp.bfloat16)
        total += lax.dot_general(
            attention, grad_ref[:, cols], (((0,), (0,)), ((), ())),
            preferred_element_type=jnp.float32,
        )
    out_ref[...] = total.astype(out_ref.dtype)


def attend(queries, keys, grads, segments):
    tokens, kv_width = keys.shape
    heads = kv_width // HEAD
    wide = queries.shape[1] // heads
    return call(
        attend_kernel, "attend",
        4 * tokens * tokens * queries.shape[1], 4 * tokens * queries.shape[1],
        grid=(heads,),
        in_specs=[
            pl.BlockSpec((tokens, wide), lambda i: (0, i)),
            pl.BlockSpec((tokens, HEAD), lambda i: (0, i)),
            pl.BlockSpec((tokens, wide), lambda i: (0, i)),
            pl.BlockSpec((1, tokens), lambda i: (0, 0)),
            pl.BlockSpec((tokens, 1), lambda i: (0, 0)),
        ],
        out_specs=pl.BlockSpec((tokens, HEAD), lambda i: (0, i)),
        out_shape=jax.ShapeDtypeStruct((tokens, kv_width), jnp.bfloat16),
    )(queries, keys, grads, segments, segments.reshape(tokens, 1))


def project_kernel(chips, steps, cuts, own_ref, other_ref, *rest):
    row_refs, out_refs, gathered = rest[:chips], rest[-chips * (len(cuts) - 1) - 1:-1], rest[-1]
    taken, depth = row_refs[0].shape
    step = pl.program_id(0)

    @pl.when(step == 0)
    def _():
        for by in range(chips):
            gathered[by] = row_refs[by][...]

    def multiply(weight_ref):
        product = lax.dot_general(
            gathered[...].reshape(chips * taken, depth), weight_ref[...], (((1,), (1,)), ((), ())),
            preferred_element_type=jnp.float32,
        ).astype(jnp.bfloat16)
        for part, (start, end) in enumerate(zip(cuts, cuts[1:])):
            for by in range(chips):
                out_refs[part * chips + by][...] = product[by * taken + start:by * taken + end]

    @pl.when(step < steps)
    def _():
        multiply(own_ref)

    @pl.when(step >= steps)
    def _():
        multiply(other_ref)


def project(rows, own, other, cuts, after):
    chips = len(rows)
    taken, depth = rows[0].shape
    width = own.shape[0]
    block = min(width, 512)
    steps = width // block
    counts = [end - start for start, end in zip(cuts, cuts[1:]) for by in range(chips)]
    results = list(call(
        functools.partial(project_kernel, chips, steps, cuts), "project",
        4 * chips * taken * depth * width, 2 * (chips * taken * (depth + 2 * width) + 2 * width * depth),
        grid=(CORES * steps,),
        in_specs=[
            pl.BlockSpec((block, depth), lambda i: (jnp.minimum(i, steps - 1), 0)),
            pl.BlockSpec((block, depth), lambda i: (jnp.maximum(i - steps, 0), 0)),
        ] + [pl.BlockSpec((taken, depth), lambda i: (0, 0))] * chips + [whole] * len(after),
        out_specs=[pl.BlockSpec((count, block), lambda i: (0, i)) for count in counts],
        out_shape=[jax.ShapeDtypeStruct((count, CORES * width), jnp.bfloat16) for count in counts],
        scratch_shapes=[pltpu.VMEM((chips, taken, depth), jnp.bfloat16)],
    )(own, other, *rows, *after))
    return [results[at:at + chips] for at in range(0, len(results), chips)]


def backward_kernel(chips, place_ref, x_ref, gain_ref, grad_ref, *rest):
    cot_refs, out_ref = rest[:chips], rest[-1]
    chip, core = place_ref[0], place_ref[1]
    values = x_ref[...].astype(jnp.float32)
    width = cot_refs[0].shape[1] // CORES
    inverse = lax.rsqrt(jnp.mean(values * values, axis=-1, keepdims=True) + norm_eps)
    inner = jnp.zeros_like(inverse)

    def parts():
        for by, cot_ref in enumerate(cot_refs):
            source = lax.rem(chip + chips - by, chips)
            for half in range(CORES):
                cols = part_columns(source, half, core, width)
                cot = cot_ref[:, half * width:(half + 1) * width].astype(jnp.float32)
                yield cols, gain_ref[:, cols].astype(jnp.float32) * cot

    for cols, scaled in parts():
        inner += jnp.sum(x_ref[:, cols].astype(jnp.float32) * scaled, axis=-1, keepdims=True)
    factor = inverse * inverse * inverse * (inner / x_ref.shape[1])
    for cols, scaled in parts():
        out_ref[:, cols] = (
            grad_ref[:, cols].astype(jnp.float32)
            + inverse * scaled
            - x_ref[:, cols].astype(jnp.float32) * factor
        ).astype(out_ref.dtype)


def norm_backward(place, cots, rows, gain, grads, start, after):
    tokens, width = rows.shape
    taken, part_width = cots[0].shape
    block = math.gcd(math.gcd(start, taken), 32)
    first = start // block
    return call(
        functools.partial(backward_kernel, len(cots)), "norm_backward",
        10 * taken * width, 8 * taken * width,
        grid=(taken // block,),
        in_specs=[
            scalars,
            pl.BlockSpec((block, width), lambda i: (first + i, 0)),
            pl.BlockSpec((1, width), lambda i: (0, 0)),
            pl.BlockSpec((block, width), lambda i: (first + i, 0)),
        ] + [pl.BlockSpec((block, part_width), lambda i: (i, 0))] * len(cots) + [whole] * len(after),
        out_specs=pl.BlockSpec((block, width), lambda i: (i, 0)),
        out_shape=jax.ShapeDtypeStruct((taken, width), jnp.bfloat16),
    )(place, rows, gain, grads, *cots, *after)


def outer_kernel(groups, sums, halves, *refs):
    arrays = sum(groups)
    cots, columns, terms = refs[:arrays], refs[arrays:2 * arrays], refs[2 * arrays:2 * arrays + sums]
    total, at = None, 0
    for size in groups:
        column, cot = columns[at][...], cots[at][...]
        for more in range(at + 1, at + size):
            column, cot = column + columns[more][...], cot + cots[more][...]
        at += size
        product = lax.dot_general(
            column, cot, (((0,), (0,)), ((), ())), preferred_element_type=jnp.float32
        )
        total = product if total is None else total + product
    for term in terms:
        total += term[...].astype(jnp.float32)
    if halves:
        lower, upper = refs[2 * arrays + sums:2 * arrays + sums + 2]
        in_lower = pl.program_id(0) < pl.num_programs(0) // 2
        total += jnp.where(in_lower, lower[...], upper[...]).astype(jnp.float32)
    refs[-1][...] = total.astype(refs[-1].dtype)


def outer(groups, cot_width, half, before, dtype, part=0, parts=1, halves=(), after=()):
    payloads = [payload for group in groups for payload in group]
    wide = payloads[0].shape[1]
    width = (wide - cot_width) // CORES
    block = math.gcd(math.gcd(width // 2, 256), cot_width)
    steps = width // parts // block
    skip = part * steps
    first = (cot_width + half * width) // block + skip
    middle = steps // 2
    tokens = sum(payload.shape[0] for payload in payloads)
    return call(
        functools.partial(outer_kernel, [len(group) for group in groups], len(before), len(halves)), "outer",
        2 * tokens * width * cot_width, 2 * tokens * width + 4 * width * cot_width,
        grid=(steps,),
        in_specs=[pl.BlockSpec((payload.shape[0], cot_width), lambda i: (0, 0)) for payload in payloads]
        + [pl.BlockSpec((payload.shape[0], block), lambda i: (0, first + i)) for payload in payloads]
        + [pl.BlockSpec((block, cot_width), lambda i: (skip + i, 0)) for term in before]
        + [
            pl.BlockSpec((block, cot_width), lambda i: (jnp.minimum(i, middle - 1), 0)),
            pl.BlockSpec((block, cot_width), lambda i: (jnp.maximum(i - middle, 0), 0)),
        ][:len(halves)]
        + [whole] * len(after),
        out_specs=pl.BlockSpec((block, cot_width), lambda i: (i, 0)),
        out_shape=jax.ShapeDtypeStruct((width // parts, cot_width), dtype),
    )(*payloads, *payloads, *before, *halves, *after)


def shards(
    new_input,
    new_gain,
    queries,
    new_keys,
    context_grad,
    segment_ids,
    frozen_input,
    frozen_gain,
    output_grad,
    kv_grad,
    kv_weight,
):
    chips = lax.axis_size("dp") // CORES
    sections = lax.axis_size("pipe")
    tokens, kv_width = new_keys.shape[1:]
    at = lax.axis_index("dp")
    place = jnp.stack([at // CORES, at % CORES]).astype(jnp.int32)
    middle = chips // 2
    near = [by for by in range(1, chips) if by != middle]
    spread = tokens // 4

    rows = [kv_grad[0]] + [along_chips(kv_grad[0], chips - by, 1) for by in range(1, chips)]
    other_weight = swap_cores(kv_weight[0])
    value_cot = attend(queries[0], new_keys[0], context_grad[0], segment_ids)

    apply = functools.partial(normalize, place, new_input[0], new_gain, value_cot, chips)
    shared = apply([middle], 0, spread, [other_weight])[0]
    brought = [between_lines(shared, section, 0) for section in range(1, sections)]
    early = apply([0] + near[:1], 0, tokens, rows[1:])
    columns = [early[0]] + [along_chips(block, by) for block, by in zip(early[1:], near)]
    joint = stack_rows([shared] + brought, early[:1])
    moved = on_line(joint, middle, 0)
    returned = [moved[:spread]] + [
        between_lines(moved[section * spread:(section + 1) * spread], 0, section) for section in range(1, sections)
    ]

    cuts = [0, tokens * 5 // 8, tokens]
    parts = project(rows, kv_weight[0], other_weight, cuts, [joint])
    arrived = [
        [part[0]] + [along_chips(part[by], by, 1) for by in range(1, chips)] for part in parts
    ]
    backward = functools.partial(norm_backward, place, rows=frozen_input[0], gain=frozen_gain, grads=output_grad[0])
    above = backward(arrived[0], start=cuts[0], after=columns[1:])
    kept = apply([middle], spread, tokens - spread, [above] + arrived[1][1:])
    late = apply(near[1:], 0, tokens, kept)
    above = [above, backward(arrived[1], start=cuts[1], after=late[:1])]
    below = [from_behind(half, "pipe", -1) for half in above]
    cot_below = join_rows(below)

    groups = [[column] for column in columns] + [returned]
    last = [[along_chips(block, by)] for block, by in zip(late + kept, near[1:] + [middle])]
    sums = [outer(groups, kv_width, half, [], jnp.float32, after=above[1:]) for half in range(CORES)]
    given = [
        outer(last, kv_width, 1, sums[1:], jnp.bfloat16, part, 2, after=sums[:1]) for part in range(2)
    ]
    taken = [swap_cores(part) for part in given]
    grad = outer(last, kv_width, 0, sums[:1], jnp.float32, halves=taken)
    return (cot_below[None], grad[None])


def solution(mesh):
    placed = (
        P("pipe", "dp", None),
        P("pipe", None),
        P("pipe", "dp", None),
        P("pipe", "dp", None),
        P("pipe", "dp", None),
        P("pipe", "dp"),
        P("pipe", "dp", None),
        P("pipe", None),
        P("pipe", "dp", None),
        P("pipe", "dp", None),
        P("pipe", "dp", None),
    )
    return jax.shard_map(
        shards,
        mesh=mesh,
        in_specs=placed,
        out_specs=(P("pipe", "dp", None), P("pipe", "dp", None)),
        check_vma=False,
    )
```

```python
import functools
import math

import jax
import jax.numpy as jnp
from jax import lax
from jax.experimental import pallas as pl
from jax.experimental.pallas import tpu as pltpu
from jax.sharding import PartitionSpec as P

HEAD = 128
CORES = 2
MIB = 1 << 20

norm_eps = 1e-05
masked_value = -1e30

whole = pl.BlockSpec(memory_space=pl.ANY)
scalars = pl.BlockSpec(memory_space=pltpu.SMEM)


def from_behind(array, axis, by):
    length = lax.axis_size(axis)
    pairs = [(i, i + by) for i in range(length) if 0 <= i + by < length]
    return lax.ppermute(array, axis, pairs)


def along_chips(array, by, first=0):
    length = lax.axis_size("dp")
    pairs = [
        (line * length + i, line * length + ((i + by * CORES) % length if line >= first else i ^ 1))
        for line in range(lax.axis_size("pipe")) for i in range(length)
    ]
    return lax.ppermute(array, ("pipe", "dp"), pairs)


def between_lines(array, source, target):
    length = lax.axis_size("dp")
    pairs = [(source * length + i, target * length + i) for i in range(length)]
    return lax.ppermute(array, ("pipe", "dp"), pairs)


def on_line(array, by, line):
    length = lax.axis_size("dp")
    pairs = [(line * length + i, line * length + (i + by * CORES) % length) for i in range(length)]
    return lax.ppermute(array, ("pipe", "dp"), pairs)


def swap_cores(array):
    length = lax.axis_size("dp")
    return lax.ppermute(array, "dp", [(i, i ^ 1) for i in range(length)])


def call(body, name, flops, nbytes, vmem=24, **kwargs):
    return pl.pallas_call(
        body,
        name=name,
        compiler_params=pltpu.CompilerParams(vmem_limit_bytes=vmem * MIB),
        cost_estimate=pl.CostEstimate(flops=flops, bytes_accessed=nbytes, transcendentals=0),
        **kwargs,
    )


def part_columns(chip, half, core, width):
    owner = chip * CORES + (core if half == 0 else CORES - 1 - core)
    return pl.ds(pl.multiple_of(owner * width, width), width)


def norm_kernel(chips, ahead, place_ref, x_ref, gain_ref, cot_ref, *rest):
    out_refs = rest[-len(ahead):]
    chip, core = place_ref[0], place_ref[1]
    values = x_ref[...].astype(jnp.float32)
    inverse = lax.rsqrt(jnp.mean(values * values, axis=-1, keepdims=True) + norm_eps)
    front = cot_ref.shape[1]
    width = (out_refs[0].shape[1] - front) // CORES
    for by, out_ref in zip(ahead, out_refs):
        to = lax.rem(chip + by, chips)
        out_ref[:, :front] = cot_ref[...]
        for half in range(CORES):
            cols = part_columns(to, half, core, width)
            out_ref[:, front + half * width:front + (half + 1) * width] = (
                x_ref[:, cols].astype(jnp.float32) * inverse * gain_ref[:, cols].astype(jnp.float32)
            ).astype(out_ref.dtype)


def normalize(place, rows, gain, cot, chips, ahead, start, count, after):
    width = rows.shape[1]
    front = cot.shape[1]
    block = math.gcd(math.gcd(start, count), 32)
    first = start // block
    out_width = front + width // chips
    return list(call(
        functools.partial(norm_kernel, chips, ahead), "norm_forward",
        4 * count * width, 2 * count * width + 2 * count * out_width * len(ahead),
        grid=(count // block,),
        in_specs=[
            scalars,
            pl.BlockSpec((block, width), lambda i: (first + i, 0)),
            pl.BlockSpec((1, width), lambda i: (0, 0)),
            pl.BlockSpec((block, front), lambda i: (first + i, 0)),
        ] + [whole] * len(after),
        out_specs=[pl.BlockSpec((block, out_width), lambda i: (i, 0))] * len(ahead),
        out_shape=[jax.ShapeDtypeStruct((count, out_width), jnp.bfloat16)] * len(ahead),
    )(place, rows, gain, cot, *after))


def stack_kernel(count, *refs):
    at = 0
    for ref in refs[:count]:
        refs[-1][at:at + ref.shape[0]] = ref[...]
        at += ref.shape[0]


def stack_rows(arrays, after):
    width = arrays[0].shape[1]
    tall = sum(array.shape[0] for array in arrays)
    return call(
        functools.partial(stack_kernel, len(arrays)), "stack_rows", 0, 4 * tall * width,
        grid=(1,),
        in_specs=[pl.BlockSpec(array.shape, lambda i: (0, 0)) for array in arrays] + [whole] * len(after),
        out_specs=pl.BlockSpec((tall, width), lambda i: (0, 0)),
        out_shape=jax.ShapeDtypeStruct((tall, width), arrays[0].dtype),
    )(*arrays, *after)


def join_kernel(count, *refs):
    out_ref, semaphores = refs[-2], refs[-1]
    at, copies = 0, []
    for index, ref in enumerate(refs[:count]):
        tall = ref.shape[0]
        copies.append(pltpu.make_async_copy(ref, out_ref.at[at:at + tall], semaphores.at[index]))
        at += tall
    for copy in copies:
        copy.start()
    for copy in copies:
        copy.wait()


def join_rows(arrays):
    width = arrays[0].shape[1]
    tall = sum(array.shape[0] for array in arrays)
    return call(
        functools.partial(join_kernel, len(arrays)), "join_rows", 0, 4 * tall * width,
        in_specs=[whole] * len(arrays),
        out_specs=pl.BlockSpec(memory_space=pltpu.HBM),
        out_shape=jax.ShapeDtypeStruct((tall, width), arrays[0].dtype),
        scratch_shapes=[pltpu.SemaphoreType.DMA((len(arrays),))],
    )(*arrays)


def attend_kernel(query_ref, key_ref, grad_ref, row_seg_ref, col_seg_ref, out_ref):
    tokens = key_ref.shape[0]
    group = query_ref.shape[1] // HEAD
    at_query = lax.broadcasted_iota(jnp.int32, (tokens, tokens), 0)
    at_key = lax.broadcasted_iota(jnp.int32, (tokens, tokens), 1)
    visible = (col_seg_ref[...] == row_seg_ref[...]) & (at_key <= at_query)
    keys = key_ref[...]
    total = jnp.zeros((tokens, HEAD), jnp.float32)
    for head in range(group):
        cols = slice(head * HEAD, (head + 1) * HEAD)
        scores = lax.dot_general(
            query_ref[:, cols], keys, (((1,), (1,)), ((), ())),
            preferred_element_type=jnp.float32,
        ) / math.sqrt(HEAD)
        masked = jnp.where(visible, scores, masked_value)
        highest = jnp.max(masked, axis=-1, keepdims=True)
        weights = jnp.where(visible, jnp.exp(masked - highest), 0.0)
        attention = (weights / jnp.sum(weights, axis=-1, keepdims=True)).astype(jnp.bfloat16)
        total += lax.dot_general(
            attention, grad_ref[:, cols], (((0,), (0,)), ((), ())),
            preferred_element_type=jnp.float32,
        )
    out_ref[...] = total.astype(out_ref.dtype)


def attend(queries, keys, grads, segments):
    tokens, kv_width = keys.shape
    heads = kv_width // HEAD
    wide = queries.shape[1] // heads
    return call(
        attend_kernel, "attend",
        4 * tokens * tokens * queries.shape[1], 4 * tokens * queries.shape[1],
        grid=(heads,),
        in_specs=[
            pl.BlockSpec((tokens, wide), lambda i: (0, i)),
            pl.BlockSpec((tokens, HEAD), lambda i: (0, i)),
            pl.BlockSpec((tokens, wide), lambda i: (0, i)),
            pl.BlockSpec((1, tokens), lambda i: (0, 0)),
            pl.BlockSpec((tokens, 1), lambda i: (0, 0)),
        ],
        out_specs=pl.BlockSpec((tokens, HEAD), lambda i: (0, i)),
        out_shape=jax.ShapeDtypeStruct((tokens, kv_width), jnp.bfloat16),
    )(queries, keys, grads, segments, segments.reshape(tokens, 1))


def project_kernel(chips, steps, cuts, own_ref, other_ref, *rest):
    row_refs, out_refs, gathered = rest[:chips], rest[-chips * (len(cuts) - 1) - 1:-1], rest[-1]
    taken, depth = row_refs[0].shape
    step = pl.program_id(0)

    @pl.when(step == 0)
    def _():
        for by in range(chips):
            gathered[by] = row_refs[by][...]

    def multiply(weight_ref):
        product = lax.dot_general(
            gathered[...].reshape(chips * taken, depth), weight_ref[...], (((1,), (1,)), ((), ())),
            preferred_element_type=jnp.float32,
        ).astype(jnp.bfloat16)
        for part, (start, end) in enumerate(zip(cuts, cuts[1:])):
            for by in range(chips):
                out_refs[part * chips + by][...] = product[by * taken + start:by * taken + end]

    @pl.when(step < steps)
    def _():
        multiply(own_ref)

    @pl.when(step >= steps)
    def _():
        multiply(other_ref)


def project(rows, own, other, cuts, after):
    chips = len(rows)
    taken, depth = rows[0].shape
    width = own.shape[0]
    block = min(width, 512)
    steps = width // block
    counts = [end - start for start, end in zip(cuts, cuts[1:]) for by in range(chips)]
    results = list(call(
        functools.partial(project_kernel, chips, steps, cuts), "project",
        4 * chips * taken * depth * width, 2 * (chips * taken * (depth + 2 * width) + 2 * width * depth),
        grid=(CORES * steps,),
        in_specs=[
            pl.BlockSpec((block, depth), lambda i: (jnp.minimum(i, steps - 1), 0)),
            pl.BlockSpec((block, depth), lambda i: (jnp.maximum(i - steps, 0), 0)),
        ] + [pl.BlockSpec((taken, depth), lambda i: (0, 0))] * chips + [whole] * len(after),
        out_specs=[pl.BlockSpec((count, block), lambda i: (0, i)) for count in counts],
        out_shape=[jax.ShapeDtypeStruct((count, CORES * width), jnp.bfloat16) for count in counts],
        scratch_shapes=[pltpu.VMEM((chips, taken, depth), jnp.bfloat16)],
    )(own, other, *rows, *after))
    return [results[at:at + chips] for at in range(0, len(results), chips)]


def backward_kernel(chips, place_ref, x_ref, gain_ref, grad_ref, *rest):
    cot_refs, out_ref = rest[:chips], rest[-1]
    chip, core = place_ref[0], place_ref[1]
    values = x_ref[...].astype(jnp.float32)
    width = cot_refs[0].shape[1] // CORES
    inverse = lax.rsqrt(jnp.mean(values * values, axis=-1, keepdims=True) + norm_eps)
    inner = jnp.zeros_like(inverse)

    def parts():
        for by, cot_ref in enumerate(cot_refs):
            source = lax.rem(chip + chips - by, chips)
            for half in range(CORES):
                cols = part_columns(source, half, core, width)
                cot = cot_ref[:, half * width:(half + 1) * width].astype(jnp.float32)
                yield cols, gain_ref[:, cols].astype(jnp.float32) * cot

    for cols, scaled in parts():
        inner += jnp.sum(x_ref[:, cols].astype(jnp.float32) * scaled, axis=-1, keepdims=True)
    factor = inverse * inverse * inverse * (inner / x_ref.shape[1])
    for cols, scaled in parts():
        out_ref[:, cols] = (
            grad_ref[:, cols].astype(jnp.float32)
            + inverse * scaled
            - x_ref[:, cols].astype(jnp.float32) * factor
        ).astype(out_ref.dtype)


def norm_backward(place, cots, rows, gain, grads, start, after):
    tokens, width = rows.shape
    taken, part_width = cots[0].shape
    block = math.gcd(math.gcd(start, taken), 32)
    first = start // block
    return call(
        functools.partial(backward_kernel, len(cots)), "norm_backward",
        10 * taken * width, 8 * taken * width,
        grid=(taken // block,),
        in_specs=[
            scalars,
            pl.BlockSpec((block, width), lambda i: (first + i, 0)),
            pl.BlockSpec((1, width), lambda i: (0, 0)),
            pl.BlockSpec((block, width), lambda i: (first + i, 0)),
        ] + [pl.BlockSpec((block, part_width), lambda i: (i, 0))] * len(cots) + [whole] * len(after),
        out_specs=pl.BlockSpec((block, width), lambda i: (i, 0)),
        out_shape=jax.ShapeDtypeStruct((taken, width), jnp.bfloat16),
    )(place, rows, gain, grads, *cots, *after)


def outer_kernel(groups, sums, halves, *refs):
    arrays = sum(groups)
    cots, columns, terms = refs[:arrays], refs[arrays:2 * arrays], refs[2 * arrays:2 * arrays + sums]
    total, at = None, 0
    for size in groups:
        column, cot = columns[at][...], cots[at][...]
        for more in range(at + 1, at + size):
            column, cot = column + columns[more][...], cot + cots[more][...]
        at += size
        product = lax.dot_general(
            column, cot, (((0,), (0,)), ((), ())), preferred_element_type=jnp.float32
        )
        total = product if total is None else total + product
    for term in terms:
        total += term[...].astype(jnp.float32)
    if halves:
        lower, upper = refs[2 * arrays + sums:2 * arrays + sums + 2]
        in_lower = pl.program_id(0) < pl.num_programs(0) // 2
        total += jnp.where(in_lower, lower[...], upper[...]).astype(jnp.float32)
    refs[-1][...] = total.astype(refs[-1].dtype)


def outer(groups, cot_width, half, before, dtype, part=0, parts=1, halves=(), after=()):
    payloads = [payload for group in groups for payload in group]
    wide = payloads[0].shape[1]
    width = (wide - cot_width) // CORES
    block = math.gcd(math.gcd(width // 2, 256), cot_width)
    steps = width // parts // block
    skip = part * steps
    first = (cot_width + half * width) // block + skip
    middle = steps // 2
    tokens = sum(payload.shape[0] for payload in payloads)
    return call(
        functools.partial(outer_kernel, [len(group) for group in groups], len(before), len(halves)), "outer",
        2 * tokens * width * cot_width, 2 * tokens * width + 4 * width * cot_width,
        grid=(steps,),
        in_specs=[pl.BlockSpec((payload.shape[0], cot_width), lambda i: (0, 0)) for payload in payloads]
        + [pl.BlockSpec((payload.shape[0], block), lambda i: (0, first + i)) for payload in payloads]
        + [pl.BlockSpec((block, cot_width), lambda i: (skip + i, 0)) for term in before]
        + [
            pl.BlockSpec((block, cot_width), lambda i: (jnp.minimum(i, middle - 1), 0)),
            pl.BlockSpec((block, cot_width), lambda i: (jnp.maximum(i - middle, 0), 0)),
        ][:len(halves)]
        + [whole] * len(after),
        out_specs=pl.BlockSpec((block, cot_width), lambda i: (i, 0)),
        out_shape=jax.ShapeDtypeStruct((width // parts, cot_width), dtype),
    )(*payloads, *payloads, *before, *halves, *after)


def shards(
    new_input,
    new_gain,
    queries,
    new_keys,
    context_grad,
    segment_ids,
    frozen_input,
    frozen_gain,
    output_grad,
    kv_grad,
    kv_weight,
):
    chips = lax.axis_size("dp") // CORES
    sections = lax.axis_size("pipe")
    tokens, kv_width = new_keys.shape[1:]
    at = lax.axis_index("dp")
    place = jnp.stack([at // CORES, at % CORES]).astype(jnp.int32)
    middle = chips // 2
    near = [by for by in range(1, chips) if by != middle]
    spread = tokens // 4

    rows = [kv_grad[0]] + [along_chips(kv_grad[0], chips - by, 1) for by in range(1, chips)]
    other_weight = swap_cores(kv_weight[0])
    value_cot = attend(queries[0], new_keys[0], context_grad[0], segment_ids)

    apply = functools.partial(normalize, place, new_input[0], new_gain, value_cot, chips)
    shared = apply([middle], 0, spread, [other_weight])[0]
    brought = [between_lines(shared, section, 0) for section in range(1, sections)]
    early = apply([0] + near[:1], 0, tokens, rows[1:])
    columns = [early[0]] + [along_chips(block, by) for block, by in zip(early[1:], near)]
    joint = stack_rows([shared] + brought, early[:1])
    moved = on_line(joint, middle, 0)
    returned = [moved[:spread]] + [
        between_lines(moved[section * spread:(section + 1) * spread], 0, section) for section in range(1, sections)
    ]

    cuts = [0, tokens * 5 // 8, tokens]
    parts = project(rows, kv_weight[0], other_weight, cuts, [joint])
    arrived = [
        [part[0]] + [along_chips(part[by], by, 1) for by in range(1, chips)] for part in parts
    ]
    backward = functools.partial(norm_backward, place, rows=frozen_input[0], gain=frozen_gain, grads=output_grad[0])
    above = backward(arrived[0], start=cuts[0], after=columns[1:])
    late = apply(near[1:], 0, tokens, [above] + [arrived[1][by] for by in near])
    kept = apply([middle], spread, tokens - spread, late + arrived[1][1:])
    above = [above, backward(arrived[1], start=cuts[1], after=kept)]
    below = [from_behind(half, "pipe", -1) for half in above]
    cot_below = join_rows(below)

    groups = [[column] for column in columns] + [returned]
    last = [[along_chips(block, by)] for block, by in zip(late + kept, near[1:] + [middle])]
    sums = [outer(groups, kv_width, half, [], jnp.float32, after=above[1:]) for half in range(CORES)]
    given = [
        outer(last, kv_width, 1, sums[1:], jnp.bfloat16, part, 2, after=sums[:1]) for part in range(2)
    ]
    taken = [swap_cores(part) for part in given]
    grad = outer(last, kv_width, 0, sums[:1], jnp.float32, halves=taken)
    return (cot_below[None], grad[None])


def solution(mesh):
    placed = (
        P("pipe", "dp", None),
        P("pipe", None),
        P("pipe", "dp", None),
        P("pipe", "dp", None),
        P("pipe", "dp", None),
        P("pipe", "dp"),
        P("pipe", "dp", None),
        P("pipe", None),
        P("pipe", "dp", None),
        P("pipe", "dp", None),
        P("pipe", "dp", None),
    )
    return jax.shard_map(
        shards,
        mesh=mesh,
        in_specs=placed,
        out_specs=(P("pipe", "dp", None), P("pipe", "dp", None)),
        check_vma=False,
    )
```
